256 devices in a mesh: blk: 16 (over z, core), head: 8 (over x, y_lo), cfg: 2 (over y_hi).
Axes of the slice: x: 4, y: 4 (y_hi: 2, y_lo: 2; y = y_hi * 2 + y_lo), z: 8, core: 2. Of those that a mesh axis runs over, the one named last changes fastest.
Arguments:
- fresh: bfloat16 [8192, 3, 5120], P(('cfg', 'blk', 'head')), parts along dimension 0, may hold values from -96 to 96, as said below
- rows_index: int32 [4096], P('blk'), may hold values from 0 to 511, as said below
- counts: int32 [16], replicated, may hold values from 64 to 256, as said below
- key_cache: bfloat16 [16384, 5120], P(('cfg', 'blk'), 'head'), parts along dimension 0, may hold values from -6 to 6
- value_cache: bfloat16 [16384, 5120], P(('cfg', 'blk'), 'head'), parts along dimension 0, may hold values from -48 to 48
- q_gain: bfloat16 [5120], replicated, may hold values from 0.099609375 to 1.8984375
- k_gain: bfloat16 [5120], replicated, may hold values from 0.099609375 to 1.8984375
- out_weight: bfloat16 [5120, 5120], P('head'), may hold values from -0.25 to 0.25
Outputs:
- mixed: bfloat16 [8192, 5120], P(('cfg', 'blk', 'head')), parts along dimension 0
The draws below stay inside these ranges and needn't reach their ends.
There are 2 independent parts, one for each index of `cfg`. The reference program is written for one: setup_inputs(seed, part) draws one part's arguments, and reference() takes and returns one part's arrays. A program takes and returns all parts, laid end to end along the dimension named above; an argument that names none is the same for every part. Nothing has to cross between parts.
Inputs may be any that keep to these rules, and one draw needn't show every extreme that they name: `rows_index`: within each shard's 256 slots the values are distinct positions of that shard. counts[j] live slots of shard j are its first slots; the counts sum to exactly 2048, and some shard has all 256 slots live; the counts of the shards before shard j sum to more than j * 128 - 3 * 64 and less than j * 128 + 3 * 64. `fresh`: slots that are not live carry data that no output reads.
All inputs are finite; a program needn't handle non-finite values.
Results may differ from the reference program's by a relative error of at most 0.035.
Values may be sent and summed in bfloat16 or wider, within the bound.
A program may use at most 128 MiB of HBM per device.

```python
import math
import jax
import jax.numpy as jnp
from jax import lax

D = 5120
HEADS = 40
HEAD_DIM = 128
L_BLK = 512
QMEAN = 128
CAP = 256
TOKENS = 8192
N_BLK = 16


def draw_fresh(key, part):
    key = jax.random.fold_in(key, 5)
    streams = jax.random.split(key, 3)
    total_rows = N_BLK * CAP
    base = jax.random.normal(streams[0], (total_rows, 3, D), jnp.float32)
    row_scale = jnp.exp(jax.random.uniform(streams[1], (total_rows, 2, 1), jnp.float32) * math.log(10.0))
    value_part = 8.0 * base[:, 2:]
    col_scale = jnp.exp(jax.random.uniform(streams[2], (1, 2, D), jnp.float32) * math.log(10.0))
    projected = base[:, :2] * row_scale * col_scale
    whole = jnp.concatenate([projected, value_part], axis=1)
    return jnp.clip(whole, -96.0, 96.0).astype(jnp.bfloat16)


def draw_rows_index(key, part):
    key = jax.random.fold_in(key, 7)
    shard_keys = jax.random.split(key, N_BLK)

    def one_shard(shard_key, shard_id):
        first_key, second_key, third_key = jax.random.split(shard_key, 3)
        order = jax.random.permutation(first_key, L_BLK).astype(jnp.int32)
        wanted = jnp.where(shard_id == 0, L_BLK - 1, jnp.where(shard_id == 1, 0, jax.random.randint(third_key, (), 0, L_BLK)))
        located = jnp.argmax((order == wanted).astype(jnp.int32))
        landing = jax.random.randint(second_key, (), 0, max(QMEAN // 2, 1))
        order = jnp.roll(order, landing - located)
        return order[:CAP]
    picked = jax.vmap(one_shard)(shard_keys, jnp.arange(N_BLK, dtype=jnp.int32))
    return picked.reshape(N_BLK * CAP).astype(jnp.int32)


def draw_counts(key, part):
    key = jax.random.fold_in(key, 11)
    first_key, second_key = jax.random.split(key)
    jitter = jax.random.randint(first_key, (N_BLK,), 0, max(QMEAN // 4, 1))
    amounts = QMEAN + jitter - jnp.roll(jitter, 1)
    fullest = jax.random.randint(second_key, (), 0, N_BLK)
    extra = CAP - amounts[fullest]
    others = N_BLK - 1
    order = (jnp.arange(N_BLK, dtype=jnp.int32) - fullest - 1) % N_BLK
    taken = extra // others + (order < extra % others).astype(jnp.int32)
    amounts = jnp.where(jnp.arange(N_BLK) == fullest, CAP, amounts - taken)
    return amounts.astype(jnp.int32)


def block_levels(rng, dims, cuts, smallest, high):
    def one(dim, blocks):
        steps = jax.random.uniform(jax.random.fold_in(jax.random.fold_in(rng, 6), dim), (blocks,), jnp.float32, smallest / len(cuts), high / len(cuts))
        return jnp.repeat(jnp.exp(steps), dims[dim] // blocks).reshape((-1,) + (1,) * (len(dims) - dim - 1))

    level = one(*cuts[0])
    for cut in cuts[1:]:
        level = level * one(*cut)
    return level


def gaussian(stream_key, dims, deviation, limit, shards=(), kind=jnp.bfloat16):
    entries = jax.random.normal(stream_key, dims, jnp.float32) * deviation
    if len(shards) > 0:
        entries = block_levels(stream_key, dims, shards, -0.22, 0.18) * entries
    return jnp.clip(entries, min=-limit, max=limit).astype(kind)


def setup_inputs(seed: int = 0, part: int = 0) -> dict:
    seeds = jax.random.split(jax.random.key(seed), 9)
    part_splits = jax.random.split(jax.random.fold_in(seeds[8], part), 9)
    return {
        "fresh": draw_fresh(jax.random.fold_in(jax.random.fold_in(seeds[8], part), 71), part),
        "rows_index": draw_rows_index(jax.random.fold_in(seeds[8], 71), part),
        "counts": draw_counts(jax.random.fold_in(seeds[8], 71), part),
        "key_cache": gaussian(part_splits[3], (TOKENS, D), 1.0, 6.0, ((0, 16), (1, 8))),
        "value_cache": gaussian(part_splits[4], (TOKENS, D), 8.0, 48.0, ((0, 16), (1, 8))),
        "q_gain": jnp.clip(1.0 + 0.18 * jax.random.normal(seeds[5], (D,), jnp.float32), 0.099609375, 1.8984375).astype(jnp.bfloat16),
        "k_gain": jnp.clip(1.0 + 0.18 * jax.random.normal(seeds[6], (D,), jnp.float32), 0.099609375, 1.8984375).astype(jnp.bfloat16),
        "out_weight": gaussian(seeds[7], (D, D), (D // 8) ** -0.5, 0.25, ((0, 8),)),
    }


EPS = 1e-06

def normalize(rows, gains):
    values = rows.astype(jnp.float32)
    mean_sq = lax.optimization_barrier(jnp.mean(values * values, axis=-1, keepdims=True))
    return (values * lax.rsqrt(mean_sq + EPS) * gains.astype(jnp.float32)).astype(jnp.bfloat16)

def reference(fresh, rows_index, counts, key_cache, value_cache, q_gain, k_gain, out_weight):
    total_rows = N_BLK * CAP
    queries = normalize(fresh[:, 0], q_gain)
    new_keys = normalize(fresh[:, 1], k_gain)
    new_values = fresh[:, 2]
    slot_ids = jnp.arange(total_rows, dtype=jnp.int32)
    shard_ids = slot_ids // CAP
    is_live = slot_ids % CAP < counts[shard_ids]
    positions = jnp.where(is_live, shard_ids * L_BLK + rows_index, N_BLK * L_BLK).astype(jnp.int32)
    keys = key_cache.at[positions].set(new_keys, mode='drop')
    values = value_cache.at[positions].set(new_values, mode='drop')
    scale = 1.0 / math.sqrt(HEAD_DIM)

    def one_head(head_id):
        first = (head_id * HEAD_DIM).astype(jnp.int32)
        q_part = lax.dynamic_slice_in_dim(queries, first, HEAD_DIM, 1)
        k_part = lax.dynamic_slice_in_dim(keys, first, HEAD_DIM, 1)
        v_part = lax.dynamic_slice_in_dim(values, first, HEAD_DIM, 1)
        scores = jnp.dot(q_part, k_part.T, preferred_element_type=jnp.float32) * scale
        highest = lax.optimization_barrier(jnp.max(scores, axis=1, keepdims=True))
        weights = jnp.exp(scores - highest)
        totals = lax.optimization_barrier(jnp.sum(weights, axis=1, keepdims=True))
        summed = jnp.dot(weights.astype(jnp.bfloat16), v_part, preferred_element_type=jnp.float32)
        return (summed / totals).astype(jnp.bfloat16)
    per_head = lax.map(one_head, jnp.arange(HEADS, dtype=jnp.int32))
    attention = jnp.transpose(per_head, (1, 0, 2)).reshape(total_rows, D)
    attention = jnp.where(is_live[:, None], attention, jnp.zeros_like(attention))
    return jnp.dot(attention, out_weight, preferred_element_type=jnp.float32).astype(jnp.bfloat16)
```

```python
import functools
import math

import jax
import jax.numpy as jnp
from jax import lax
from jax.experimental import pallas as pl
from jax.experimental.pallas import tpu as pltpu
from jax.sharding import PartitionSpec as P

HEAD_DIM = 128
EPS = 1e-06
MESH = pl.DeviceIdType.MESH
BF = jnp.bfloat16
F32 = jnp.float32

D = 5120
GROUP = 640
NH = GROUP // HEAD_DIM
NG = 8
NB = 16
CAP = 256
L_BLK = 512
ROWS = 32
CH = 128
SPAN = 512
BASE = 192
PART = ((0, 3), (3, 5))
C1 = 3072
C1H = C1 // 2
C2 = D - C1
C2H = C2 // 2
SCALE2 = math.log2(math.e) / math.sqrt(HEAD_DIM)


def nt(a, b):
    return lax.dot_general(a, b, (((1,), (1,)), ((), ())), preferred_element_type=F32)


def mm(a, b):
    return jnp.dot(a, b, preferred_element_type=F32)


def kernel(
    fresh, ridx, counts, kcache, vcache, qgain, kgain, weight, out,
    fv, gq, gk, kc, vc, wv, sent, got, selq, rbuf, kfull, vt, qs,
    of, st, so, ss, ro, rs, abuf, cat, att, pb,
    rx1, ac1, ry1, sy1, ry2, sx2, rx2, ac2,
    lsem, asend, arecv, rsend, rrecv, ksend, krecv, gsend, grecv,
    dsend, drecv, tsend, trecv, usend, urecv, esend, erecv,
):
    j = lax.axis_index("blk")
    h = lax.axis_index("head")
    core = lax.rem(j, 2)
    x, y = lax.div(h, 2), lax.rem(h, 2)
    pending = []

    def blk_at(offset):
        return {"blk": lax.rem(j + offset + NB, NB)}

    sibling = {"blk": j + 1 - 2 * core}

    def head_at(dx, dy):
        other_y = 1 - y if dy else y
        return lax.rem(x + dx, 4) * 2 + other_y

    def send(src, dst, s, r, dev):
        copy = pltpu.make_async_remote_copy(
            src_ref=src, dst_ref=dst, send_sem=s, recv_sem=r, device_id=dev, device_id_type=MESH
        )
        copy.start()
        pending.append(copy)
        return copy

    loads = [
        pltpu.make_async_copy(src, dst, lsem.at[i])
        for i, (src, dst) in enumerate((
            (fresh.at[0], fv.at[0]), (qgain, gq), (fresh.at[1], fv.at[1]), (kgain, gk),
            (fresh.at[2], fv.at[2]), (kcache, kc), (vcache, vc), (weight, wv),
        ))
    ]
    for load in loads:
        load.start()

    barrier = pltpu.get_barrier_semaphore()
    pairs = [(dx, dy) for dx in range(4) for dy in range(2) if dx or dy]
    for dx, dy in pairs:
        pl.semaphore_signal(barrier, inc=1, device_id={"head": head_at(dx, dy)}, device_id_type=MESH)
    for offset in (-2, -1, 1, 2):
        pl.semaphore_signal(barrier, inc=1, device_id=blk_at(offset), device_id_type=MESH)
    pl.semaphore_wait(barrier, len(pairs) + 4)

    live = counts[j]
    before = jnp.int32(0)
    for i in range(NB):
        before = before + jnp.where(i < j, counts[i], 0)
    shift = before - CH * j + BASE

    my_rows = pl.ds(pl.multiple_of(h * ROWS, ROWS), ROWS)
    a_copies = [[], [], []]
    for t in range(3):
        loads[2 * t].wait()
        if t < 2:
            loads[2 * t + 1].wait()
            rows = fv[t].astype(F32)
            mean_sq = jnp.mean(rows * rows, axis=-1, keepdims=True)
            gains = (gq if t == 0 else gk)[...].astype(F32)
            rows = (rows * lax.rsqrt(mean_sq + EPS) * gains).astype(BF)
        else:
            rows = fv[2]
        for g in range(NG):
            sent[t, g] = rows[:, g * GROUP:(g + 1) * GROUP]
        for n, (dx, dy) in enumerate(pairs):
            peer = head_at(dx, dy)
            a_copies[t].append(send(
                sent.at[t, peer], got.at[t, my_rows], asend.at[t, n], arecv.at[t, n], {"head": peer}
            ))
        got[t, my_rows] = sent[t, h]

    for copy in a_copies[0]:
        copy.wait_recv()
    r_id = lax.broadcasted_iota(jnp.int32, (SPAN, CAP), 0)
    s_id = lax.broadcasted_iota(jnp.int32, (SPAN, CAP), 1)
    place = ((r_id - s_id) == shift) & (s_id < live)
    selq[...] = mm(place.astype(F32).astype(BF), got[0]).astype(BF)
    r_copies = [
        send(selq.at[pl.ds(first, size)], rbuf.at[pl.ds(to, size)], rsend.at[n], rrecv.at[n], blk_at(offset))
        for n, (first, size, to, offset) in enumerate(
            ((64, 128, 0, -1), (320, 128, 128, 1), (0, 64, 256, -2), (448, 64, 320, 2))
        )
    ]
    for copy in r_copies:
        copy.wait_recv()
    mine = (selq[192:320].astype(F32) + rbuf[0:128].astype(F32)) + rbuf[128:256].astype(F32)
    qs[0, 0:64] = (mine[0:64] + rbuf[320:384].astype(F32)).astype(BF)
    qs[0, 64:128] = (mine[64:128] + rbuf[256:320].astype(F32)).astype(BF)

    halves = (pl.ds(0, 64), pl.ds(64, 64))

    def gather_step(step):
        copies = []
        for half in range(2):
            for way in range(2):
                if step == 4 and half != way:
                    continue
                src = (8 - (step - 1)) % 8 if way == 0 else step - 1
                dst = 8 - step if way == 0 else step
                copies.append(send(
                    qs.at[src, halves[half]], qs.at[dst, halves[half]],
                    gsend.at[way, step - 1, half], grecv.at[way, step - 1, half],
                    blk_at(2 if way == 0 else -2),
                ))
        return copies

    g_copies = gather_step(1)

    for t in (1, 2):
        for copy in a_copies[t]:
            copy.wait_recv()
    loads[5].wait()
    loads[6].wait()
    pos = lax.broadcasted_iota(jnp.int32, (L_BLK, CAP), 0)
    slot = lax.broadcasted_iota(jnp.int32, (L_BLK, CAP), 1)
    hits = ((pos == ridx[...]) & (slot < live)).astype(F32)
    hit = jnp.sum(hits, axis=1, keepdims=True) > 0.5
    hits = hits.astype(BF)
    kfull[0] = jnp.where(hit, mm(hits, got[1]), kc[...].astype(F32)).astype(BF)
    k_copy = send(kfull.at[0], kfull.at[1], ksend.at[0], krecv.at[0], sibling)
    vt[0] = jnp.where(hit, mm(hits, got[2]), vc[...].astype(F32)).T.astype(BF)
    v_copy = send(vt.at[0], vt.at[1], ksend.at[1], krecv.at[1], sibling)

    def attend(slots):
        width = CH * len(slots)
        for i in range(NH):
            cols = slice(i * HEAD_DIM, (i + 1) * HEAD_DIM)
            if len(slots) == 1:
                query = qs[slots[0], :, cols]
            else:
                query = jnp.concatenate([qs[s, :, cols] for s in slots], axis=0)
            s0 = nt(kfull[0, :, cols], query)
            s1 = nt(kfull[1, :, cols], query)
            top = jnp.maximum(jnp.max(s0, axis=0, keepdims=True), jnp.max(s1, axis=0, keepdims=True)) * SCALE2
            p0 = jnp.exp2(s0 * SCALE2 - top)
            p1 = jnp.exp2(s1 * SCALE2 - top)
            total = jnp.sum(p0, axis=0, keepdims=True) + jnp.sum(p1, axis=0, keepdims=True)
            o = mm(vt[0, cols, :], p0.astype(BF)) + mm(vt[1, cols, :], p1.astype(BF))
            part, row = (0, i) if i < 3 else (1, i - 3)
            for n, s in enumerate(slots):
                lanes = slice(n * CH, (n + 1) * CH)
                of[s, cols, :] = o[:, lanes]
                st[s, part, row:row + 1, :] = top[:, lanes]
                st[s, part, 8 + row:9 + row, :] = total[:, lanes]

    st[...] = jnp.zeros_like(st)
    for copy in g_copies:
        copy.wait_recv()
    g_copies = gather_step(2)
    k_copy.wait_recv()
    v_copy.wait_recv()
    attend((7, 1))
    for copy in g_copies:
        copy.wait_recv()
    g_copies = gather_step(3)
    attend((6, 2))
    for copy in g_copies:
        copy.wait_recv()
    g_copies = gather_step(4)
    attend((5, 3))
    for copy in g_copies:
        copy.wait_recv()
    attend((4,))

    def part_rows(part):
        first, last = PART[part]
        return pl.ds(first * HEAD_DIM, (last - first) * HEAD_DIM)

    def joined(slot, part, arrivals):
        first, last = PART[part]
        tops = [st[slot, part, 0:8]] + [rs[way, step, part, 0:8] for way, step in arrivals]
        sums = [st[slot, part, 8:16]] + [rs[way, step, part, 8:16] for way, step in arrivals]
        top = functools.reduce(jnp.maximum, tops)
        factors = [jnp.exp2(t - top) for t in tops]
        total = sum(a * f for a, f in zip(sums, factors))
        values = []
        for i in range(first, last):
            rows = slice(i * HEAD_DIM, (i + 1) * HEAD_DIM)
            k = i - first
            value = of[slot, rows, :] * factors[0][k:k + 1]
            for n, (way, step) in enumerate(arrivals):
                value = value + ro[way, step, rows, :].astype(F32) * factors[n + 1][k:k + 1]
            values.append(value)
        return values, top, total

    d_copies = {}

    def give(way, step, part):
        ahead = 5 - step
        slot = ahead if way == 0 else 8 - ahead
        first_step = 1 if part == way else 2
        if step > first_step:
            for copy in d_copies[way, step - 1, part]:
                copy.wait_recv()
            values, top, total = joined(slot, part, [(way, step - 2)])
        else:
            first, last = PART[part]
            values = [of[slot, i * HEAD_DIM:(i + 1) * HEAD_DIM, :] for i in range(first, last)]
            top, total = st[slot, part, 0:8], st[slot, part, 8:16]
        for n, value in enumerate(values):
            i = PART[part][0] + n
            so[way, step - 1, i * HEAD_DIM:(i + 1) * HEAD_DIM, :] = value.astype(BF)
        ss[way, step - 1, part, 0:8] = top
        ss[way, step - 1, part, 8:16] = total
        rows = part_rows(part)
        dev = blk_at(2 if way == 0 else -2)
        d_copies[way, step, part] = [
            send(ss.at[way, step - 1, part], rs.at[way, step - 1, part],
                 tsend.at[way, step - 1, part], trecv.at[way, step - 1, part], dev),
            send(so.at[way, step - 1, rows], ro.at[way, step - 1, rows],
                 dsend.at[way, step - 1, part], drecv.at[way, step - 1, part], dev),
        ]

    give(0, 1, 0)
    give(1, 1, 1)
    give(0, 2, 1)
    give(1, 2, 0)
    attend((0,))
    give(0, 2, 0)
    give(1, 2, 1)
    for step in (3, 4):
        give(0, step, 1)
        give(1, step, 0)
        give(0, step, 0)
        give(1, step, 1)
    for part in (1, 0):
        for way in range(2):
            for copy in d_copies[way, 4, part]:
                copy.wait_recv()
        values, _, total = joined(0, part, [(0, 3), (1, 3)])
        for n, value in enumerate(values):
            i = PART[part][0] + n
            result = (value / total[n:n + 1]).T.astype(BF)
            abuf[:, i * HEAD_DIM:(i + 1) * HEAD_DIM] = result

    u_copies = [
        send(abuf.at[pl.ds(first, size)], cat.at[pl.ds(to, size)], usend.at[n], urecv.at[n], blk_at(offset))
        for n, (first, size, to, offset) in enumerate(
            ((0, 128, 320, -1), (0, 128, 64, 1), (0, 64, 448, -2), (64, 64, 0, 2))
        )
    ]
    cat[192:320] = abuf[...]
    r_id = lax.broadcasted_iota(jnp.int32, (CAP, SPAN), 1)
    s_id = lax.broadcasted_iota(jnp.int32, (CAP, SPAN), 0)
    place = (((r_id - s_id) == shift) & (s_id < live)).astype(F32).astype(BF)
    for copy in u_copies:
        copy.wait_recv()
    att[...] = mm(place, cat[...]).astype(BF)

    loads[7].wait()

    def project(first, last):
        @pl.loop(first // 256, last // 256)
        def _(i):
            cols = pl.ds(pl.multiple_of(i * 256, 256), 256)
            tile = mm(att[...], wv[:, cols]).astype(BF)
            for g in range(NG):
                pb[g // 2, g % 2, :, cols] = tile[g * ROWS:(g + 1) * ROWS]

    up, down, far = lax.rem(x + 1, 4), lax.rem(x + 3, 4), lax.rem(x + 2, 4)
    to_up, to_down = {"head": up * 2 + y}, {"head": down * 2 + y}
    to_pair = {"head": x * 2 + 1 - y}
    a1, b1 = pl.ds(0, C1H), pl.ds(C1H, C1H)
    a2, b2 = pl.ds(C1, C2H), pl.ds(C1 + C2H, C2H)

    project(0, C1H)
    e = {}
    e["p1"] = send(pb.at[far, :, :, a1], rx1.at[0], esend.at[0], erecv.at[0], to_up)
    e["m2"] = send(pb.at[down, :, :, a1], rx1.at[1], esend.at[1], erecv.at[1], to_down)
    project(C1, D)
    e["y2"] = send(pb.at[:, 1 - y, :, pl.ds(C1, C2)], ry2, esend.at[2], erecv.at[2], to_pair)
    project(C1H, C1)
    e["m1"] = send(pb.at[far, :, :, b1], rx1.at[2], esend.at[3], erecv.at[3], to_down)
    e["p2"] = send(pb.at[up, :, :, b1], rx1.at[3], esend.at[4], erecv.at[4], to_up)

    e["p1"].wait_recv()
    ac1[0] = (rx1[0].astype(F32) + pb[up, :, :, 0:C1H].astype(F32)).astype(BF)
    e["p3"] = send(ac1.at[0], rx1.at[4], esend.at[5], erecv.at[5], to_up)
    e["m1"].wait_recv()
    ac1[1] = (rx1[2].astype(F32) + pb[down, :, :, C1H:C1].astype(F32)).astype(BF)
    e["m3"] = send(ac1.at[1], rx1.at[5], esend.at[6], erecv.at[6], to_down)

    e["y2"].wait_recv()
    for i in range(4):
        sx2[i] = (ry2[i].astype(F32) + pb[i, y, :, C1:D].astype(F32)).astype(BF)
    a2, b2 = pl.ds(0, C2H), pl.ds(C2H, C2H)
    e["P1"] = send(sx2.at[far, :, a2], rx2.at[0], esend.at[7], erecv.at[7], to_up)
    e["M1"] = send(sx2.at[far, :, b2], rx2.at[2], esend.at[8], erecv.at[8], to_down)
    e["M2"] = send(sx2.at[down, :, a2], rx2.at[1], esend.at[9], erecv.at[9], to_down)
    e["P2"] = send(sx2.at[up, :, b2], rx2.at[3], esend.at[10], erecv.at[10], to_up)

    def five(own, one, two):
        return own.astype(F32) + one.astype(F32) + two.astype(F32)

    for name in ("m2", "p2", "p3", "m3"):
        e[name].wait_recv()
    sy1[:, 0:C1H] = five(pb[x, 1 - y, :, 0:C1H], rx1[4, 1 - y], rx1[1, 1 - y]).astype(BF)
    sy1[:, C1H:C1] = five(pb[x, 1 - y, :, C1H:C1], rx1[5, 1 - y], rx1[3, 1 - y]).astype(BF)
    e["y1"] = send(sy1, ry1, esend.at[11], erecv.at[11], to_pair)

    e["P1"].wait_recv()
    ac2[0] = (rx2[0].astype(F32) + sx2[up, :, 0:C2H].astype(F32)).astype(BF)
    e["P3"] = send(ac2.at[0], rx2.at[4], esend.at[12], erecv.at[12], to_up)
    e["M1"].wait_recv()
    ac2[1] = (rx2[2].astype(F32) + sx2[down, :, C2H:C2].astype(F32)).astype(BF)
    e["M3"] = send(ac2.at[1], rx2.at[5], esend.at[13], erecv.at[13], to_down)

    e["y1"].wait_recv()
    own_a = five(pb[x, y, :, 0:C1H], rx1[4, y], rx1[1, y])
    out[:, 0:C1H] = (own_a + ry1[:, 0:C1H].astype(F32)).astype(BF)
    own_b = five(pb[x, y, :, C1H:C1], rx1[5, y], rx1[3, y])
    out[:, C1H:C1] = (own_b + ry1[:, C1H:C1].astype(F32)).astype(BF)
    for name in ("M2", "P2", "P3", "M3"):
        e[name].wait_recv()
    out[:, C1:C1 + C2H] = five(sx2[x, :, 0:C2H], rx2[4], rx2[1]).astype(BF)
    out[:, C1 + C2H:D] = five(sx2[x, :, C2H:C2], rx2[5], rx2[3]).astype(BF)

    for copy in pending:
        copy.wait_send()


def local(fresh, rows_index, counts, key_cache, value_cache, q_gain, k_gain, out_weight):
    any_spec = pl.BlockSpec(memory_space=pl.ANY)
    vmem = pl.BlockSpec(memory_space=pltpu.VMEM)
    dma = pltpu.SemaphoreType.DMA
    V = pltpu.VMEM
    return pl.pallas_call(
        kernel,
        out_shape=jax.ShapeDtypeStruct((ROWS, D), BF),
        in_specs=[any_spec, vmem, pl.BlockSpec(memory_space=pltpu.SMEM)] + [any_spec] * 5,
        out_specs=vmem,
        scratch_shapes=[
            V((3, ROWS, D), BF), V((1, D), BF), V((1, D), BF),
            V((L_BLK, GROUP), BF), V((L_BLK, GROUP), BF), V((GROUP, D), BF),
            V((3, NG, ROWS, GROUP), BF), V((3, CAP, GROUP), BF),
            V((SPAN, GROUP), BF), V((384, GROUP), BF),
            V((2, L_BLK, GROUP), BF), V((2, GROUP, L_BLK), BF), V((8, CH, GROUP), BF),
            V((8, GROUP, CH), F32), V((8, 2, 16, CH), F32),
            V((2, 4, GROUP, CH), BF), V((2, 4, 2, 16, CH), F32),
            V((2, 4, GROUP, CH), BF), V((2, 4, 2, 16, CH), F32),
            V((CH, GROUP), BF), V((SPAN, GROUP), BF), V((CAP, GROUP), BF),
            V((4, 2, ROWS, D), BF),
            V((6, 2, ROWS, C1H), BF), V((2, 2, ROWS, C1H), BF),
            V((ROWS, C1), BF), V((ROWS, C1), BF),
            V((4, ROWS, C2), BF), V((4, ROWS, C2), BF),
            V((6, ROWS, C2H), BF), V((2, ROWS, C2H), BF),
            dma((8,)), dma((3, 7)), dma((3, 7)), dma((4,)), dma((4,)), dma((2,)), dma((2,)),
            dma((2, 4, 2)), dma((2, 4, 2)),
            dma((2, 4, 2)), dma((2, 4, 2)), dma((2, 4, 2)), dma((2, 4, 2)),
            dma((4,)), dma((4,)), dma((14,)), dma((14,)),
        ],
        compiler_params=pltpu.CompilerParams(
            collective_id=0, has_side_effects=True, vmem_limit_bytes=56 * 1024 * 1024
        ),
    )(
        jnp.transpose(fresh, (1, 0, 2)), rows_index.reshape(1, CAP), counts, key_cache, value_cache,
        q_gain.reshape(1, D), k_gain.reshape(1, D), out_weight,
    )


def solution(mesh):
    placed = (
        P(("cfg", "blk", "head"), None, None),
        P("blk"),
        P(),
        P(("cfg", "blk"), "head"),
        P(("cfg", "blk"), "head"),
        P(),
        P(),
        P("head", None),
    )
    return jax.shard_map(
        local,
        mesh=mesh,
        in_specs=placed,
        out_specs=P(("cfg", "blk", "head"), None),
        check_vma=False,
    )
```

```python
import functools
import math

import jax
import jax.numpy as jnp
from jax import lax
from jax.experimental import pallas as pl
from jax.experimental.pallas import tpu as pltpu
from jax.sharding import PartitionSpec as P

HEAD_DIM = 128
EPS = 1e-06
MESH = pl.DeviceIdType.MESH
BF = jnp.bfloat16
F32 = jnp.float32

D = 5120
GROUP = 640
NH = GROUP // HEAD_DIM
NG = 8
NB = 16
CAP = 256
L_BLK = 512
ROWS = 32
CH = 128
SPAN = 512
BASE = 192
PART = ((0, 3), (3, 5))
C1 = 3072
C1H = C1 // 2
C2 = D - C1
C2H = C2 // 2
SCALE2 = math.log2(math.e) / math.sqrt(HEAD_DIM)


def nt(a, b):
    return lax.dot_general(a, b, (((1,), (1,)), ((), ())), preferred_element_type=F32)


def mm(a, b):
    return jnp.dot(a, b, preferred_element_type=F32)


def kernel(
    fresh, ridx, counts, kcache, vcache, qgain, kgain, weight, out,
    fv, gq, gk, kc, vc, wv, sent, got, selq, rbuf, kfull, vt, qs,
    of, st, so, ss, ro, rs, abuf, cat, back, att, pb,
    rx1, ac1, ry1, sy1, ry2, sx2, rx2, ac2,
    lsem, asend, arecv, rsend, rrecv, ksend, krecv, gsend, grecv,
    dsend, drecv, tsend, trecv, usend, urecv, esend, erecv,
):
    j = lax.axis_index("blk")
    h = lax.axis_index("head")
    core = lax.rem(j, 2)
    x, y = lax.div(h, 2), lax.rem(h, 2)
    pending = []

    def blk_at(offset):
        return {"blk": lax.rem(j + offset + NB, NB)}

    sibling = {"blk": j + 1 - 2 * core}

    def head_at(dx, dy):
        other_y = 1 - y if dy else y
        return lax.rem(x + dx, 4) * 2 + other_y

    def send(src, dst, s, r, dev):
        copy = pltpu.make_async_remote_copy(
            src_ref=src, dst_ref=dst, send_sem=s, recv_sem=r, device_id=dev, device_id_type=MESH
        )
        copy.start()
        pending.append(copy)
        return copy

    loads = [
        pltpu.make_async_copy(src, dst, lsem.at[i])
        for i, (src, dst) in enumerate((
            (fresh.at[0], fv.at[0]), (qgain, gq), (fresh.at[1], fv.at[1]), (kgain, gk),
            (fresh.at[2], fv.at[2]), (kcache, kc), (vcache, vc), (weight, wv),
        ))
    ]
    for load in loads:
        load.start()

    barrier = pltpu.get_barrier_semaphore()
    pairs = [(dx, dy) for dx in range(4) for dy in range(2) if dx or dy]
    for dx, dy in pairs:
        pl.semaphore_signal(barrier, inc=1, device_id={"head": head_at(dx, dy)}, device_id_type=MESH)
    for offset in (-2, -1, 1, 2):
        pl.semaphore_signal(barrier, inc=1, device_id=blk_at(offset), device_id_type=MESH)

    live = counts[j]
    before = jnp.int32(0)
    for i in range(NB):
        before = before + jnp.where(i < j, counts[i], 0)
    shift = before - CH * j + BASE

    my_rows = pl.ds(pl.multiple_of(h * ROWS, ROWS), ROWS)
    a_copies = [[], [], []]

    def prepare(t):
        loads[2 * t].wait()
        if t == 2:
            for g in range(NG):
                sent[t, g] = fv[t, :, g * GROUP:(g + 1) * GROUP]
        else:
            loads[2 * t + 1].wait()
            rows = fv[t].astype(F32)
            factor = lax.rsqrt(jnp.mean(rows * rows, axis=-1, keepdims=True) + EPS)
            gains = (gq if t == 0 else gk)[...].astype(F32)
            for c in range(D // HEAD_DIM):
                cols = slice(c * HEAD_DIM, (c + 1) * HEAD_DIM)
                to = slice(c % NH * HEAD_DIM, (c % NH + 1) * HEAD_DIM)
                sent[t, c // NH, :, to] = (rows[:, cols] * factor * gains[c:c + 1]).astype(BF)
        got[t, my_rows] = sent[t, h]

    def spread(t):
        for n, (dx, dy) in enumerate(pairs):
            peer = head_at(dx, dy)
            a_copies[t].append(send(
                sent.at[t, peer], got.at[t, my_rows], asend.at[t, n], arecv.at[t, n], {"head": peer}
            ))

    prepare(0)
    pl.semaphore_wait(barrier, len(pairs) + 4)
    spread(0)
    prepare(1)
    prepare(2)

    r_id = lax.broadcasted_iota(jnp.int32, (SPAN, CAP), 0)
    s_id = lax.broadcasted_iota(jnp.int32, (1, CAP), 1)
    place = jnp.where(r_id == jnp.where(s_id < live, s_id + shift, -1), 1.0, 0.0).astype(BF)
    for copy in a_copies[0]:
        copy.wait_recv()
    selq[...] = mm(place, got[0]).astype(BF)
    r_copies = [
        send(selq.at[pl.ds(first, size)], rbuf.at[pl.ds(to, size)], rsend.at[n], rrecv.at[n], blk_at(offset))
        for n, (first, size, to, offset) in enumerate(
            ((64, 128, 0, -1), (320, 128, 128, 1), (0, 64, 256, -2), (448, 64, 320, 2))
        )
    ]
    spread(1)
    spread(2)
    back[...] = place.T
    st[...] = jnp.zeros_like(st)
    pos = lax.broadcasted_iota(jnp.int32, (L_BLK, CAP), 0)
    hits = jnp.where(pos == jnp.where(s_id < live, ridx[...], -1), 1.0, 0.0)
    hit = jnp.sum(hits, axis=1, keepdims=True) > 0.5
    hits = hits.astype(BF)
    for copy in r_copies:
        copy.wait_recv()
    mine = (selq[192:320].astype(F32) + rbuf[0:128].astype(F32)) + rbuf[128:256].astype(F32)
    qs[0, 0:64] = (mine[0:64] + rbuf[320:384].astype(F32)).astype(BF)
    qs[0, 64:128] = (mine[64:128] + rbuf[256:320].astype(F32)).astype(BF)

    halves = (pl.ds(0, 64), pl.ds(64, 64))

    def gather_step(step):
        copies = []
        for half in range(2):
            for way in range(2):
                if step == 4 and half != way:
                    continue
                src = (8 - (step - 1)) % 8 if way == 0 else step - 1
                dst = 8 - step if way == 0 else step
                copies.append(send(
                    qs.at[src, halves[half]], qs.at[dst, halves[half]],
                    gsend.at[way, step - 1, half], grecv.at[way, step - 1, half],
                    blk_at(2 if way == 0 else -2),
                ))
        return copies

    g_copies = gather_step(1)
    for copy in g_copies:
        copy.wait_recv()
    g_copies = gather_step(2)

    for t in (1, 2):
        for copy in a_copies[t]:
            copy.wait_recv()
    loads[5].wait()
    loads[6].wait()
    kfull[0] = jnp.where(hit, mm(hits, got[1]), kc[...].astype(F32)).astype(BF)
    k_copy = send(kfull.at[0], kfull.at[1], ksend.at[0], krecv.at[0], sibling)
    vt[0] = jnp.where(hit, mm(hits, got[2]), vc[...].astype(F32)).T.astype(BF)
    v_copy = send(vt.at[0], vt.at[1], ksend.at[1], krecv.at[1], sibling)

    def attend(slots):
        width = CH * len(slots)
        for i in range(NH):
            cols = slice(i * HEAD_DIM, (i + 1) * HEAD_DIM)
            if len(slots) == 1:
                query = qs[slots[0], :, cols]
            else:
                query = jnp.concatenate([qs[s, :, cols] for s in slots], axis=0)
            s0 = nt(kfull[0, :, cols], query)
            s1 = nt(kfull[1, :, cols], query)
            top = jnp.maximum(jnp.max(s0, axis=0, keepdims=True), jnp.max(s1, axis=0, keepdims=True)) * SCALE2
            p0 = jnp.exp2(s0 * SCALE2 - top)
            p1 = jnp.exp2(s1 * SCALE2 - top)
            total = jnp.sum(p0, axis=0, keepdims=True) + jnp.sum(p1, axis=0, keepdims=True)
            o = mm(vt[0, cols, :], p0.astype(BF)) + mm(vt[1, cols, :], p1.astype(BF))
            part, row = (0, i) if i < 3 else (1, i - 3)
            for n, s in enumerate(slots):
                lanes = slice(n * CH, (n + 1) * CH)
                of[s, cols, :] = o[:, lanes]
                st[s, part, row:row + 1, :] = top[:, lanes]
                st[s, part, 8 + row:9 + row, :] = total[:, lanes]

    for copy in g_copies:
        copy.wait_recv()
    g_copies = gather_step(3)
    k_copy.wait_recv()
    v_copy.wait_recv()
    attend((7, 1))
    attend((6, 2))
    for copy in g_copies:
        copy.wait_recv()
    g_copies = gather_step(4)
    attend((5, 3))
    for copy in g_copies:
        copy.wait_recv()
    attend((4,))

    def part_rows(part):
        first, last = PART[part]
        return pl.ds(first * HEAD_DIM, (last - first) * HEAD_DIM)

    def joined(slot, part, arrivals):
        first, last = PART[part]
        tops = [st[slot, part, 0:8]] + [rs[way, step, part, 0:8] for way, step in arrivals]
        sums = [st[slot, part, 8:16]] + [rs[way, step, part, 8:16] for way, step in arrivals]
        top = functools.reduce(jnp.maximum, tops)
        factors = [jnp.exp2(t - top) for t in tops]
        total = sum(a * f for a, f in zip(sums, factors))
        values = []
        for i in range(first, last):
            rows = slice(i * HEAD_DIM, (i + 1) * HEAD_DIM)
            k = i - first
            value = of[slot, rows, :] * factors[0][k:k + 1]
            for n, (way, step) in enumerate(arrivals):
                value = value + ro[way, step, rows, :].astype(F32) * factors[n + 1][k:k + 1]
            values.append(value)
        return values, top, total

    d_copies = {}

    def give(way, step, part):
        ahead = 5 - step
        slot = ahead if way == 0 else 8 - ahead
        first_step = 1 if part == way else 2
        if step > first_step:
            for copy in d_copies[way, step - 1, part]:
                copy.wait_recv()
            values, top, total = joined(slot, part, [(way, step - 2)])
        else:
            first, last = PART[part]
            values = [of[slot, i * HEAD_DIM:(i + 1) * HEAD_DIM, :] for i in range(first, last)]
            top, total = st[slot, part, 0:8], st[slot, part, 8:16]
        for n, value in enumerate(values):
            i = PART[part][0] + n
            so[way, step - 1, i * HEAD_DIM:(i + 1) * HEAD_DIM, :] = value.astype(BF)
        ss[way, step - 1, part, 0:8] = top
        ss[way, step - 1, part, 8:16] = total
        rows = part_rows(part)
        dev = blk_at(2 if way == 0 else -2)
        d_copies[way, step, part] = [
            send(ss.at[way, step - 1, part], rs.at[way, step - 1, part],
                 tsend.at[way, step - 1, part], trecv.at[way, step - 1, part], dev),
            send(so.at[way, step - 1, rows], ro.at[way, step - 1, rows],
                 dsend.at[way, step - 1, part], drecv.at[way, step - 1, part], dev),
        ]

    give(0, 1, 0)
    give(1, 1, 1)
    give(0, 2, 1)
    give(1, 2, 0)
    attend((0,))
    give(0, 2, 0)
    give(1, 2, 1)
    for step in (3, 4):
        give(0, step, 1)
        give(1, step, 0)
        give(0, step, 0)
        give(1, step, 1)
    for part in (1, 0):
        for way in range(2):
            for copy in d_copies[way, 4, part]:
                copy.wait_recv()
        values, _, total = joined(0, part, [(0, 3), (1, 3)])
        for n, value in enumerate(values):
            i = PART[part][0] + n
            result = (value / total[n:n + 1]).T.astype(BF)
            abuf[:, i * HEAD_DIM:(i + 1) * HEAD_DIM] = result

    u_copies = [
        send(abuf.at[pl.ds(first, size)], cat.at[pl.ds(to, size)], usend.at[n], urecv.at[n], blk_at(offset))
        for n, (first, size, to, offset) in enumerate(
            ((0, 128, 320, -1), (0, 128, 64, 1), (0, 64, 448, -2), (64, 64, 0, 2))
        )
    ]
    cat[192:320] = abuf[...]
    for copy in u_copies:
        copy.wait_recv()
    att[...] = mm(back[...], cat[...]).astype(BF)

    loads[7].wait()

    def project(first, last):
        @pl.loop(first // 512, last // 512)
        def _(i):
            cols = pl.ds(pl.multiple_of(i * 512, 512), 512)
            tile = mm(att[...], wv[:, cols]).astype(BF)
            for g in range(NG):
                pb[g // 2, g % 2, :, cols] = tile[g * ROWS:(g + 1) * ROWS]

    up, down, far = lax.rem(x + 1, 4), lax.rem(x + 3, 4), lax.rem(x + 2, 4)
    to_up, to_down = {"head": up * 2 + y}, {"head": down * 2 + y}
    to_pair = {"head": x * 2 + 1 - y}
    a1, b1 = pl.ds(0, C1H), pl.ds(C1H, C1H)
    a2, b2 = pl.ds(C1, C2H), pl.ds(C1 + C2H, C2H)

    project(0, C1H)
    e = {}
    e["p1"] = send(pb.at[far, :, :, a1], rx1.at[0], esend.at[0], erecv.at[0], to_up)
    e["m2"] = send(pb.at[down, :, :, a1], rx1.at[1], esend.at[1], erecv.at[1], to_down)
    project(C1, C1 + C2H)
    e["y2"] = send(pb.at[:, 1 - y, :, a2], ry2.at[:, :, 0:C2H], esend.at[2], erecv.at[2], to_pair)
    project(C1H, C1)
    e["m1"] = send(pb.at[far, :, :, b1], rx1.at[2], esend.at[3], erecv.at[3], to_down)
    e["p2"] = send(pb.at[up, :, :, b1], rx1.at[3], esend.at[4], erecv.at[4], to_up)
    project(C1 + C2H, D)
    e["y3"] = send(pb.at[:, 1 - y, :, b2], ry2.at[:, :, C2H:C2], esend.at[14], erecv.at[14], to_pair)

    e["p1"].wait_recv()
    ac1[0] = (rx1[0].astype(F32) + pb[up, :, :, 0:C1H].astype(F32)).astype(BF)
    e["p3"] = send(ac1.at[0], rx1.at[4], esend.at[5], erecv.at[5], to_up)
    e["m1"].wait_recv()
    ac1[1] = (rx1[2].astype(F32) + pb[down, :, :, C1H:C1].astype(F32)).astype(BF)
    e["m3"] = send(ac1.at[1], rx1.at[5], esend.at[6], erecv.at[6], to_down)

    e["y2"].wait_recv()
    e["y3"].wait_recv()
    for i in range(4):
        sx2[i] = (ry2[i].astype(F32) + pb[i, y, :, C1:D].astype(F32)).astype(BF)
    a2, b2 = pl.ds(0, C2H), pl.ds(C2H, C2H)
    e["P1"] = send(sx2.at[far, :, a2], rx2.at[0], esend.at[7], erecv.at[7], to_up)
    e["M1"] = send(sx2.at[far, :, b2], rx2.at[2], esend.at[8], erecv.at[8], to_down)
    e["M2"] = send(sx2.at[down, :, a2], rx2.at[1], esend.at[9], erecv.at[9], to_down)
    e["P2"] = send(sx2.at[up, :, b2], rx2.at[3], esend.at[10], erecv.at[10], to_up)

    def five(own, one, two):
        return own.astype(F32) + one.astype(F32) + two.astype(F32)

    for name in ("m2", "p2", "p3", "m3"):
        e[name].wait_recv()
    sy1[:, 0:C1H] = five(pb[x, 1 - y, :, 0:C1H], rx1[4, 1 - y], rx1[1, 1 - y]).astype(BF)
    sy1[:, C1H:C1] = five(pb[x, 1 - y, :, C1H:C1], rx1[5, 1 - y], rx1[3, 1 - y]).astype(BF)
    e["y1"] = send(sy1, ry1, esend.at[11], erecv.at[11], to_pair)

    e["P1"].wait_recv()
    ac2[0] = (rx2[0].astype(F32) + sx2[up, :, 0:C2H].astype(F32)).astype(BF)
    e["P3"] = send(ac2.at[0], rx2.at[4], esend.at[12], erecv.at[12], to_up)
    e["M1"].wait_recv()
    ac2[1] = (rx2[2].astype(F32) + sx2[down, :, C2H:C2].astype(F32)).astype(BF)
    e["M3"] = send(ac2.at[1], rx2.at[5], esend.at[13], erecv.at[13], to_down)

    e["y1"].wait_recv()
    own_a = five(pb[x, y, :, 0:C1H], rx1[4, y], rx1[1, y])
    out[:, 0:C1H] = (own_a + ry1[:, 0:C1H].astype(F32)).astype(BF)
    own_b = five(pb[x, y, :, C1H:C1], rx1[5, y], rx1[3, y])
    out[:, C1H:C1] = (own_b + ry1[:, C1H:C1].astype(F32)).astype(BF)
    for name in ("M2", "P2", "P3", "M3"):
        e[name].wait_recv()
    out[:, C1:C1 + C2H] = five(sx2[x, :, 0:C2H], rx2[4], rx2[1]).astype(BF)
    out[:, C1 + C2H:D] = five(sx2[x, :, C2H:C2], rx2[5], rx2[3]).astype(BF)

    for copy in pending:
        copy.wait_send()


def local(fresh, rows_index, counts, key_cache, value_cache, q_gain, k_gain, out_weight):
    any_spec = pl.BlockSpec(memory_space=pl.ANY)
    vmem = pl.BlockSpec(memory_space=pltpu.VMEM)
    dma = pltpu.SemaphoreType.DMA
    V = pltpu.VMEM
    return pl.pallas_call(
        kernel,
        out_shape=jax.ShapeDtypeStruct((ROWS, D), BF),
        in_specs=[any_spec, vmem, pl.BlockSpec(memory_space=pltpu.SMEM)] + [any_spec] * 5,
        out_specs=vmem,
        scratch_shapes=[
            V((3, ROWS, D), BF), V((D // 128, 128), BF), V((D // 128, 128), BF),
            V((L_BLK, GROUP), BF), V((L_BLK, GROUP), BF), V((GROUP, D), BF),
            V((3, NG, ROWS, GROUP), BF), V((3, CAP, GROUP), BF),
            V((SPAN, GROUP), BF), V((384, GROUP), BF),
            V((2, L_BLK, GROUP), BF), V((2, GROUP, L_BLK), BF), V((8, CH, GROUP), BF),
            V((8, GROUP, CH), F32), V((8, 2, 16, CH), F32),
            V((2, 4, GROUP, CH), BF), V((2, 4, 2, 16, CH), F32),
            V((2, 4, GROUP, CH), BF), V((2, 4, 2, 16, CH), F32),
            V((CH, GROUP), BF), V((SPAN, GROUP), BF), V((CAP, SPAN), BF), V((CAP, GROUP), BF),
            V((4, 2, ROWS, D), BF),
            V((6, 2, ROWS, C1H), BF), V((2, 2, ROWS, C1H), BF),
            V((ROWS, C1), BF), V((ROWS, C1), BF),
            V((4, ROWS, C2), BF), V((4, ROWS, C2), BF),
            V((6, ROWS, C2H), BF), V((2, ROWS, C2H), BF),
            dma((8,)), dma((3, 7)), dma((3, 7)), dma((4,)), dma((4,)), dma((2,)), dma((2,)),
            dma((2, 4, 2)), dma((2, 4, 2)),
            dma((2, 4, 2)), dma((2, 4, 2)), dma((2, 4, 2)), dma((2, 4, 2)),
            dma((4,)), dma((4,)), dma((15,)), dma((15,)),
        ],
        compiler_params=pltpu.CompilerParams(
            collective_id=0, has_side_effects=True, vmem_limit_bytes=56 * 1024 * 1024
        ),
    )(
        jnp.transpose(fresh, (1, 0, 2)), rows_index.reshape(1, CAP), counts, key_cache, value_cache,
        q_gain.reshape(D // 128, 128), k_gain.reshape(D // 128, 128), out_weight,
    )


def solution(mesh):
    placed = (
        P(("cfg", "blk", "head"), None, None),
        P("blk"),
        P(),
        P(("cfg", "blk"), "head"),
        P(("cfg", "blk"), "head"),
        P(),
        P(),
        P("head", None),
    )
    return jax.shard_map(
        local,
        mesh=mesh,
        in_specs=placed,
        out_specs=P(("cfg", "blk", "head"), None),
        check_vma=False,
    )
```

```python
import functools
import math

import jax
import jax.numpy as jnp
from jax import lax
from jax.experimental import pallas as pl
from jax.experimental.pallas import tpu as pltpu
from jax.sharding import PartitionSpec as P

HEAD_DIM = 128
EPS = 1e-06
MESH = pl.DeviceIdType.MESH
BF = jnp.bfloat16
F32 = jnp.float32

D = 5120
GROUP = 640
NH = GROUP // HEAD_DIM
NG = 8
NB = 16
CAP = 256
L_BLK = 512
ROWS = 32
CH = 128
SPAN = 512
BASE = 192
PIECES = ((0, 2), (2, 4), (4, 5))
NP = len(PIECES)
WIDTH = tuple((last - first) * HEAD_DIM for first, last in PIECES)
LONG = ((0,), (1, 2))
C1 = 3072
C1H = C1 // 2
C2 = D - C1
C2H = C2 // 2
SCALE2 = math.log2(math.e) / math.sqrt(HEAD_DIM)


def nt(a, b):
    return lax.dot_general(a, b, (((1,), (1,)), ((), ())), preferred_element_type=F32)


def mm(a, b):
    return jnp.dot(a, b, preferred_element_type=F32)


def kernel(
    fresh, ridx, counts, kcache, vcache, qgain, kgain, weight, out,
    fv, gq, gk, kc, vc, wv, sent, got, sentq, gotq, selq, rbuf, kfull, vt, qs,
    of, st, so, ss, ro, rs, abuf, cat, back, att, pb,
    rx1, ac1, ry1, sy1, ry2, sx2, rx2, ac2,
    lsem, qsend, qrecv, asend, arecv, rsend, rrecv, ksend, krecv, gsend, grecv,
    dsend, drecv, tsend, trecv, usend, urecv, esend, erecv,
):
    j = lax.axis_index("blk")
    h = lax.axis_index("head")
    core = lax.rem(j, 2)
    x, y = lax.div(h, 2), lax.rem(h, 2)
    pending = []

    def blk_at(offset):
        return {"blk": lax.rem(j + offset + NB, NB)}

    sibling = {"blk": j + 1 - 2 * core}

    def head_at(dx, dy):
        other_y = 1 - y if dy else y
        return lax.rem(x + dx, 4) * 2 + other_y

    def send(src, dst, s, r, dev):
        copy = pltpu.make_async_remote_copy(
            src_ref=src, dst_ref=dst, send_sem=s, recv_sem=r, device_id=dev, device_id_type=MESH
        )
        copy.start()
        pending.append(copy)
        return copy

    loads = [
        pltpu.make_async_copy(src, dst, lsem.at[i])
        for i, (src, dst) in enumerate((
            (fresh.at[0], fv.at[0]), (qgain, gq), (fresh.at[1], fv.at[1]), (kgain, gk),
            (fresh.at[2], fv.at[2]), (kcache, kc), (vcache, vc), (weight, wv),
        ))
    ]
    for load in loads[:6]:
        load.start()

    barrier = pltpu.get_barrier_semaphore()
    pairs = [(dx, dy) for dx in range(4) for dy in range(2) if dx or dy]
    for dx, dy in pairs:
        pl.semaphore_signal(barrier, inc=1, device_id={"head": head_at(dx, dy)}, device_id_type=MESH)
    for offset in (-2, -1, 1, 2):
        pl.semaphore_signal(barrier, inc=1, device_id=blk_at(offset), device_id_type=MESH)

    live = counts[j]
    before = jnp.int32(0)
    for i in range(NB):
        before = before + jnp.where(i < j, counts[i], 0)
    shift = before - CH * j + BASE

    my_rows = pl.ds(pl.multiple_of(h * ROWS, ROWS), ROWS)
    a_copies = [[], []]
    q_copies = [[] for _ in PIECES]

    def piece_of(head):
        for p, (first, last) in enumerate(PIECES):
            if head < last:
                return p, head - first

    def prepare(t):
        loads[2 * t].wait()
        if t == 2:
            for g in range(NG):
                sent[1, g] = fv[t, :, g * GROUP:(g + 1) * GROUP]
            got[1, my_rows] = sent[1, h]
            return
        loads[2 * t + 1].wait()
        rows = fv[t].astype(F32)
        factor = lax.rsqrt(jnp.mean(rows * rows, axis=-1, keepdims=True) + EPS)
        gains = (gq if t == 0 else gk)[...].astype(F32)
        for c in range(D // HEAD_DIM):
            cols = slice(c * HEAD_DIM, (c + 1) * HEAD_DIM)
            g, i = c // NH, c % NH
            value = (rows[:, cols] * factor * gains[c:c + 1]).astype(BF)
            if t == 0:
                p, n = piece_of(i)
                sentq[p][g, :, n * HEAD_DIM:(n + 1) * HEAD_DIM] = value
            else:
                sent[0, g, :, i * HEAD_DIM:(i + 1) * HEAD_DIM] = value
        if t == 0:
            for p in range(NP):
                gotq[p][my_rows] = sentq[p][h]
        else:
            got[0, my_rows] = sent[0, h]

    def spread(t):
        for n, (dx, dy) in enumerate(pairs):
            peer = head_at(dx, dy)
            a_copies[t].append(send(
                sent.at[t, peer], got.at[t, my_rows], asend.at[t, n], arecv.at[t, n], {"head": peer}
            ))

    prepare(0)
    pl.semaphore_wait(barrier, len(pairs) + 4)
    for p in range(NP):
        for n, (dx, dy) in enumerate(pairs):
            peer = head_at(dx, dy)
            q_copies[p].append(send(
                sentq[p].at[peer], gotq[p].at[my_rows], qsend.at[p, n], qrecv.at[p, n], {"head": peer}
            ))
    for load in loads[6:]:
        load.start()
    prepare(1)
    prepare(2)

    r_id = lax.broadcasted_iota(jnp.int32, (SPAN, CAP), 0)
    s_id = lax.broadcasted_iota(jnp.int32, (1, CAP), 1)
    place = jnp.where(r_id == jnp.where(s_id < live, s_id + shift, -1), 1.0, 0.0).astype(BF)
    r_copies = []
    for p in range(NP):
        for copy in q_copies[p]:
            copy.wait_recv()
        selq[p][...] = mm(place, gotq[p][...]).astype(BF)
        r_copies.append([
            send(selq[p].at[pl.ds(first, size)], rbuf[p].at[pl.ds(to, size)],
                 rsend.at[p, n], rrecv.at[p, n], blk_at(offset))
            for n, (first, size, to, offset) in enumerate(
                ((64, 128, 0, -1), (320, 128, 128, 1), (0, 64, 256, -2), (448, 64, 320, 2))
            )
        ])
        if p < 2:
            spread(p)
    back[...] = place.T
    st[...] = jnp.zeros_like(st)
    pos = lax.broadcasted_iota(jnp.int32, (L_BLK, CAP), 0)
    hits = jnp.where(pos == jnp.where(s_id < live, ridx[...], -1), 1.0, 0.0)
    hit = jnp.sum(hits, axis=1, keepdims=True) > 0.5
    hits = hits.astype(BF)

    g_copies = {}

    def gather_send(way, step, p):
        src = (8 - (step - 1)) % 8 if way == 0 else step - 1
        dst = 8 - step if way == 0 else step
        g_copies[way, step, p] = send(
            qs[p].at[src], qs[p].at[dst],
            gsend.at[way, step - 1, p], grecv.at[way, step - 1, p], blk_at(2 if way == 0 else -2),
        )

    def gather_step(step):
        for p in range(NP):
            for way in range(2):
                g_copies[way, step - 1, p].wait_recv()
                if step < 4 or p in LONG[way]:
                    gather_send(way, step, p)

    for p in range(NP):
        for copy in r_copies[p]:
            copy.wait_recv()
        mine = (selq[p][192:320].astype(F32) + rbuf[p][0:128].astype(F32)) + rbuf[p][128:256].astype(F32)
        qs[p][0, 0:64] = (mine[0:64] + rbuf[p][320:384].astype(F32)).astype(BF)
        qs[p][0, 64:128] = (mine[64:128] + rbuf[p][256:320].astype(F32)).astype(BF)
        gather_send(0, 1, p)
        gather_send(1, 1, p)
    gather_step(2)

    for t in range(2):
        for copy in a_copies[t]:
            copy.wait_recv()
    loads[5].wait()
    loads[6].wait()
    kfull[0] = jnp.where(hit, mm(hits, got[0]), kc[...].astype(F32)).astype(BF)
    k_copy = send(kfull.at[0], kfull.at[1], ksend.at[0], krecv.at[0], sibling)
    vt[0] = jnp.where(hit, mm(hits, got[1]), vc[...].astype(F32)).T.astype(BF)
    v_copy = send(vt.at[0], vt.at[1], ksend.at[1], krecv.at[1], sibling)

    def attend(slots, heads):
        for i in heads:
            p, k = piece_of(i)
            cols = slice(i * HEAD_DIM, (i + 1) * HEAD_DIM)
            query = [qs[p][s, :, k * HEAD_DIM:(k + 1) * HEAD_DIM] for s in slots]
            query = query[0] if len(slots) == 1 else jnp.concatenate(query, axis=0)
            s0 = nt(kfull[0, :, cols], query)
            s1 = nt(kfull[1, :, cols], query)
            top = jnp.maximum(jnp.max(s0, axis=0, keepdims=True), jnp.max(s1, axis=0, keepdims=True)) * SCALE2
            p0 = jnp.exp2(s0 * SCALE2 - top)
            p1 = jnp.exp2(s1 * SCALE2 - top)
            total = jnp.sum(p0, axis=0, keepdims=True) + jnp.sum(p1, axis=0, keepdims=True)
            o = mm(vt[0, cols, :], p0.astype(BF)) + mm(vt[1, cols, :], p1.astype(BF))
            for n, s in enumerate(slots):
                lanes = slice(n * CH, (n + 1) * CH)
                of[s, cols, :] = o[:, lanes]
                st[s, p, k:k + 1, :] = top[:, lanes]
                st[s, p, 4 + k:5 + k, :] = total[:, lanes]

    gather_step(3)
    k_copy.wait_recv()
    v_copy.wait_recv()
    attend((7, 1), range(3))
    gather_step(4)
    attend((7, 1), range(3, NH))
    attend((6, 2), range(NH))

    def joined(slot, p, arrivals):
        first, last = PIECES[p]
        tops = [st[slot, p, 0:4]] + [rs[way, step, p, 0:4] for way, step in arrivals]
        sums = [st[slot, p, 4:8]] + [rs[way, step, p, 4:8] for way, step in arrivals]
        top = functools.reduce(jnp.maximum, tops)
        factors = [jnp.exp2(t - top) for t in tops]
        total = sum(a * f for a, f in zip(sums, factors))
        values = []
        for i in range(first, last):
            rows = slice(i * HEAD_DIM, (i + 1) * HEAD_DIM)
            k = i - first
            value = of[slot, rows, :] * factors[0][k:k + 1]
            for n, (way, step) in enumerate(arrivals):
                value = value + ro[way, step, rows, :].astype(F32) * factors[n + 1][k:k + 1]
            values.append(value)
        return values, top, total

    d_copies = {}

    def give(way, step, p):
        ahead = 5 - step
        slot = ahead if way == 0 else 8 - ahead
        first, last = PIECES[p]
        if step > (1 if p in LONG[way] else 2):
            for copy in d_copies[way, step - 1, p]:
                copy.wait_recv()
            values, top, total = joined(slot, p, [(way, step - 2)])
        else:
            values = [of[slot, i * HEAD_DIM:(i + 1) * HEAD_DIM, :] for i in range(first, last)]
            top, total = st[slot, p, 0:4], st[slot, p, 4:8]
        for n, value in enumerate(values):
            i = first + n
            so[way, step - 1, i * HEAD_DIM:(i + 1) * HEAD_DIM, :] = value.astype(BF)
        ss[way, step - 1, p, 0:4] = top
        ss[way, step - 1, p, 4:8] = total
        rows = pl.ds(first * HEAD_DIM, WIDTH[p])
        dev = blk_at(2 if way == 0 else -2)
        d_copies[way, step, p] = [
            send(ss.at[way, step - 1, p], rs.at[way, step - 1, p],
                 tsend.at[way, step - 1, p], trecv.at[way, step - 1, p], dev),
            send(so.at[way, step - 1, rows], ro.at[way, step - 1, rows],
                 dsend.at[way, step - 1, p], drecv.at[way, step - 1, p], dev),
        ]

    for p in range(NP):
        way = 0 if p in LONG[0] else 1
        g_copies[way, 4, p].wait_recv()
        attend((4,), range(*PIECES[p]))
        give(way, 1, p)
    for way in range(2):
        for p in LONG[1 - way]:
            attend((5, 3), range(*PIECES[p]))
            give(way, 2, p)
    for way in range(2):
        for p in LONG[way]:
            give(way, 2, p)
    attend((0,), range(NH))
    order = ((0, 1), (1, 0), (0, 2), (0, 0), (1, 1), (1, 2))
    for step in (3, 4):
        for way, p in order:
            give(way, step, p)

    u_copies = {}
    for p in (1, 0, 2):
        for way in range(2):
            for copy in d_copies[way, 4, p]:
                copy.wait_recv()
        values, _, total = joined(0, p, [(0, 3), (1, 3)])
        for n, value in enumerate(values):
            result = (value / total[n:n + 1]).T.astype(BF)
            abuf[p][:, n * HEAD_DIM:(n + 1) * HEAD_DIM] = result
        u_copies[p] = [
            send(abuf[p].at[pl.ds(first, size)], cat[p].at[pl.ds(to, size)],
                 usend.at[p, n], urecv.at[p, n], blk_at(offset))
            for n, (first, size, to, offset) in enumerate(
                ((0, 128, 320, -1), (0, 128, 64, 1), (0, 64, 448, -2), (64, 64, 0, 2))
            )
        ]
        cat[p][192:320] = abuf[p][...]
    for p in (1, 0, 2):
        for copy in u_copies[p]:
            copy.wait_recv()
        first = PIECES[p][0] * HEAD_DIM
        att[:, first:first + WIDTH[p]] = mm(back[...], cat[p][...]).astype(BF)

    loads[7].wait()

    def project(first, last):
        @pl.loop(first // 512, last // 512)
        def _(i):
            cols = pl.ds(pl.multiple_of(i * 512, 512), 512)
            tile = mm(att[...], wv[:, cols]).astype(BF)
            for g in range(NG):
                pb[g // 2, g % 2, :, cols] = tile[g * ROWS:(g + 1) * ROWS]

    up, down, far = lax.rem(x + 1, 4), lax.rem(x + 3, 4), lax.rem(x + 2, 4)
    to_up, to_down = {"head": up * 2 + y}, {"head": down * 2 + y}
    to_pair = {"head": x * 2 + 1 - y}
    a1, b1 = pl.ds(0, C1H), pl.ds(C1H, C1H)
    a2, b2 = pl.ds(C1, C2H), pl.ds(C1 + C2H, C2H)

    project(0, C1H)
    e = {}
    e["p1"] = send(pb.at[far, :, :, a1], rx1.at[0], esend.at[0], erecv.at[0], to_up)
    e["m2"] = send(pb.at[down, :, :, a1], rx1.at[1], esend.at[1], erecv.at[1], to_down)
    project(C1, C1 + C2H)
    e["y2"] = send(pb.at[:, 1 - y, :, a2], ry2.at[:, :, 0:C2H], esend.at[2], erecv.at[2], to_pair)
    project(C1H, C1)
    e["m1"] = send(pb.at[far, :, :, b1], rx1.at[2], esend.at[3], erecv.at[3], to_down)
    e["p2"] = send(pb.at[up, :, :, b1], rx1.at[3], esend.at[4], erecv.at[4], to_up)
    project(C1 + C2H, D)
    e["y3"] = send(pb.at[:, 1 - y, :, b2], ry2.at[:, :, C2H:C2], esend.at[14], erecv.at[14], to_pair)

    e["p1"].wait_recv()
    ac1[0] = (rx1[0].astype(F32) + pb[up, :, :, 0:C1H].astype(F32)).astype(BF)
    e["p3"] = send(ac1.at[0], rx1.at[4], esend.at[5], erecv.at[5], to_up)
    e["m1"].wait_recv()
    ac1[1] = (rx1[2].astype(F32) + pb[down, :, :, C1H:C1].astype(F32)).astype(BF)
    e["m3"] = send(ac1.at[1], rx1.at[5], esend.at[6], erecv.at[6], to_down)

    e["y2"].wait_recv()
    e["y3"].wait_recv()
    for i in range(4):
        sx2[i] = (ry2[i].astype(F32) + pb[i, y, :, C1:D].astype(F32)).astype(BF)
    a2, b2 = pl.ds(0, C2H), pl.ds(C2H, C2H)
    e["P1"] = send(sx2.at[far, :, a2], rx2.at[0], esend.at[7], erecv.at[7], to_up)
    e["M1"] = send(sx2.at[far, :, b2], rx2.at[2], esend.at[8], erecv.at[8], to_down)
    e["M2"] = send(sx2.at[down, :, a2], rx2.at[1], esend.at[9], erecv.at[9], to_down)
    e["P2"] = send(sx2.at[up, :, b2], rx2.at[3], esend.at[10], erecv.at[10], to_up)

    def five(own, one, two):
        return own.astype(F32) + one.astype(F32) + two.astype(F32)

    for name in ("m2", "p2", "p3", "m3"):
        e[name].wait_recv()
    sy1[:, 0:C1H] = five(pb[x, 1 - y, :, 0:C1H], rx1[4, 1 - y], rx1[1, 1 - y]).astype(BF)
    sy1[:, C1H:C1] = five(pb[x, 1 - y, :, C1H:C1], rx1[5, 1 - y], rx1[3, 1 - y]).astype(BF)
    e["y1"] = send(sy1, ry1, esend.at[11], erecv.at[11], to_pair)

    e["P1"].wait_recv()
    ac2[0] = (rx2[0].astype(F32) + sx2[up, :, 0:C2H].astype(F32)).astype(BF)
    e["P3"] = send(ac2.at[0], rx2.at[4], esend.at[12], erecv.at[12], to_up)
    e["M1"].wait_recv()
    ac2[1] = (rx2[2].astype(F32) + sx2[down, :, C2H:C2].astype(F32)).astype(BF)
    e["M3"] = send(ac2.at[1], rx2.at[5], esend.at[13], erecv.at[13], to_down)

    e["y1"].wait_recv()
    own_a = five(pb[x, y, :, 0:C1H], rx1[4, y], rx1[1, y])
    out[:, 0:C1H] = (own_a + ry1[:, 0:C1H].astype(F32)).astype(BF)
    own_b = five(pb[x, y, :, C1H:C1], rx1[5, y], rx1[3, y])
    out[:, C1H:C1] = (own_b + ry1[:, C1H:C1].astype(F32)).astype(BF)
    for name in ("M2", "P2", "P3", "M3"):
        e[name].wait_recv()
    out[:, C1:C1 + C2H] = five(sx2[x, :, 0:C2H], rx2[4], rx2[1]).astype(BF)
    out[:, C1 + C2H:D] = five(sx2[x, :, C2H:C2], rx2[5], rx2[3]).astype(BF)

    for copy in pending:
        copy.wait_send()


def local(fresh, rows_index, counts, key_cache, value_cache, q_gain, k_gain, out_weight):
    any_spec = pl.BlockSpec(memory_space=pl.ANY)
    vmem = pl.BlockSpec(memory_space=pltpu.VMEM)
    dma = pltpu.SemaphoreType.DMA
    V = pltpu.VMEM

    def by_piece(*dims):
        return [V(dims + (width,), BF) for width in WIDTH]

    return pl.pallas_call(
        kernel,
        out_shape=jax.ShapeDtypeStruct((ROWS, D), BF),
        in_specs=[any_spec, vmem, pl.BlockSpec(memory_space=pltpu.SMEM)] + [any_spec] * 5,
        out_specs=vmem,
        scratch_shapes=[
            V((3, ROWS, D), BF), V((D // 128, 128), BF), V((D // 128, 128), BF),
            V((L_BLK, GROUP), BF), V((L_BLK, GROUP), BF), V((GROUP, D), BF),
            V((2, NG, ROWS, GROUP), BF), V((2, CAP, GROUP), BF),
            by_piece(NG, ROWS), by_piece(CAP), by_piece(SPAN), by_piece(384),
            V((2, L_BLK, GROUP), BF), V((2, GROUP, L_BLK), BF), by_piece(8, CH),
            V((8, GROUP, CH), F32), V((8, NP, 8, CH), F32),
            V((2, 4, GROUP, CH), BF), V((2, 4, NP, 8, CH), F32),
            V((2, 4, GROUP, CH), BF), V((2, 4, NP, 8, CH), F32),
            by_piece(CH), by_piece(SPAN), V((CAP, SPAN), BF), V((CAP, GROUP), BF),
            V((4, 2, ROWS, D), BF),
            V((6, 2, ROWS, C1H), BF), V((2, 2, ROWS, C1H), BF),
            V((ROWS, C1), BF), V((ROWS, C1), BF),
            V((4, ROWS, C2), BF), V((4, ROWS, C2), BF),
            V((6, ROWS, C2H), BF), V((2, ROWS, C2H), BF),
            dma((8,)), dma((NP, 7)), dma((NP, 7)), dma((2, 7)), dma((2, 7)),
            dma((NP, 4)), dma((NP, 4)), dma((2,)), dma((2,)),
            dma((2, 4, NP)), dma((2, 4, NP)),
            dma((2, 4, NP)), dma((2, 4, NP)), dma((2, 4, NP)), dma((2, 4, NP)),
            dma((NP, 4)), dma((NP, 4)), dma((15,)), dma((15,)),
        ],
        compiler_params=pltpu.CompilerParams(
            collective_id=0, has_side_effects=True, vmem_limit_bytes=56 * 1024 * 1024
        ),
    )(
        jnp.transpose(fresh, (1, 0, 2)), rows_index.reshape(1, CAP), counts, key_cache, value_cache,
        q_gain.reshape(D // 128, 128), k_gain.reshape(D // 128, 128), out_weight,
    )


def solution(mesh):
    placed = (
        P(("cfg", "blk", "head"), None, None),
        P("blk"),
        P(),
        P(("cfg", "blk"), "head"),
        P(("cfg", "blk"), "head"),
        P(),
        P(),
        P("head", None),
    )
    return jax.shard_map(
        local,
        mesh=mesh,
        in_specs=placed,
        out_specs=P(("cfg", "blk", "head"), None),
        check_vma=False,
    )
```

```python
import functools
import math

import jax
import jax.numpy as jnp
from jax import lax
from jax.experimental import pallas as pl
from jax.experimental.pallas import tpu as pltpu
from jax.sharding import PartitionSpec as P

HEAD_DIM = 128
EPS = 1e-06
MESH = pl.DeviceIdType.MESH
BF = jnp.bfloat16
F32 = jnp.float32

D = 5120
GROUP = 640
NH = GROUP // HEAD_DIM
NG = 8
NB = 16
CAP = 256
L_BLK = 512
ROWS = 32
CH = 128
SPAN = 512
BASE = 192
PIECES = ((0, 1), (1, 2), (2, 3), (3, 4), (4, 5))
NP = len(PIECES)
WIDTH = tuple((last - first) * HEAD_DIM for first, last in PIECES)
LONG = ((0, 1), (2, 3, 4))
XG = ((0, 1536), (1536, 1024), (2560, 512))
YG = ((3072, 1024), (4096, 512), (4608, 512))
SCALE2 = math.log2(math.e) / math.sqrt(HEAD_DIM)


def nt(a, b):
    return lax.dot_general(a, b, (((1,), (1,)), ((), ())), preferred_element_type=F32)


def mm(a, b):
    return jnp.dot(a, b, preferred_element_type=F32)


def kernel(
    fresh, ridx, counts, kcache, vcache, qgain, kgain, weight, out,
    fv, gq, gk, kc, vc, wv, sent, got, sentq, gotq, selq, rbuf, kfull, vt, qs,
    of, st, so, ss, ro, rs, abuf, cat, back, att, pb,
    rx1, ac1, ry1, sy1, ry2, sx2, rx2, ac2, outv,
    lsem, qsend, qrecv, asend, arecv, rsend, rrecv, ksend, krecv, gsend, grecv,
    dsend, drecv, tsend, trecv, usend, urecv, esend, erecv, osem,
):
    j = lax.axis_index("blk")
    h = lax.axis_index("head")
    core = lax.rem(j, 2)
    x, y = lax.div(h, 2), lax.rem(h, 2)
    pending = []

    def blk_at(offset):
        return {"blk": lax.rem(j + offset + NB, NB)}

    sibling = {"blk": j + 1 - 2 * core}

    def head_at(dx, dy):
        other_y = 1 - y if dy else y
        return lax.rem(x + dx, 4) * 2 + other_y

    def send(src, dst, s, r, dev):
        copy = pltpu.make_async_remote_copy(
            src_ref=src, dst_ref=dst, send_sem=s, recv_sem=r, device_id=dev, device_id_type=MESH
        )
        copy.start()
        pending.append(copy)
        return copy

    loads = [
        pltpu.make_async_copy(src, dst, lsem.at[i])
        for i, (src, dst) in enumerate((
            (fresh.at[0], fv.at[0]), (qgain, gq), (fresh.at[1], fv.at[1]), (kgain, gk),
            (fresh.at[2], fv.at[2]), (kcache, kc), (vcache, vc), (weight, wv),
        ))
    ]
    for load in loads[:6]:
        load.start()

    barrier = pltpu.get_barrier_semaphore()
    pairs = [(dx, dy) for dx in range(4) for dy in range(2) if dx or dy]
    for dx, dy in pairs:
        pl.semaphore_signal(barrier, inc=1, device_id={"head": head_at(dx, dy)}, device_id_type=MESH)
    for offset in (-2, -1, 1, 2):
        pl.semaphore_signal(barrier, inc=1, device_id=blk_at(offset), device_id_type=MESH)

    live = counts[j]
    before = jnp.int32(0)
    for i in range(NB):
        before = before + jnp.where(i < j, counts[i], 0)
    shift = before - CH * j + BASE

    my_rows = pl.ds(pl.multiple_of(h * ROWS, ROWS), ROWS)
    a_copies = [[], []]
    q_copies = [[] for _ in PIECES]

    def piece_of(head):
        for p, (first, last) in enumerate(PIECES):
            if head < last:
                return p, head - first

    def prepare(t):
        loads[2 * t].wait()
        if t == 2:
            for g in range(NG):
                sent[1, g] = fv[t, :, g * GROUP:(g + 1) * GROUP]
            got[1, my_rows] = sent[1, h]
            return
        loads[2 * t + 1].wait()
        rows = fv[t].astype(F32)
        factor = lax.rsqrt(jnp.mean(rows * rows, axis=-1, keepdims=True) + EPS)
        gains = (gq if t == 0 else gk)[...].astype(F32)
        for c in range(D // HEAD_DIM):
            cols = slice(c * HEAD_DIM, (c + 1) * HEAD_DIM)
            g, i = c // NH, c % NH
            value = (rows[:, cols] * factor * gains[c:c + 1] * (SCALE2 if t == 0 else 1.0)).astype(BF)
            if t == 0:
                p, n = piece_of(i)
                sentq[p][g, :, n * HEAD_DIM:(n + 1) * HEAD_DIM] = value
            else:
                sent[0, g, :, i * HEAD_DIM:(i + 1) * HEAD_DIM] = value
        if t == 0:
            for p in range(NP):
                gotq[p][my_rows] = sentq[p][h]
        else:
            got[0, my_rows] = sent[0, h]

    def spread(t):
        for n, (dx, dy) in enumerate(pairs):
            peer = head_at(dx, dy)
            a_copies[t].append(send(
                sent.at[t, peer], got.at[t, my_rows], asend.at[t, n], arecv.at[t, n], {"head": peer}
            ))

    prepare(0)
    pl.semaphore_wait(barrier, len(pairs) + 4)
    for p in range(NP):
        for n, (dx, dy) in enumerate(pairs):
            peer = head_at(dx, dy)
            q_copies[p].append(send(
                sentq[p].at[peer], gotq[p].at[my_rows], qsend.at[p, n], qrecv.at[p, n], {"head": peer}
            ))
    for load in loads[6:]:
        load.start()
    prepare(1)
    spread(0)
    prepare(2)
    spread(1)

    r_id = lax.broadcasted_iota(jnp.int32, (SPAN, CAP), 0)
    s_id = lax.broadcasted_iota(jnp.int32, (1, CAP), 1)
    place = jnp.where(r_id == jnp.where(s_id < live, s_id + shift, -1), 1.0, 0.0).astype(BF)
    r_copies = []
    for p in range(NP):
        for copy in q_copies[p]:
            copy.wait_recv()
        selq[p][...] = mm(place, gotq[p][...]).astype(BF)
        r_copies.append([
            send(selq[p].at[pl.ds(first, size)], rbuf[p].at[pl.ds(to, size)],
                 rsend.at[p, n], rrecv.at[p, n], blk_at(offset))
            for n, (first, size, to, offset) in enumerate(
                ((64, 128, 0, -1), (320, 128, 128, 1), (0, 64, 256, -2), (448, 64, 320, 2))
            )
        ])
    back[...] = place.T
    pos = lax.broadcasted_iota(jnp.int32, (L_BLK, CAP), 0)
    hits = jnp.where(pos == jnp.where(s_id < live, ridx[...], -1), 1.0, 0.0)
    hit = jnp.sum(hits, axis=1, keepdims=True) > 0.5
    hits = hits.astype(BF)

    g_copies = {}

    def gather_send(way, step, p):
        src = (8 - (step - 1)) % 8 if way == 0 else step - 1
        dst = 8 - step if way == 0 else step
        g_copies[way, step, p] = send(
            qs[p].at[src], qs[p].at[dst],
            gsend.at[way, step - 1, p], grecv.at[way, step - 1, p], blk_at(2 if way == 0 else -2),
        )

    def gather_step(step):
        for p in range(NP):
            for way in range(2):
                g_copies[way, step - 1, p].wait_recv()
                if step < 4 or p in LONG[way]:
                    gather_send(way, step, p)

    for p in range(NP):
        for copy in r_copies[p]:
            copy.wait_recv()
        mine = (selq[p][192:320].astype(F32) + rbuf[p][0:128].astype(F32)) + rbuf[p][128:256].astype(F32)
        qs[p][0, 0:64] = (mine[0:64] + rbuf[p][320:384].astype(F32)).astype(BF)
        qs[p][0, 64:128] = (mine[64:128] + rbuf[p][256:320].astype(F32)).astype(BF)
        gather_send(0, 1, p)
        gather_send(1, 1, p)

    for t in range(2):
        for copy in a_copies[t]:
            copy.wait_recv()
    loads[5].wait()
    loads[6].wait()
    kfull[0] = jnp.where(hit, mm(hits, got[0]), kc[...].astype(F32)).astype(BF)
    k_copy = send(kfull.at[0], kfull.at[1], ksend.at[0], krecv.at[0], sibling)
    vt[0] = jnp.where(hit, mm(hits, got[1]), vc[...].astype(F32)).T.astype(BF)
    v_copy = send(vt.at[0], vt.at[1], ksend.at[1], krecv.at[1], sibling)

    def attend(slots, heads):
        for i in heads:
            p, k = piece_of(i)
            cols = slice(i * HEAD_DIM, (i + 1) * HEAD_DIM)
            query = [qs[p][s, :, k * HEAD_DIM:(k + 1) * HEAD_DIM] for s in slots]
            query = query[0] if len(slots) == 1 else jnp.concatenate(query, axis=0)
            s0 = nt(kfull[0, :, cols], query)
            s1 = nt(kfull[1, :, cols], query)
            top = jnp.maximum(jnp.max(s0, axis=0, keepdims=True), jnp.max(s1, axis=0, keepdims=True))
            p0 = jnp.exp2(s0 - top)
            p1 = jnp.exp2(s1 - top)
            total = jnp.sum(p0, axis=0, keepdims=True) + jnp.sum(p1, axis=0, keepdims=True)
            o = mm(vt[0, cols, :], p0.astype(BF)) + mm(vt[1, cols, :], p1.astype(BF))
            for n, s in enumerate(slots):
                lanes = slice(n * CH, (n + 1) * CH)
                of[s, cols, :] = o[:, lanes]
                st[s, i, 0:1, :] = top[:, lanes]
                st[s, i, 1:2, :] = total[:, lanes]

    gather_step(2)
    k_copy.wait_recv()
    v_copy.wait_recv()
    attend((0,), range(NH))
    attend((7, 1), range(2))
    gather_step(3)
    attend((7, 1), range(2, NH))
    attend((6, 2), range(2))
    gather_step(4)

    def joined(slot, i, arrivals):
        rows = slice(i * HEAD_DIM, (i + 1) * HEAD_DIM)
        tops = [st[slot, i, 0:1]] + [rs[way, step, i, 0:1] for way, step in arrivals]
        sums = [st[slot, i, 1:2]] + [rs[way, step, i, 1:2] for way, step in arrivals]
        top = functools.reduce(jnp.maximum, tops)
        factors = [jnp.exp2(t - top) for t in tops]
        total = sum(a * f for a, f in zip(sums, factors))
        value = of[slot, rows, :] * factors[0]
        for n, (way, step) in enumerate(arrivals):
            value = value + ro[way, step, rows, :].astype(F32) * factors[n + 1]
        return value, top, total

    d_copies = {}

    def give(way, step, p):
        ahead = 5 - step
        slot = ahead if way == 0 else 8 - ahead
        first, last = PIECES[p]
        chained = step > (1 if p in LONG[way] else 2)
        if chained:
            for copy in d_copies[way, step - 1, p]:
                copy.wait_recv()
        for i in range(first, last):
            rows = slice(i * HEAD_DIM, (i + 1) * HEAD_DIM)
            if chained:
                value, top, total = joined(slot, i, [(way, step - 2)])
            else:
                value, top, total = of[slot, rows, :], st[slot, i, 0:1], st[slot, i, 1:2]
            so[way, step - 1, rows, :] = value.astype(BF)
            ss[way, step - 1, i, 0:1] = top
            ss[way, step - 1, i, 1:2] = total
        rows = pl.ds(first * HEAD_DIM, WIDTH[p])
        heads = pl.ds(first, last - first)
        dev = blk_at(2 if way == 0 else -2)
        d_copies[way, step, p] = [
            send(ss.at[way, step - 1, heads], rs.at[way, step - 1, heads],
                 tsend.at[way, step - 1, p], trecv.at[way, step - 1, p], dev),
            send(so.at[way, step - 1, rows], ro.at[way, step - 1, rows],
                 dsend.at[way, step - 1, p], drecv.at[way, step - 1, p], dev),
        ]

    for way in range(2):
        for p in LONG[1 - way]:
            attend((5, 3), range(*PIECES[p]))
            give(way, 2, p)
    for p in range(NP):
        way = 0 if p in LONG[0] else 1
        g_copies[way, 4, p].wait_recv()
        attend((4,), range(*PIECES[p]))
        give(way, 1, p)
    attend((6, 2), range(2, NH))
    for way in range(2):
        for p in LONG[way]:
            give(way, 2, p)
    order = (LONG[1] + LONG[0], LONG[0] + LONG[1])
    for step in (3, 4):
        for both in zip(*order):
            for way in range(2):
                give(way, step, both[way])
    last_in = sorted(range(NP), key=lambda p: max(order[0].index(p), order[1].index(p)))

    u_copies = {}
    for p in last_in:
        for way in range(2):
            for copy in d_copies[way, 4, p]:
                copy.wait_recv()
        for i in range(*PIECES[p]):
            value, _, total = joined(0, i, [(0, 3), (1, 3)])
            n = i - PIECES[p][0]
            abuf[p][:, n * HEAD_DIM:(n + 1) * HEAD_DIM] = (value / total).T.astype(BF)
        u_copies[p] = [
            send(abuf[p].at[pl.ds(first, size)], cat[p].at[pl.ds(to, size)],
                 usend.at[p, n], urecv.at[p, n], blk_at(offset))
            for n, (first, size, to, offset) in enumerate(
                ((0, 128, 320, -1), (0, 128, 64, 1), (0, 64, 448, -2), (64, 64, 0, 2))
            )
        ]
        cat[p][192:320] = abuf[p][...]
    for p in last_in:
        for copy in u_copies[p]:
            copy.wait_recv()
        first = PIECES[p][0] * HEAD_DIM
        att[:, first:first + WIDTH[p]] = mm(back[...], cat[p][...]).astype(BF)

    loads[7].wait()

    def project(first, last):
        @pl.loop(first // 512, last // 512)
        def _(i):
            cols = pl.ds(pl.multiple_of(i * 512, 512), 512)
            tile = mm(att[...], wv[:, cols]).astype(BF)
            for g in range(NG):
                pb[g // 2, g % 2, :, cols] = tile[g * ROWS:(g + 1) * ROWS]

    up, down, far = lax.rem(x + 1, 4), lax.rem(x + 3, 4), lax.rem(x + 2, 4)
    to_up, to_down = {"head": up * 2 + y}, {"head": down * 2 + y}
    to_pair = {"head": x * 2 + 1 - y}
    e = {}
    stores = []

    def give_sum(kind, g, n, src, dst, dev):
        e[kind, g, n] = send(src, dst, esend.at[kind, g, n], erecv.at[kind, g, n], dev)

    def arrived(kind, g, *names):
        for n in names:
            e[kind, g, n].wait_recv()

    def ring_start(kind, g, part, dst, first, half):
        a, b = pl.ds(first, half), pl.ds(first + half, half)
        give_sum(kind, g, 0, part(far, a), dst.at[0], to_up)
        give_sum(kind, g, 2, part(far, b), dst.at[2], to_down)
        give_sum(kind, g, 1, part(down, a), dst.at[1], to_down)
        give_sum(kind, g, 3, part(up, b), dst.at[3], to_up)

    def ring_pass(kind, g, load, dst, total, first, half):
        for n, other, cols, dev in ((0, up, first, to_up), (2, down, first + half, to_down)):
            arrived(kind, g, n)
            total[n // 2] = (dst[n].astype(F32) + load(other, slice(cols, cols + half)).astype(F32)).astype(BF)
            give_sum(kind, g, 4 + n // 2, total.at[n // 2], dst.at[4 + n // 2], dev)

    def add(*terms):
        return functools.reduce(jnp.add, [t.astype(F32) for t in terms])

    def store(cols):
        copy = pltpu.make_async_copy(outv.at[:, cols], out.at[:, cols], osem.at[len(stores)])
        copy.start()
        stores.append(copy)

    def x_start(g):
        first, width = XG[g]
        project(first, first + width)
        ring_start(0, g, lambda to, cols: pb.at[to, :, :, cols], rx1[g], first, width // 2)

    def x_pass(g):
        first, width = XG[g]
        ring_pass(0, g, lambda to, cols: pb[to, :, :, cols], rx1[g], ac1[g], first, width // 2)

    def x_sums(g, row):
        first, width = XG[g]
        half = width // 2
        return (
            add(pb[x, row, :, first:first + half], rx1[g][4, row], rx1[g][1, row]),
            add(pb[x, row, :, first + half:first + width], rx1[g][5, row], rx1[g][3, row]),
        )

    def x_turn(g):
        half = XG[g][1] // 2
        arrived(0, g, 1, 3, 4, 5)
        one, two = x_sums(g, 1 - y)
        sy1[g][:, 0:half] = one.astype(BF)
        sy1[g][:, half:2 * half] = two.astype(BF)
        give_sum(0, g, 6, sy1[g], ry1[g], to_pair)

    def x_end(g):
        first, width = XG[g]
        half = width // 2
        arrived(0, g, 6)
        one, two = x_sums(g, y)
        outv[:, first:first + half] = add(one, ry1[g][:, 0:half]).astype(BF)
        outv[:, first + half:first + width] = add(two, ry1[g][:, half:width]).astype(BF)
        store(pl.ds(first, width))

    def y_start(g):
        first, width = YG[g]
        project(first, first + width)
        give_sum(1, g, 6, pb.at[:, 1 - y, :, pl.ds(first, width)], ry2[g], to_pair)

    def y_turn(g):
        first, width = YG[g]
        arrived(1, g, 6)
        for i in range(4):
            sx2[g][i] = add(ry2[g][i], pb[i, y, :, first:first + width]).astype(BF)
        ring_start(1, g, lambda to, cols: sx2[g].at[to, :, cols], rx2[g], 0, width // 2)

    def y_pass(g):
        ring_pass(1, g, lambda to, cols: sx2[g][to, :, cols], rx2[g], ac2[g], 0, YG[g][1] // 2)

    def y_end(g):
        first, width = YG[g]
        half = width // 2
        arrived(1, g, 1, 3, 4, 5)
        outv[:, first:first + half] = add(sx2[g][x, :, 0:half], rx2[g][4], rx2[g][1]).astype(BF)
        outv[:, first + half:first + width] = add(sx2[g][x, :, half:width], rx2[g][5], rx2[g][3]).astype(BF)
        store(pl.ds(first, width))

    y_start(0)
    x_start(0)
    x_start(1)
    y_start(1)
    x_start(2)
    y_start(2)
    x_pass(0)
    y_turn(0)
    x_pass(1)
    x_turn(0)
    x_pass(2)
    y_turn(1)
    y_pass(0)
    x_turn(1)
    y_turn(2)
    x_turn(2)
    y_pass(1)
    y_pass(2)
    x_end(0)
    y_end(0)
    x_end(1)
    y_end(1)
    x_end(2)
    y_end(2)

    for copy in stores:
        copy.wait()
    for copy in pending:
        copy.wait_send()


def local(fresh, rows_index, counts, key_cache, value_cache, q_gain, k_gain, out_weight):
    any_spec = pl.BlockSpec(memory_space=pl.ANY)
    vmem = pl.BlockSpec(memory_space=pltpu.VMEM)
    dma = pltpu.SemaphoreType.DMA
    V = pltpu.VMEM

    def by_piece(*dims):
        return [V(dims + (width,), BF) for width in WIDTH]

    return pl.pallas_call(
        kernel,
        out_shape=jax.ShapeDtypeStruct((ROWS, D), BF),
        in_specs=[any_spec, vmem, pl.BlockSpec(memory_space=pltpu.SMEM)] + [any_spec] * 5,
        out_specs=any_spec,
        scratch_shapes=[
            V((3, ROWS, D), BF), V((D // 128, 128), BF), V((D // 128, 128), BF),
            V((L_BLK, GROUP), BF), V((L_BLK, GROUP), BF), V((GROUP, D), BF),
            V((2, NG, ROWS, GROUP), BF), V((2, CAP, GROUP), BF),
            by_piece(NG, ROWS), by_piece(CAP), by_piece(SPAN), by_piece(384),
            V((2, L_BLK, GROUP), BF), V((2, GROUP, L_BLK), BF), by_piece(8, CH),
            V((8, GROUP, CH), F32), V((8, NH, 2, CH), F32),
            V((2, 4, GROUP, CH), BF), V((2, 4, NH, 2, CH), F32),
            V((2, 4, GROUP, CH), BF), V((2, 4, NH, 2, CH), F32),
            by_piece(CH), by_piece(SPAN), V((CAP, SPAN), BF), V((CAP, GROUP), BF),
            V((4, 2, ROWS, D), BF),
            [V((6, 2, ROWS, w // 2), BF) for _, w in XG], [V((2, 2, ROWS, w // 2), BF) for _, w in XG],
            [V((ROWS, w), BF) for _, w in XG], [V((ROWS, w), BF) for _, w in XG],
            [V((4, ROWS, w), BF) for _, w in YG], [V((4, ROWS, w), BF) for _, w in YG],
            [V((6, ROWS, w // 2), BF) for _, w in YG], [V((2, ROWS, w // 2), BF) for _, w in YG],
            V((ROWS, D), BF),
            dma((8,)), dma((NP, 7)), dma((NP, 7)), dma((2, 7)), dma((2, 7)),
            dma((NP, 4)), dma((NP, 4)), dma((2,)), dma((2,)),
            dma((2, 4, NP)), dma((2, 4, NP)),
            dma((2, 4, NP)), dma((2, 4, NP)), dma((2, 4, NP)), dma((2, 4, NP)),
            dma((NP, 4)), dma((NP, 4)), dma((2, 3, 7)), dma((2, 3, 7)), dma((6,)),
        ],
        compiler_params=pltpu.CompilerParams(
            collective_id=0, has_side_effects=True, vmem_limit_bytes=56 * 1024 * 1024
        ),
    )(
        jnp.transpose(fresh, (1, 0, 2)), rows_index.reshape(1, CAP), counts, key_cache, value_cache,
        q_gain.reshape(D // 128, 128), k_gain.reshape(D // 128, 128), out_weight,
    )


def solution(mesh):
    placed = (
        P(("cfg", "blk", "head"), None, None),
        P("blk"),
        P(),
        P(("cfg", "blk"), "head"),
        P(("cfg", "blk"), "head"),
        P(),
        P(),
        P("head", None),
    )
    return jax.shard_map(
        local,
        mesh=mesh,
        in_specs=placed,
        out_specs=P(("cfg", "blk", "head"), None),
        check_vma=False,
    )
```

```python
import functools
import math

import jax
import jax.numpy as jnp
from jax import lax
from jax.experimental import pallas as pl
from jax.experimental.pallas import tpu as pltpu
from jax.sharding import PartitionSpec as P

HEAD_DIM = 128
EPS = 1e-06
MESH = pl.DeviceIdType.MESH
BF = jnp.bfloat16
F32 = jnp.float32

D = 5120
GROUP = 640
NH = GROUP // HEAD_DIM
NG = 8
NB = 16
CAP = 256
L_BLK = 512
ROWS = 32
CH = 128
SPAN = 512
BASE = 192
NP = NH
LONG = ((0, 1), (2, 3, 4))
XG = ((0, 1024), (1024, 1536), (2560, 512))
YG = ((3072, 1536), (4608, 512))
SCALE2 = math.log2(math.e) / math.sqrt(HEAD_DIM)


def nt(a, b):
    return lax.dot_general(a, b, (((1,), (1,)), ((), ())), preferred_element_type=F32)


def mm(a, b):
    return jnp.dot(a, b, preferred_element_type=F32)


def kernel(
    fresh, ridx, counts, kcache, vcache, qgain, kgain, weight, out,
    fv, gq, gk, kc, vc, wv, sent, got, sentq, gotq, selq, rbuf, kfull, vt, qs,
    of, st, so, ss, ro, rs, abuf, cat, back, att, pb,
    rx1, ac1, ry1, sy1, ry2, sx2, rx2, ac2, outv,
    unit, lsem, ssem, qrecv, arecv, rrecv, krecv, grecv, drecv, urecv, erecv, osem,
):
    j = lax.axis_index("blk")
    h = lax.axis_index("head")
    core = lax.rem(j, 2)
    x, y = lax.div(h, 2), lax.rem(h, 2)

    def blk_at(offset):
        return {"blk": lax.rem(j + offset + NB, NB)}

    sibling = {"blk": j + 1 - 2 * core}

    def head_at(dx, dy):
        other_y = 1 - y if dy else y
        return lax.rem(x + dx, 4) * 2 + other_y

    def send(src, dst, phase, r, dev):
        pltpu.make_async_remote_copy(
            src_ref=src, dst_ref=dst, send_sem=ssem.at[phase], recv_sem=r, device_id=dev, device_id_type=MESH
        ).start()

    def landed(like, sem):
        pltpu.make_async_copy(like, like, sem).wait()

    loads = [
        pltpu.make_async_copy(src, dst, lsem.at[i])
        for i, (src, dst) in enumerate((
            (fresh.at[0], fv.at[0]), (qgain, gq), (fresh.at[1], fv.at[1]), (kgain, gk),
            (fresh.at[2], fv.at[2]), (kcache, kc), (vcache, vc), (weight, wv),
        ))
    ]
    for load in loads[:6]:
        load.start()

    barrier = pltpu.get_barrier_semaphore()
    pairs = [(2, 1), (1, 1), (3, 1), (2, 0), (0, 1), (1, 0), (3, 0)]
    for dx, dy in pairs:
        pl.semaphore_signal(barrier, inc=1, device_id={"head": head_at(dx, dy)}, device_id_type=MESH)
    for offset in (-2, -1, 1, 2):
        pl.semaphore_signal(barrier, inc=1, device_id=blk_at(offset), device_id_type=MESH)

    live = counts[j]
    before = jnp.int32(0)
    for i in range(NB):
        before = before + jnp.where(i < j, counts[i], 0)
    shift = before - CH * j + BASE

    my_rows = pl.ds(pl.multiple_of(h * ROWS, ROWS), ROWS)

    def prepare(t):
        loads[2 * t].wait()
        if t == 2:
            for g in range(NG):
                sent[1, g] = fv[t, :, g * GROUP:(g + 1) * GROUP]
            got[1, my_rows] = sent[1, h]
            return
        loads[2 * t + 1].wait()
        rows = fv[t].astype(F32)
        factor = lax.rsqrt(jnp.mean(rows * rows, axis=-1, keepdims=True) + EPS)
        gains = (gq if t == 0 else gk)[...].astype(F32)
        for c in range(D // HEAD_DIM):
            cols = slice(c * HEAD_DIM, (c + 1) * HEAD_DIM)
            g, i = c // NH, c % NH
            value = (rows[:, cols] * factor * gains[c:c + 1] * (SCALE2 if t == 0 else 1.0)).astype(BF)
            if t == 0:
                sentq[i][g] = value
            else:
                sent[0, g, :, i * HEAD_DIM:(i + 1) * HEAD_DIM] = value
        if t == 0:
            for p in range(NP):
                gotq[p][my_rows] = sentq[p][h]
        else:
            got[0, my_rows] = sent[0, h]

    def spread(t):
        for dx, dy in pairs:
            peer = head_at(dx, dy)
            send(sent.at[t, peer], got.at[t, my_rows], 1, arecv.at[t], {"head": peer})

    prepare(0)
    pl.semaphore_wait(barrier, len(pairs) + 4)
    for p in range(NP):
        for dx, dy in pairs:
            peer = head_at(dx, dy)
            send(sentq[p].at[peer], gotq[p].at[my_rows], 0, qrecv.at[p], {"head": peer})
    for load in loads[6:]:
        load.start()
    prepare(1)
    spread(0)
    prepare(2)
    spread(1)

    r_id = lax.broadcasted_iota(jnp.int32, (SPAN, CAP), 0)
    s_id = lax.broadcasted_iota(jnp.int32, (1, CAP), 1)
    place = jnp.where(r_id == jnp.where(s_id < live, s_id + shift, -1), 1.0, 0.0).astype(BF)
    for p in range(NP):
        landed(gotq[p].at[0:CAP - ROWS], qrecv.at[p])
        selq[p][...] = mm(place, gotq[p][...]).astype(BF)
        for first, size, to, offset in ((64, 128, 0, -1), (320, 128, 128, 1), (0, 64, 256, -2), (448, 64, 320, 2)):
            send(selq[p].at[pl.ds(first, size)], rbuf[p].at[pl.ds(to, size)], 2, rrecv.at[p], blk_at(offset))
    back[...] = place.T
    pos = lax.broadcasted_iota(jnp.int32, (L_BLK, CAP), 0)
    hits = jnp.where(pos == jnp.where(s_id < live, ridx[...], -1), 1.0, 0.0)
    hit = jnp.sum(hits, axis=1, keepdims=True) > 0.5
    hits = hits.astype(BF)

    def gather_send(way, step, p):
        src = (8 - (step - 1)) % 8 if way == 0 else step - 1
        dst = 8 - step if way == 0 else step
        send(qs[p].at[src], qs[p].at[dst], 4, grecv.at[way, step - 1, p], blk_at(2 if way == 0 else -2))

    def gathered(way, step, p):
        landed(qs[p].at[0], grecv.at[way, step - 1, p])

    def gather_step(step, p):
        for way in range(2):
            gathered(way, step - 1, p)
            if step < 4 or p in LONG[way]:
                gather_send(way, step, p)

    for p in range(NP):
        landed(rbuf[p], rrecv.at[p])
        mine = (selq[p][192:320].astype(F32) + rbuf[p][0:128].astype(F32)) + rbuf[p][128:256].astype(F32)
        qs[p][0, 0:64] = (mine[0:64] + rbuf[p][320:384].astype(F32)).astype(BF)
        qs[p][0, 64:128] = (mine[64:128] + rbuf[p][256:320].astype(F32)).astype(BF)
        gather_send(0, 1, p)
        gather_send(1, 1, p)

    for t in range(2):
        landed(got.at[t, 0:CAP - ROWS], arecv.at[t])
    loads[5].wait()
    loads[6].wait()
    kfull[0] = jnp.where(hit, mm(hits, got[0]), kc[...].astype(F32)).astype(BF)
    send(kfull.at[0], kfull.at[1], 3, krecv.at[0], sibling)
    vt[0] = jnp.where(hit, mm(hits, got[1]), vc[...].astype(F32)).T.astype(BF)
    send(vt.at[0], vt.at[1], 3, krecv.at[1], sibling)

    def attend(slots, need=None, done=None):
        def scores(i, b):
            query = [qs[i][s] for s in slots]
            query = query[0] if len(slots) == 1 else jnp.concatenate(query, axis=0)
            cols = slice(i * HEAD_DIM, (i + 1) * HEAD_DIM)
            return nt(kfull[b // 2, b % 2 * 256:b % 2 * 256 + 256, cols], query)

        def weighted(i, b, weights):
            return mm(vt[b // 2, i * HEAD_DIM:(i + 1) * HEAD_DIM, b % 2 * 256:b % 2 * 256 + 256], weights)

        def keep(i, value):
            for n, s in enumerate(slots):
                of[s, i * HEAD_DIM:(i + 1) * HEAD_DIM, :] = value[:, n * CH:(n + 1) * CH]
            if done is not None:
                done(i)

        if need is not None:
            need(0)
        now = [scores(0, b) for b in range(4)]
        last = []
        for i in range(NH):
            top = functools.reduce(jnp.maximum, [jnp.max(block, axis=0, keepdims=True) for block in now])
            if i + 1 < NH and need is not None:
                need(i + 1)
            ahead, weights, total, value = [], [], 0.0, 0.0
            for b in range(4):
                if i + 1 < NH:
                    ahead.append(scores(i + 1, b))
                one = jnp.exp2(now[b] - top)
                total = total + jnp.sum(one, axis=0, keepdims=True)
                weights.append(one.astype(BF))
                if i:
                    value = value + weighted(i - 1, b, last[b])
            for n, s in enumerate(slots):
                st[s, i, 0:1, :] = top[:, n * CH:(n + 1) * CH]
                st[s, i, 1:2, :] = total[:, n * CH:(n + 1) * CH]
            if i:
                keep(i - 1, value)
            now, last = ahead, weights
        value = functools.reduce(jnp.add, [weighted(NH - 1, b, last[b]) for b in range(4)])
        keep(NH - 1, value)

    for p in range(NP):
        gather_step(2, p)
    landed(kfull.at[1], krecv.at[0])
    landed(vt.at[1], krecv.at[1])
    attend((0, 7, 1), need=functools.partial(gather_step, 3))
    attend((6, 2), need=functools.partial(gather_step, 4))

    def joined(slot, i, arrivals):
        rows = slice(i * HEAD_DIM, (i + 1) * HEAD_DIM)
        tops = [st[slot, i, 0:1]] + [rs[way, step, i, 0:1] for way, step in arrivals]
        sums = [st[slot, i, 1:2]] + [rs[way, step, i, 1:2] for way, step in arrivals]
        top = functools.reduce(jnp.maximum, tops)
        factors = [jnp.exp2(t - top) for t in tops]
        total = sum(a * f for a, f in zip(sums, factors))
        value = of[slot, rows, :] * factors[0]
        for n, (way, step) in enumerate(arrivals):
            value = value + ro[way, step, rows, :].astype(F32) * factors[n + 1]
        return value, top, total

    def give(way, step, p):
        ahead = 5 - step
        slot = ahead if way == 0 else 8 - ahead
        rows = slice(p * HEAD_DIM, (p + 1) * HEAD_DIM)
        if step > (1 if p in LONG[way] else 2):
            landed(unit.at[0:33], drecv.at[way, step - 2, p])
            value, top, total = joined(slot, p, [(way, step - 2)])
        else:
            value, top, total = of[slot, rows, :], st[slot, p, 0:1], st[slot, p, 1:2]
        so[way, step - 1, rows, :] = value.astype(BF)
        ss[way, step - 1, p, 0:1] = top
        ss[way, step - 1, p, 1:2] = total
        rows = pl.ds(p * HEAD_DIM, HEAD_DIM)
        dev = blk_at(2 if way == 0 else -2)
        send(ss.at[way, step - 1, p], rs.at[way, step - 1, p], 6, drecv.at[way, step - 1, p], dev)
        send(so.at[way, step - 1, rows], ro.at[way, step - 1, rows], 5, drecv.at[way, step - 1, p], dev)

    def long_way(p):
        return 0 if p in LONG[0] else 1

    attend((5, 3), done=lambda p: give(1 - long_way(p), 2, p))
    attend((4,), need=lambda p: gathered(long_way(p), 4, p), done=lambda p: give(long_way(p), 1, p))
    for p in range(NP):
        give(long_way(p), 2, p)
    order = (LONG[1] + LONG[0], LONG[0] + LONG[1])
    for step in (3, 4):
        for both in zip(*order):
            for way in range(2):
                give(way, step, both[way])
    last_in = sorted(range(NP), key=lambda p: max(order[0].index(p), order[1].index(p)))

    for p in last_in:
        for way in range(2):
            landed(unit.at[0:33], drecv.at[way, 3, p])
        value, _, total = joined(0, p, [(0, 3), (1, 3)])
        abuf[p][...] = (value / total).T.astype(BF)
        for first, size, to, offset in ((0, 128, 320, -1), (0, 128, 64, 1), (0, 64, 448, -2), (64, 64, 0, 2)):
            send(abuf[p].at[pl.ds(first, size)], cat[p].at[pl.ds(to, size)], 7, urecv.at[p], blk_at(offset))
        cat[p][192:320] = abuf[p][...]
    for p in last_in:
        landed(rbuf[p], urecv.at[p])
        att[:, p * HEAD_DIM:(p + 1) * HEAD_DIM] = mm(back[...], cat[p][...]).astype(BF)

    loads[7].wait()

    def project(first, last):
        for at in range(first, last, 512):
            cols = slice(at, at + 512)
            tile = mm(att[...], wv[:, cols]).astype(BF)
            for g in range(NG):
                pb[g // 2, g % 2, :, cols] = tile[g * ROWS:(g + 1) * ROWS]

    up, down, far = lax.rem(x + 1, 4), lax.rem(x + 3, 4), lax.rem(x + 2, 4)
    to_up, to_down = {"head": up * 2 + y}, {"head": down * 2 + y}
    to_pair = {"head": x * 2 + 1 - y}
    stores = []

    def give_sum(kind, g, n, src, dst, dev):
        send(src, dst, 8, erecv.at[kind, g, (0, 2, 1, 2, 2, 2, 3)[n]], dev)

    def ring_start(kind, g, part, dst, first, half):
        a, b = pl.ds(first, half), pl.ds(first + half, half)
        give_sum(kind, g, 0, part(far, a), dst.at[0], to_up)
        give_sum(kind, g, 2, part(far, b), dst.at[2], to_down)
        give_sum(kind, g, 1, part(down, a), dst.at[1], to_down)
        give_sum(kind, g, 3, part(up, b), dst.at[3], to_up)

    def ring_pass(kind, g, load, dst, total, first, half):
        for n, other, cols, dev in ((0, up, first, to_up), (2, down, first + half, to_down)):
            landed(dst.at[n], erecv.at[kind, g, n // 2])
            total[n // 2] = (dst[n].astype(F32) + load(other, slice(cols, cols + half)).astype(F32)).astype(BF)
            give_sum(kind, g, 4 + n // 2, total.at[n // 2], dst.at[4 + n // 2], dev)

    def add(*terms):
        return functools.reduce(jnp.add, [t.astype(F32) for t in terms])

    def store(cols):
        copy = pltpu.make_async_copy(outv.at[:, cols], out.at[:, cols], osem.at[len(stores)])
        copy.start()
        stores.append(copy)

    def x_start(g):
        first, width = XG[g]
        project(first, first + width)
        ring_start(0, g, lambda to, cols: pb.at[to, :, :, cols], rx1[g], first, width // 2)

    def x_pass(g):
        first, width = XG[g]
        ring_pass(0, g, lambda to, cols: pb[to, :, :, cols], rx1[g], ac1[g], first, width // 2)

    def x_sums(g, row):
        first, width = XG[g]
        half = width // 2
        return (
            add(pb[x, row, :, first:first + half], rx1[g][4, row], rx1[g][1, row]),
            add(pb[x, row, :, first + half:first + width], rx1[g][5, row], rx1[g][3, row]),
        )

    def x_turn(g):
        half = XG[g][1] // 2
        landed(rx1[g].at[0:4], erecv.at[0, g, 2])
        one, two = x_sums(g, 1 - y)
        sy1[g][:, 0:half] = one.astype(BF)
        sy1[g][:, half:2 * half] = two.astype(BF)
        give_sum(0, g, 6, sy1[g], ry1[g], to_pair)

    def x_end(g):
        first, width = XG[g]
        half = width // 2
        landed(ry1[g], erecv.at[0, g, 3])
        one, two = x_sums(g, y)
        outv[:, first:first + half] = add(one, ry1[g][:, 0:half]).astype(BF)
        outv[:, first + half:first + width] = add(two, ry1[g][:, half:width]).astype(BF)
        store(pl.ds(first, width))

    def y_start(g):
        first, width = YG[g]
        project(first, first + width)
        give_sum(1, g, 6, pb.at[:, 1 - y, :, pl.ds(first, width)], ry2[g], to_pair)

    def y_turn(g):
        first, width = YG[g]
        landed(ry2[g], erecv.at[1, g, 3])
        for i in range(4):
            sx2[g][i] = add(ry2[g][i], pb[i, y, :, first:first + width]).astype(BF)
        ring_start(1, g, lambda to, cols: sx2[g].at[to, :, cols], rx2[g], 0, width // 2)

    def y_pass(g):
        ring_pass(1, g, lambda to, cols: sx2[g][to, :, cols], rx2[g], ac2[g], 0, YG[g][1] // 2)

    def y_end(g):
        first, width = YG[g]
        half = width // 2
        landed(rx2[g].at[0:4], erecv.at[1, g, 2])
        outv[:, first:first + half] = add(sx2[g][x, :, 0:half], rx2[g][4], rx2[g][1]).astype(BF)
        outv[:, first + half:first + width] = add(sx2[g][x, :, half:width], rx2[g][5], rx2[g][3]).astype(BF)
        store(pl.ds(first, width))

    x_start(0)
    y_start(0)
    x_start(1)
    y_start(1)
    x_start(2)
    x_pass(0)
    x_pass(1)
    y_turn(0)
    x_turn(0)
    x_pass(2)
    y_turn(1)
    x_turn(1)
    y_pass(0)
    x_turn(2)
    y_pass(1)
    x_end(0)
    x_end(1)
    y_end(0)
    x_end(2)
    y_end(1)

    for copy in stores:
        copy.wait()
    for phase, rows, cols in (
        (0, 32, 4480), (1, 64, 4480), (2, 64, 3840), (3, 128, 5120), (4, 128, 4480), (5, 128, 4480),
        (7, 64, 3840), (8, 256, 4480),
    ):
        landed(wv.at[0:rows, 0:cols], ssem.at[phase])
    landed(unit, ssem.at[6])


def local(fresh, rows_index, counts, key_cache, value_cache, q_gain, k_gain, out_weight):
    any_spec = pl.BlockSpec(memory_space=pl.ANY)
    vmem = pl.BlockSpec(memory_space=pltpu.VMEM)
    dma = pltpu.SemaphoreType.DMA
    V = pltpu.VMEM

    def by_piece(*dims):
        return [V(dims + (HEAD_DIM,), BF)] * NP

    return pl.pallas_call(
        kernel,
        out_shape=jax.ShapeDtypeStruct((ROWS, D), BF),
        in_specs=[any_spec, vmem, pl.BlockSpec(memory_space=pltpu.SMEM)] + [any_spec] * 5,
        out_specs=any_spec,
        scratch_shapes=[
            V((3, ROWS, D), BF), V((D // 128, 128), BF), V((D // 128, 128), BF),
            V((L_BLK, GROUP), BF), V((L_BLK, GROUP), BF), V((GROUP, D), BF),
            V((2, NG, ROWS, GROUP), BF), V((2, CAP, GROUP), BF),
            by_piece(NG, ROWS), by_piece(CAP), by_piece(SPAN), by_piece(384),
            V((2, L_BLK, GROUP), BF), V((2, GROUP, L_BLK), BF), by_piece(8, CH),
            V((8, GROUP, CH), F32), V((8, NH, 2, CH), F32),
            V((2, 4, GROUP, CH), BF), V((2, 4, NH, 2, CH), F32),
            V((2, 4, GROUP, CH), BF), V((2, 4, NH, 2, CH), F32),
            by_piece(CH), by_piece(SPAN), V((CAP, SPAN), BF), V((CAP, GROUP), BF),
            V((4, 2, ROWS, D), BF),
            [V((6, 2, ROWS, w // 2), BF) for _, w in XG], [V((2, 2, ROWS, w // 2), BF) for _, w in XG],
            [V((ROWS, w), BF) for _, w in XG], [V((ROWS, w), BF) for _, w in XG],
            [V((4, ROWS, w), BF) for _, w in YG], [V((4, ROWS, w), BF) for _, w in YG],
            [V((6, ROWS, w // 2), BF) for _, w in YG], [V((2, ROWS, w // 2), BF) for _, w in YG],
            V((ROWS, D), BF),
            V((35, 2, CH), F32), dma((8,)), dma((9,)), dma((NP,)), dma((2,)), dma((NP,)), dma((2,)),
            dma((2, 4, NP)), dma((2, 4, NP)), dma((NP,)), dma((2, 3, 4)), dma((5,)),
        ],
        compiler_params=pltpu.CompilerParams(
            collective_id=0, has_side_effects=True, vmem_limit_bytes=56 * 1024 * 1024
        ),
    )(
        jnp.transpose(fresh, (1, 0, 2)), rows_index.reshape(1, CAP), counts, key_cache, value_cache,
        q_gain.reshape(D // 128, 128), k_gain.reshape(D // 128, 128), out_weight,
    )


def solution(mesh):
    placed = (
        P(("cfg", "blk", "head"), None, None),
        P("blk"),
        P(),
        P(("cfg", "blk"), "head"),
        P(("cfg", "blk"), "head"),
        P(),
        P(),
        P("head", None),
    )
    return jax.shard_map(
        local,
        mesh=mesh,
        in_specs=placed,
        out_specs=P(("cfg", "blk", "head"), None),
        check_vma=False,
    )
```

```python
import functools
import math

import jax
import jax.numpy as jnp
from jax import lax
from jax.experimental import pallas as pl
from jax.experimental.pallas import tpu as pltpu
from jax.sharding import PartitionSpec as P

HEAD_DIM = 128
EPS = 1e-06
MESH = pl.DeviceIdType.MESH
BF = jnp.bfloat16
F32 = jnp.float32

D = 5120
GROUP = 640
NH = GROUP // HEAD_DIM
NG = 8
NB = 16
CAP = 256
L_BLK = 512
ROWS = 32
CH = 128
SPAN = 512
BASE = 192
NP = NH
LONG = ((0, 1), (2, 3, 4))
XG = ((0, 1024), (1024, 1536), (2560, 512))
YG = ((3072, 1536), (4608, 512))
SCALE2 = math.log2(math.e) / math.sqrt(HEAD_DIM)


def nt(a, b):
    return lax.dot_general(a, b, (((1,), (1,)), ((), ())), preferred_element_type=F32)


def mm(a, b):
    return jnp.dot(a, b, preferred_element_type=F32)


def kernel(
    fresh, ridx, counts, kcache, vcache, qgain, kgain, weight, out,
    fv, gq, gk, kc, vc, wv, sent, got, sentq, gotq, selq, rbuf, kfull, vt, qs,
    of, st, so, ss, ro, rs, abuf, cat, back, att, pb,
    rx1, ac1, ry1, sy1, ry2, sx2, rx2, ac2, outv,
    unit, lsem, ssem, qrecv, arecv, rrecv, krecv, grecv, drecv, urecv, erecv, osem,
):
    j = lax.axis_index("blk")
    h = lax.axis_index("head")
    core = lax.rem(j, 2)
    x, y = lax.div(h, 2), lax.rem(h, 2)

    def blk_at(offset):
        return {"blk": lax.rem(j + offset + NB, NB)}

    sibling = {"blk": j + 1 - 2 * core}

    def head_at(dx, dy):
        other_y = 1 - y if dy else y
        return lax.rem(x + dx, 4) * 2 + other_y

    def send(src, dst, phase, r, dev):
        pltpu.make_async_remote_copy(
            src_ref=src, dst_ref=dst, send_sem=ssem.at[phase], recv_sem=r, device_id=dev, device_id_type=MESH
        ).start()

    def landed(like, sem):
        pltpu.make_async_copy(like, like, sem).wait()

    loads = [
        pltpu.make_async_copy(src, dst, lsem.at[i])
        for i, (src, dst) in enumerate((
            (fresh.at[0], fv.at[0]), (qgain, gq), (fresh.at[1], fv.at[1]), (kgain, gk),
            (fresh.at[2], fv.at[2]), (kcache, kc), (vcache, vc), (weight, wv),
        ))
    ]
    for load in loads[:6]:
        load.start()

    barrier = pltpu.get_barrier_semaphore()
    pairs = [(2, 1), (1, 1), (3, 1), (2, 0), (0, 1), (1, 0), (3, 0)]
    for dx, dy in pairs:
        pl.semaphore_signal(barrier, inc=1, device_id={"head": head_at(dx, dy)}, device_id_type=MESH)
    for offset in (-2, -1, 1, 2):
        pl.semaphore_signal(barrier, inc=1, device_id=blk_at(offset), device_id_type=MESH)

    live = counts[j]
    before = jnp.int32(0)
    for i in range(NB):
        before = before + jnp.where(i < j, counts[i], 0)
    shift = before - CH * j + BASE

    my_rows = pl.ds(pl.multiple_of(h * ROWS, ROWS), ROWS)

    def prepare(t):
        loads[2 * t].wait()
        if t == 2:
            for g in range(NG):
                sent[1, g] = fv[t, :, g * GROUP:(g + 1) * GROUP]
            got[1, my_rows] = sent[1, h]
            return
        loads[2 * t + 1].wait()
        rows = fv[t].astype(F32)
        factor = lax.rsqrt(jnp.mean(rows * rows, axis=-1, keepdims=True) + EPS)
        gains = (gq if t == 0 else gk)[...].astype(F32)
        for c in range(D // HEAD_DIM):
            cols = slice(c * HEAD_DIM, (c + 1) * HEAD_DIM)
            g, i = c // NH, c % NH
            value = (rows[:, cols] * factor * gains[c:c + 1] * (SCALE2 if t == 0 else 1.0)).astype(BF)
            if t == 0:
                sentq[i][g] = value
            else:
                sent[0, g, :, i * HEAD_DIM:(i + 1) * HEAD_DIM] = value
        if t == 0:
            for p in range(NP):
                gotq[p][my_rows] = sentq[p][h]
        else:
            got[0, my_rows] = sent[0, h]

    def spread(t):
        for dx, dy in pairs:
            peer = head_at(dx, dy)
            send(sent.at[t, peer], got.at[t, my_rows], 1, arecv.at[t], {"head": peer})

    prepare(0)
    pl.semaphore_wait(barrier, len(pairs) + 4)
    for p in range(NP):
        for dx, dy in pairs:
            peer = head_at(dx, dy)
            send(sentq[p].at[peer], gotq[p].at[my_rows], 0, qrecv.at[p], {"head": peer})
    for load in loads[6:]:
        load.start()
    prepare(1)
    spread(0)
    prepare(2)
    spread(1)

    r_id = lax.broadcasted_iota(jnp.int32, (SPAN, CAP), 0)
    s_id = lax.broadcasted_iota(jnp.int32, (1, CAP), 1)
    place = jnp.where(r_id == jnp.where(s_id < live, s_id + shift, -1), 1.0, 0.0).astype(BF)
    for p in range(NP):
        landed(gotq[p].at[0:CAP - ROWS], qrecv.at[p])
        selq[p][...] = mm(place, gotq[p][...]).astype(BF)
        for first, size, to, offset in ((64, 128, 0, -1), (320, 128, 128, 1), (0, 64, 256, -2), (448, 64, 320, 2)):
            send(selq[p].at[pl.ds(first, size)], rbuf[p].at[pl.ds(to, size)], 2, rrecv.at[p], blk_at(offset))
    back[...] = place.T
    pos = lax.broadcasted_iota(jnp.int32, (L_BLK, CAP), 0)
    hits = jnp.where(pos == jnp.where(s_id < live, ridx[...], -1), 1.0, 0.0)
    hit = jnp.sum(hits, axis=1, keepdims=True) > 0.5
    hits = hits.astype(BF)

    def gather_send(way, step, p):
        src = (8 - (step - 1)) % 8 if way == 0 else step - 1
        dst = 8 - step if way == 0 else step
        send(qs[p].at[src], qs[p].at[dst], 4, grecv.at[step - 1, p], blk_at(2 if way == 0 else -2))

    def gathered(step, p):
        landed(qs[p].at[0:2] if step < 4 else qs[p].at[0], grecv.at[step - 1, p])

    def gather_step(step, p):
        gathered(step - 1, p)
        for way in range(2):
            if step < 4 or p in LONG[way]:
                gather_send(way, step, p)

    for p in range(NP):
        landed(rbuf[p], rrecv.at[p])
        mine = (selq[p][192:320].astype(F32) + rbuf[p][0:128].astype(F32)) + rbuf[p][128:256].astype(F32)
        qs[p][0, 0:64] = (mine[0:64] + rbuf[p][320:384].astype(F32)).astype(BF)
        qs[p][0, 64:128] = (mine[64:128] + rbuf[p][256:320].astype(F32)).astype(BF)
        gather_send(0, 1, p)
        gather_send(1, 1, p)

    landed(got.at[0, 0:CAP - ROWS], arecv.at[0])
    loads[5].wait()
    kfull[0] = jnp.where(hit, mm(hits, got[0]), kc[...].astype(F32)).astype(BF)
    send(kfull.at[0], kfull.at[1], 3, krecv.at[0], sibling)
    for p in (0, 1):
        gather_step(2, p)
    landed(got.at[1, 0:CAP - ROWS], arecv.at[1])
    loads[6].wait()
    vt[0] = jnp.where(hit, mm(hits, got[1]), vc[...].astype(F32)).T.astype(BF)
    send(vt.at[0], vt.at[1], 3, krecv.at[1], sibling)
    for p in (2, 3, 4):
        gather_step(2, p)

    def attend(slots, need=None, done=None):
        def scores(i, b):
            query = [qs[i][s] for s in slots]
            query = query[0] if len(slots) == 1 else jnp.concatenate(query, axis=0)
            cols = slice(i * HEAD_DIM, (i + 1) * HEAD_DIM)
            return nt(kfull[b // 2, b % 2 * 256:b % 2 * 256 + 256, cols], query)

        def weighted(i, b, weights):
            return mm(vt[b // 2, i * HEAD_DIM:(i + 1) * HEAD_DIM, b % 2 * 256:b % 2 * 256 + 256], weights)

        def keep(i, value):
            for n, s in enumerate(slots):
                of[s, i * HEAD_DIM:(i + 1) * HEAD_DIM, :] = value[:, n * CH:(n + 1) * CH]
            if done is not None:
                done(i)

        if need is not None:
            need(0)
        now = [scores(0, b) for b in range(4)]
        last = []
        for i in range(NH):
            top = functools.reduce(jnp.maximum, [jnp.max(block, axis=0, keepdims=True) for block in now])
            if i + 1 < NH and need is not None:
                need(i + 1)
            ahead, weights, total, value = [], [], 0.0, 0.0
            for b in range(4):
                if i + 1 < NH:
                    ahead.append(scores(i + 1, b))
                one = jnp.exp2(now[b] - top)
                total = total + jnp.sum(one, axis=0, keepdims=True)
                weights.append(one.astype(BF))
                if i:
                    value = value + weighted(i - 1, b, last[b])
            for n, s in enumerate(slots):
                st[s, i, 0:1, :] = top[:, n * CH:(n + 1) * CH]
                st[s, i, 1:2, :] = total[:, n * CH:(n + 1) * CH]
            if i:
                keep(i - 1, value)
            now, last = ahead, weights
        value = functools.reduce(jnp.add, [weighted(NH - 1, b, last[b]) for b in range(4)])
        keep(NH - 1, value)

    def first_needs(p):
        gather_step(3, p)
        if p == 2:
            landed(vt.at[1], krecv.at[1])

    landed(kfull.at[1], krecv.at[0])
    attend((0, 7, 1), need=first_needs)
    attend((6, 2), need=functools.partial(gather_step, 4))

    def joined(slot, i, arrivals):
        rows = slice(i * HEAD_DIM, (i + 1) * HEAD_DIM)
        tops = [st[slot, i, 0:1]] + [rs[way, step, i, 0:1] for way, step in arrivals]
        sums = [st[slot, i, 1:2]] + [rs[way, step, i, 1:2] for way, step in arrivals]
        top = functools.reduce(jnp.maximum, tops)
        factors = [jnp.exp2(t - top) for t in tops]
        total = sum(a * f for a, f in zip(sums, factors))
        value = of[slot, rows, :] * factors[0]
        for n, (way, step) in enumerate(arrivals):
            value = value + ro[way, step, rows, :].astype(F32) * factors[n + 1]
        return value, top, total

    def give(way, step, p):
        ahead = 5 - step
        slot = ahead if way == 0 else 8 - ahead
        rows = slice(p * HEAD_DIM, (p + 1) * HEAD_DIM)
        if step > (1 if p in LONG[way] else 2):
            landed(unit.at[0:33], drecv.at[way, step - 2, p])
            value, top, total = joined(slot, p, [(way, step - 2)])
        else:
            value, top, total = of[slot, rows, :], st[slot, p, 0:1], st[slot, p, 1:2]
        so[way, step - 1, rows, :] = value.astype(BF)
        ss[way, step - 1, p, 0:1] = top
        ss[way, step - 1, p, 1:2] = total
        rows = pl.ds(p * HEAD_DIM, HEAD_DIM)
        dev = blk_at(2 if way == 0 else -2)
        send(ss.at[way, step - 1, p], rs.at[way, step - 1, p], 6, drecv.at[way, step - 1, p], dev)
        send(so.at[way, step - 1, rows], ro.at[way, step - 1, rows], 5, drecv.at[way, step - 1, p], dev)

    def long_way(p):
        return 0 if p in LONG[0] else 1

    attend((4,), need=lambda p: gathered(4, p), done=lambda p: give(long_way(p), 1, p))
    attend((5, 3), done=lambda p: give(1 - long_way(p), 2, p))
    for p in range(NP):
        give(long_way(p), 2, p)
    order = (LONG[1] + LONG[0], LONG[0] + LONG[1])
    for step in (3, 4):
        for both in zip(*order):
            for way in range(2):
                give(way, step, both[way])
    last_in = sorted(range(NP), key=lambda p: max(order[0].index(p), order[1].index(p)))

    for p in last_in:
        for way in range(2):
            landed(unit.at[0:33], drecv.at[way, 3, p])
        value, _, total = joined(0, p, [(0, 3), (1, 3)])
        abuf[p][...] = (value / total).T.astype(BF)
        for first, size, to, offset in ((0, 128, 320, -1), (0, 128, 64, 1), (0, 64, 448, -2), (64, 64, 0, 2)):
            send(abuf[p].at[pl.ds(first, size)], cat[p].at[pl.ds(to, size)], 7, urecv.at[p], blk_at(offset))
        cat[p][192:320] = abuf[p][...]
    for p in last_in:
        landed(rbuf[p], urecv.at[p])
        att[:, p * HEAD_DIM:(p + 1) * HEAD_DIM] = mm(back[...], cat[p][...]).astype(BF)

    loads[7].wait()

    def project(first, last):
        for at in range(first, last, 512):
            cols = slice(at, at + 512)
            tile = mm(att[...], wv[:, cols]).astype(BF)
            for g in range(NG):
                pb[g // 2, g % 2, :, cols] = tile[g * ROWS:(g + 1) * ROWS]

    up, down, far = lax.rem(x + 1, 4), lax.rem(x + 3, 4), lax.rem(x + 2, 4)
    to_up, to_down = {"head": up * 2 + y}, {"head": down * 2 + y}
    to_pair = {"head": x * 2 + 1 - y}

    def give_sum(kind, g, n, src, dst, dev):
        send(src, dst, 8, erecv.at[kind, g, (0, 2, 1, 2, 2, 2, 3)[n]], dev)

    def ring_start(kind, g, part, dst, first, half):
        a, b = pl.ds(first, half), pl.ds(first + half, half)
        give_sum(kind, g, 0, part(far, a), dst.at[0], to_up)
        give_sum(kind, g, 2, part(far, b), dst.at[2], to_down)
        give_sum(kind, g, 1, part(down, a), dst.at[1], to_down)
        give_sum(kind, g, 3, part(up, b), dst.at[3], to_up)

    def ring_pass(kind, g, load, dst, total, first, half):
        for n, other, cols, dev in ((0, up, first, to_up), (2, down, first + half, to_down)):
            landed(dst.at[n], erecv.at[kind, g, n // 2])
            total[n // 2] = (dst[n].astype(F32) + load(other, slice(cols, cols + half)).astype(F32)).astype(BF)
            give_sum(kind, g, 4 + n // 2, total.at[n // 2], dst.at[4 + n // 2], dev)

    def add(*terms):
        return functools.reduce(jnp.add, [t.astype(F32) for t in terms])

    def store(cols):
        pltpu.make_async_copy(outv.at[:, cols], out.at[:, cols], osem.at[0]).start()

    def x_start(g):
        first, width = XG[g]
        project(first, first + width)
        ring_start(0, g, lambda to, cols: pb.at[to, :, :, cols], rx1[g], first, width // 2)

    def x_pass(g):
        first, width = XG[g]
        ring_pass(0, g, lambda to, cols: pb[to, :, :, cols], rx1[g], ac1[g], first, width // 2)

    def x_sums(g, row):
        first, width = XG[g]
        half = width // 2
        return (
            add(pb[x, row, :, first:first + half], rx1[g][4, row], rx1[g][1, row]),
            add(pb[x, row, :, first + half:first + width], rx1[g][5, row], rx1[g][3, row]),
        )

    def x_turn(g):
        half = XG[g][1] // 2
        landed(rx1[g].at[0:4], erecv.at[0, g, 2])
        one, two = x_sums(g, 1 - y)
        sy1[g][:, 0:half] = one.astype(BF)
        sy1[g][:, half:2 * half] = two.astype(BF)
        give_sum(0, g, 6, sy1[g], ry1[g], to_pair)

    def x_end(g):
        first, width = XG[g]
        half = width // 2
        landed(ry1[g], erecv.at[0, g, 3])
        one, two = x_sums(g, y)
        outv[:, first:first + half] = add(one, ry1[g][:, 0:half]).astype(BF)
        outv[:, first + half:first + width] = add(two, ry1[g][:, half:width]).astype(BF)
        store(pl.ds(first, width))

    def y_start(g):
        first, width = YG[g]
        project(first, first + width)
        give_sum(1, g, 6, pb.at[:, 1 - y, :, pl.ds(first, width)], ry2[g], to_pair)

    def y_turn(g):
        first, width = YG[g]
        landed(ry2[g], erecv.at[1, g, 3])
        for i in range(4):
            sx2[g][i] = add(ry2[g][i], pb[i, y, :, first:first + width]).astype(BF)
        ring_start(1, g, lambda to, cols: sx2[g].at[to, :, cols], rx2[g], 0, width // 2)

    def y_pass(g):
        ring_pass(1, g, lambda to, cols: sx2[g][to, :, cols], rx2[g], ac2[g], 0, YG[g][1] // 2)

    def y_end(g):
        first, width = YG[g]
        half = width // 2
        landed(rx2[g].at[0:4], erecv.at[1, g, 2])
        outv[:, first:first + half] = add(sx2[g][x, :, 0:half], rx2[g][4], rx2[g][1]).astype(BF)
        outv[:, first + half:first + width] = add(sx2[g][x, :, half:width], rx2[g][5], rx2[g][3]).astype(BF)
        store(pl.ds(first, width))

    x_start(0)
    y_start(0)
    x_start(1)
    y_start(1)
    x_start(2)
    x_pass(0)
    x_pass(1)
    y_turn(0)
    x_turn(0)
    x_pass(2)
    y_turn(1)
    x_turn(1)
    y_pass(0)
    x_turn(2)
    y_pass(1)
    x_end(0)
    x_end(1)
    y_end(0)
    x_end(2)
    y_end(1)

    landed(outv, osem.at[0])
    for phase, rows, cols in (
        (0, 32, 4480), (1, 64, 4480), (2, 64, 3840), (3, 128, 5120), (4, 128, 4480), (5, 128, 4480),
        (7, 64, 3840), (8, 256, 4480),
    ):
        landed(wv.at[0:rows, 0:cols], ssem.at[phase])
    landed(unit, ssem.at[6])


def local(fresh, rows_index, counts, key_cache, value_cache, q_gain, k_gain, out_weight):
    any_spec = pl.BlockSpec(memory_space=pl.ANY)
    vmem = pl.BlockSpec(memory_space=pltpu.VMEM)
    dma = pltpu.SemaphoreType.DMA
    V = pltpu.VMEM

    def by_piece(*dims):
        return [V(dims + (HEAD_DIM,), BF)] * NP

    return pl.pallas_call(
        kernel,
        out_shape=jax.ShapeDtypeStruct((ROWS, D), BF),
        in_specs=[any_spec, vmem, pl.BlockSpec(memory_space=pltpu.SMEM)] + [any_spec] * 5,
        out_specs=any_spec,
        scratch_shapes=[
            V((3, ROWS, D), BF), V((D // 128, 128), BF), V((D // 128, 128), BF),
            V((L_BLK, GROUP), BF), V((L_BLK, GROUP), BF), V((GROUP, D), BF),
            V((2, NG, ROWS, GROUP), BF), V((2, CAP, GROUP), BF),
            by_piece(NG, ROWS), by_piece(CAP), by_piece(SPAN), by_piece(384),
            V((2, L_BLK, GROUP), BF), V((2, GROUP, L_BLK), BF), by_piece(8, CH),
            V((8, GROUP, CH), F32), V((8, NH, 2, CH), F32),
            V((2, 4, GROUP, CH), BF), V((2, 4, NH, 2, CH), F32),
            V((2, 4, GROUP, CH), BF), V((2, 4, NH, 2, CH), F32),
            by_piece(CH), by_piece(SPAN), V((CAP, SPAN), BF), V((CAP, GROUP), BF),
            V((4, 2, ROWS, D), BF),
            [V((6, 2, ROWS, w // 2), BF) for _, w in XG], [V((2, 2, ROWS, w // 2), BF) for _, w in XG],
            [V((ROWS, w), BF) for _, w in XG], [V((ROWS, w), BF) for _, w in XG],
            [V((4, ROWS, w), BF) for _, w in YG], [V((4, ROWS, w), BF) for _, w in YG],
            [V((6, ROWS, w // 2), BF) for _, w in YG], [V((2, ROWS, w // 2), BF) for _, w in YG],
            V((ROWS, D), BF),
            V((35, 2, CH), F32), dma((8,)), dma((9,)), dma((NP,)), dma((2,)), dma((NP,)), dma((2,)),
            dma((4, NP)), dma((2, 4, NP)), dma((NP,)), dma((2, 3, 4)), dma((1,)),
        ],
        compiler_params=pltpu.CompilerParams(
            collective_id=0, has_side_effects=True, vmem_limit_bytes=56 * 1024 * 1024
        ),
    )(
        jnp.transpose(fresh, (1, 0, 2)), rows_index.reshape(1, CAP), counts, key_cache, value_cache,
        q_gain.reshape(D // 128, 128), k_gain.reshape(D // 128, 128), out_weight,
    )


def solution(mesh):
    placed = (
        P(("cfg", "blk", "head"), None, None),
        P("blk"),
        P(),
        P(("cfg", "blk"), "head"),
        P(("cfg", "blk"), "head"),
        P(),
        P(),
        P("head", None),
    )
    return jax.shard_map(
        local,
        mesh=mesh,
        in_specs=placed,
        out_specs=P(("cfg", "blk", "head"), None),
        check_vma=False,
    )
```

```python
import functools
import math

import jax
import jax.numpy as jnp
from jax import lax
from jax.experimental import pallas as pl
from jax.experimental.pallas import tpu as pltpu
from jax.sharding import PartitionSpec as P

HEAD_DIM = 128
EPS = 1e-06
MESH = pl.DeviceIdType.MESH
BF = jnp.bfloat16
F32 = jnp.float32

D = 5120
GROUP = 640
NH = GROUP // HEAD_DIM
NG = 8
NB = 16
CAP = 256
L_BLK = 512
ROWS = 32
CH = 128
SPAN = 512
BASE = 192
NP = NH
LONG = ((0, 1), (2, 3, 4))
XG = ((0, 1024), (1024, 1536), (2560, 512))
YG = ((3072, 1536), (4608, 512))
SCALE2 = math.log2(math.e) / math.sqrt(HEAD_DIM)


def nt(a, b):
    return lax.dot_general(a, b, (((1,), (1,)), ((), ())), preferred_element_type=F32)


def mm(a, b):
    return jnp.dot(a, b, preferred_element_type=F32)


def kernel(
    fresh, ridx, counts, kcache, vcache, qgain, kgain, weight, out,
    fv, gq, gk, kc, vc, wv, sent, got, sentq, gotq, selq, rbuf, kfull, vt, qs,
    of, st, so, ss, ro, rs, abuf, cat, back, att, pb,
    rx1, ac1, ry1, sy1, ry2, sx2, rx2, ac2, rx3,
    unit, lsem, ssem, qrecv, arecv, rrecv, krecv, grecv, drecv, urecv, erecv,
):
    j = lax.axis_index("blk")
    h = lax.axis_index("head")
    core = lax.rem(j, 2)
    x, y = lax.div(h, 2), lax.rem(h, 2)

    def blk_at(offset):
        return {"blk": lax.rem(j + offset + NB, NB)}

    sibling = {"blk": j + 1 - 2 * core}

    def head_at(dx, dy):
        other_y = 1 - y if dy else y
        return lax.rem(x + dx, 4) * 2 + other_y

    def send(src, dst, phase, r, dev):
        pltpu.make_async_remote_copy(
            src_ref=src, dst_ref=dst, send_sem=ssem.at[phase], recv_sem=r, device_id=dev, device_id_type=MESH
        ).start()

    def landed(like, sem):
        pltpu.make_async_copy(like, like, sem).wait()

    loads = [
        pltpu.make_async_copy(src, dst, lsem.at[i])
        for i, (src, dst) in enumerate((
            (fresh.at[0], fv.at[0]), (qgain, gq), (fresh.at[1], fv.at[1]), (kgain, gk),
            (fresh.at[2], fv.at[2]), (kcache, kc), (vcache, vc), (weight, wv),
        ))
    ]
    for load in loads[:6]:
        load.start()

    barrier = pltpu.get_barrier_semaphore()
    pairs = [(2, 1), (1, 1), (3, 1), (2, 0), (0, 1), (1, 0), (3, 0)]
    for dx, dy in pairs:
        pl.semaphore_signal(barrier, inc=1, device_id={"head": head_at(dx, dy)}, device_id_type=MESH)
    for offset in (-2, -1, 1, 2):
        pl.semaphore_signal(barrier, inc=1, device_id=blk_at(offset), device_id_type=MESH)

    live = counts[j]
    before = jnp.int32(0)
    for i in range(NB):
        before = before + jnp.where(i < j, counts[i], 0)
    shift = before - CH * j + BASE

    my_rows = pl.ds(pl.multiple_of(h * ROWS, ROWS), ROWS)

    def prepare(t):
        loads[2 * t].wait()
        if t == 2:
            for g in range(NG):
                sent[1, g] = fv[t, :, g * GROUP:(g + 1) * GROUP]
            got[1, my_rows] = sent[1, h]
            return
        loads[2 * t + 1].wait()
        rows = fv[t].astype(F32)
        factor = lax.rsqrt(jnp.mean(rows * rows, axis=-1, keepdims=True) + EPS)
        gains = (gq if t == 0 else gk)[...].astype(F32)
        for c in range(D // HEAD_DIM):
            cols = slice(c * HEAD_DIM, (c + 1) * HEAD_DIM)
            g, i = c // NH, c % NH
            value = (rows[:, cols] * factor * gains[c:c + 1] * (SCALE2 if t == 0 else 1.0)).astype(BF)
            if t == 0:
                sentq[i][g] = value
            else:
                sent[0, g, :, i * HEAD_DIM:(i + 1) * HEAD_DIM] = value
        if t == 0:
            for p in range(NP):
                gotq[p][my_rows] = sentq[p][h]
        else:
            got[0, my_rows] = sent[0, h]

    def spread(t):
        for dx, dy in pairs:
            peer = head_at(dx, dy)
            send(sent.at[t, peer], got.at[t, my_rows], 1, arecv.at[t], {"head": peer})

    prepare(0)
    pl.semaphore_wait(barrier, len(pairs) + 4)
    for p in range(NP):
        for dx, dy in pairs:
            peer = head_at(dx, dy)
            send(sentq[p].at[peer], gotq[p].at[my_rows], 0, qrecv.at[p], {"head": peer})
    for load in loads[6:]:
        load.start()
    prepare(1)
    spread(0)
    prepare(2)
    spread(1)

    r_id = lax.broadcasted_iota(jnp.int32, (SPAN, CAP), 0)
    s_id = lax.broadcasted_iota(jnp.int32, (1, CAP), 1)
    place = jnp.where(r_id == jnp.where(s_id < live, s_id + shift, -1), 1.0, 0.0).astype(BF)
    for p in range(NP):
        landed(gotq[p].at[0:CAP - ROWS], qrecv.at[p])
        selq[p][...] = mm(place, gotq[p][...]).astype(BF)
        for first, size, to, offset in ((64, 128, 0, -1), (320, 128, 128, 1), (0, 64, 256, -2), (448, 64, 320, 2)):
            send(selq[p].at[pl.ds(first, size)], rbuf[p].at[pl.ds(to, size)], 2, rrecv.at[p], blk_at(offset))
    back[...] = place.T
    pos = lax.broadcasted_iota(jnp.int32, (L_BLK, CAP), 0)
    hits = jnp.where(pos == jnp.where(s_id < live, ridx[...], -1), 1.0, 0.0)
    hit = jnp.sum(hits, axis=1, keepdims=True) > 0.5
    hits = hits.astype(BF)

    def gather_send(way, step, p):
        src = (8 - (step - 1)) % 8 if way == 0 else step - 1
        dst = 8 - step if way == 0 else step
        send(qs[p].at[src], qs[p].at[dst], 4, grecv.at[step - 1, p], blk_at(2 if way == 0 else -2))

    def gathered(step, p):
        landed(qs[p].at[0:2] if step < 4 else qs[p].at[0], grecv.at[step - 1, p])

    def gather_step(step, p):
        gathered(step - 1, p)
        for way in range(2):
            if step < 4 or p in LONG[way]:
                gather_send(way, step, p)

    for p in range(NP):
        landed(rbuf[p], rrecv.at[p])
        mine = (selq[p][192:320].astype(F32) + rbuf[p][0:128].astype(F32)) + rbuf[p][128:256].astype(F32)
        qs[p][0, 0:64] = (mine[0:64] + rbuf[p][320:384].astype(F32)).astype(BF)
        qs[p][0, 64:128] = (mine[64:128] + rbuf[p][256:320].astype(F32)).astype(BF)
        gather_send(0, 1, p)
        gather_send(1, 1, p)

    landed(got.at[0, 0:CAP - ROWS], arecv.at[0])
    loads[5].wait()
    kfull[0] = jnp.where(hit, mm(hits, got[0]), kc[...].astype(F32)).astype(BF)
    send(kfull.at[0], kfull.at[1], 3, krecv.at[0], sibling)
    for p in (0, 1):
        gather_step(2, p)
    landed(got.at[1, 0:CAP - ROWS], arecv.at[1])
    loads[6].wait()
    vt[0] = jnp.where(hit, mm(hits, got[1]), vc[...].astype(F32)).T.astype(BF)
    send(vt.at[0], vt.at[1], 3, krecv.at[1], sibling)
    for p in (2, 3, 4):
        gather_step(2, p)

    def attend(slots, need=None, done=None):
        def scores(i, b):
            query = [qs[i][s] for s in slots]
            query = query[0] if len(slots) == 1 else jnp.concatenate(query, axis=0)
            cols = slice(i * HEAD_DIM, (i + 1) * HEAD_DIM)
            return nt(kfull[b // 2, b % 2 * 256:b % 2 * 256 + 256, cols], query)

        def weighted(i, b, weights):
            return mm(vt[b // 2, i * HEAD_DIM:(i + 1) * HEAD_DIM, b % 2 * 256:b % 2 * 256 + 256], weights)

        def keep(i, value):
            for n, s in enumerate(slots):
                of[s, i * HEAD_DIM:(i + 1) * HEAD_DIM, :] = value[:, n * CH:(n + 1) * CH]
            if done is not None:
                done(i)

        if need is not None:
            need(0)
        now = [scores(0, b) for b in range(4)]
        last = []
        for i in range(NH):
            top = functools.reduce(jnp.maximum, [jnp.max(block, axis=0, keepdims=True) for block in now])
            if i + 1 < NH and need is not None:
                need(i + 1)
            ahead, weights, total, value = [], [], 0.0, 0.0
            for b in range(4):
                if i + 1 < NH:
                    ahead.append(scores(i + 1, b))
                one = jnp.exp2(now[b] - top)
                total = total + jnp.sum(one, axis=0, keepdims=True)
                weights.append(one.astype(BF))
                if i:
                    value = value + weighted(i - 1, b, last[b])
            for n, s in enumerate(slots):
                st[s, i, 0:1, :] = top[:, n * CH:(n + 1) * CH]
                st[s, i, 1:2, :] = total[:, n * CH:(n + 1) * CH]
            if i:
                keep(i - 1, value)
            now, last = ahead, weights
        value = functools.reduce(jnp.add, [weighted(NH - 1, b, last[b]) for b in range(4)])
        keep(NH - 1, value)

    def first_needs(p):
        gather_step(3, p)
        if p == 2:
            landed(vt.at[1], krecv.at[1])

    landed(kfull.at[1], krecv.at[0])
    attend((0, 7, 1), need=first_needs)
    attend((6, 2), need=functools.partial(gather_step, 4))

    def joined(slot, i, arrivals):
        rows = slice(i * HEAD_DIM, (i + 1) * HEAD_DIM)
        tops = [st[slot, i, 0:1]] + [rs[way, step, i, 0:1] for way, step in arrivals]
        sums = [st[slot, i, 1:2]] + [rs[way, step, i, 1:2] for way, step in arrivals]
        top = functools.reduce(jnp.maximum, tops)
        factors = [jnp.exp2(t - top) for t in tops]
        total = sum(a * f for a, f in zip(sums, factors))
        value = of[slot, rows, :] * factors[0]
        for n, (way, step) in enumerate(arrivals):
            value = value + ro[way, step, rows, :].astype(F32) * factors[n + 1]
        return value, top, total

    def give(way, step, p):
        ahead = 5 - step
        slot = ahead if way == 0 else 8 - ahead
        rows = slice(p * HEAD_DIM, (p + 1) * HEAD_DIM)
        if step > (1 if p in LONG[way] else 2):
            landed(unit.at[0:33], drecv.at[way, step - 2, p])
            value, top, total = joined(slot, p, [(way, step - 2)])
        else:
            value, top, total = of[slot, rows, :], st[slot, p, 0:1], st[slot, p, 1:2]
        so[way, step - 1, rows, :] = value.astype(BF)
        ss[way, step - 1, p, 0:1] = top
        ss[way, step - 1, p, 1:2] = total
        rows = pl.ds(p * HEAD_DIM, HEAD_DIM)
        dev = blk_at(2 if way == 0 else -2)
        send(ss.at[way, step - 1, p], rs.at[way, step - 1, p], 6, drecv.at[way, step - 1, p], dev)
        send(so.at[way, step - 1, rows], ro.at[way, step - 1, rows], 5, drecv.at[way, step - 1, p], dev)

    def long_way(p):
        return 0 if p in LONG[0] else 1

    attend((4,), need=lambda p: gathered(4, p), done=lambda p: give(long_way(p), 1, p))
    attend((5, 3), done=lambda p: give(1 - long_way(p), 2, p))
    for p in range(NP):
        give(long_way(p), 2, p)
    order = (LONG[1] + LONG[0], LONG[0] + LONG[1])
    for step in (3, 4):
        for both in zip(*order):
            for way in range(2):
                give(way, step, both[way])
    last_in = sorted(range(NP), key=lambda p: max(order[0].index(p), order[1].index(p)))

    for p in last_in:
        for way in range(2):
            landed(unit.at[0:33], drecv.at[way, 3, p])
        value, _, total = joined(0, p, [(0, 3), (1, 3)])
        abuf[p][...] = (value / total).T.astype(BF)
        for first, size, to, offset in ((0, 128, 320, -1), (0, 128, 64, 1), (0, 64, 448, -2), (64, 64, 0, 2)):
            send(abuf[p].at[pl.ds(first, size)], cat[p].at[pl.ds(to, size)], 7, urecv.at[p], blk_at(offset))
        cat[p][192:320] = abuf[p][...]
    for p in last_in:
        landed(rbuf[p], urecv.at[p])
        att[:, p * HEAD_DIM:(p + 1) * HEAD_DIM] = mm(back[...], cat[p][...]).astype(BF)

    loads[7].wait()

    def project(first, last):
        for at in range(first, last, 512):
            cols = slice(at, at + 512)
            tile = mm(att[...], wv[:, cols]).astype(BF)
            for g in range(NG):
                pb[g // 2, g % 2, :, cols] = tile[g * ROWS:(g + 1) * ROWS]

    up, down, far = lax.rem(x + 1, 4), lax.rem(x + 3, 4), lax.rem(x + 2, 4)
    to_up, to_down = {"head": up * 2 + y}, {"head": down * 2 + y}
    to_pair = {"head": x * 2 + 1 - y}

    def give_sum(kind, g, n, src, dst, dev):
        send(src, dst, 8, erecv.at[kind, g, (0, 2, 1, 2, 2, 2, 3)[n]], dev)

    def ring_start(kind, g, part, dst, first, half):
        a, b = pl.ds(first, half), pl.ds(first + half, half)
        give_sum(kind, g, 0, part(far, a), dst.at[0], to_up)
        give_sum(kind, g, 2, part(far, b), dst.at[2], to_down)
        give_sum(kind, g, 1, part(down, a), dst.at[1], to_down)
        give_sum(kind, g, 3, part(up, b), dst.at[3], to_up)

    def ring_pass(kind, g, load, dst, total, first, half):
        for n, other, cols, dev in ((0, up, first, to_up), (2, down, first + half, to_down)):
            landed(dst.at[n], erecv.at[kind, g, n // 2])
            total[n // 2] = (dst[n].astype(F32) + load(other, slice(cols, cols + half)).astype(F32)).astype(BF)
            give_sum(kind, g, 4 + n // 2, total.at[n // 2], dst.at[4 + n // 2], dev)

    def add(*terms):
        return functools.reduce(jnp.add, [t.astype(F32) for t in terms])

    def x_start(g):
        first, width = XG[g]
        project(first, first + width)
        ring_start(0, g, lambda to, cols: pb.at[to, :, :, cols], rx1[g], first, width // 2)

    def x_pass(g):
        first, width = XG[g]
        ring_pass(0, g, lambda to, cols: pb[to, :, :, cols], rx1[g], ac1[g], first, width // 2)

    def x_sums(g, row):
        first, width = XG[g]
        half = width // 2
        return (
            add(pb[x, row, :, first:first + half], rx1[g][4, row], rx1[g][1, row]),
            add(pb[x, row, :, first + half:first + width], rx1[g][5, row], rx1[g][3, row]),
        )

    def x_turn(g):
        half = XG[g][1] // 2
        landed(rx1[g].at[0:4], erecv.at[0, g, 2])
        one, two = x_sums(g, 1 - y)
        sy1[g][:, 0:half] = one.astype(BF)
        sy1[g][:, half:2 * half] = two.astype(BF)
        give_sum(0, g, 6, sy1[g], ry1[g], to_pair)

    def x_end(g):
        first, width = XG[g]
        half = width // 2
        landed(ry1[g], erecv.at[0, g, 3])
        one, two = x_sums(g, y)
        out[:, first:first + half] = add(one, ry1[g][:, 0:half]).astype(BF)
        out[:, first + half:first + width] = add(two, ry1[g][:, half:width]).astype(BF)

    def y_start(g):
        first, width = YG[g]
        project(first, first + width)
        give_sum(1, g, 6, pb.at[:, 1 - y, :, pl.ds(first, width)], ry2[g], to_pair)

    def y_turn(g):
        first, width = YG[g]
        landed(ry2[g], erecv.at[1, g, 3])
        for i in range(4):
            sx2[g][i] = add(ry2[g][i], pb[i, y, :, first:first + width]).astype(BF)
        if g < len(YG) - 1:
            ring_start(1, g, lambda to, cols: sx2[g].at[to, :, cols], rx2[g], 0, width // 2)
            return
        for n, (to, dev) in enumerate(((far, {"head": far * 2 + y}), (up, to_up), (down, to_down))):
            send(sx2[g].at[to], rx3.at[n], 8, erecv.at[1, g, 2], dev)

    def y_pass(g):
        ring_pass(1, g, lambda to, cols: sx2[g][to, :, cols], rx2[g], ac2[g], 0, YG[g][1] // 2)

    def y_end(g):
        first, width = YG[g]
        half = width // 2
        if g == len(YG) - 1:
            landed(rx3, erecv.at[1, g, 2])
            out[:, first:first + width] = add(sx2[g][x], rx3[0], rx3[1], rx3[2]).astype(BF)
            return
        landed(rx2[g].at[0:4], erecv.at[1, g, 2])
        out[:, first:first + half] = add(sx2[g][x, :, 0:half], rx2[g][4], rx2[g][1]).astype(BF)
        out[:, first + half:first + width] = add(sx2[g][x, :, half:width], rx2[g][5], rx2[g][3]).astype(BF)

    x_start(0)
    y_start(0)
    x_start(1)
    y_start(1)
    x_start(2)
    x_pass(0)
    x_pass(1)
    y_turn(0)
    x_turn(0)
    x_pass(2)
    y_turn(1)
    x_turn(1)
    y_pass(0)
    x_turn(2)
    x_end(0)
    x_end(1)
    y_end(0)
    x_end(2)
    y_end(1)

    for phase, rows, cols in (
        (0, 32, 4480), (1, 64, 4480), (2, 64, 3840), (3, 128, 5120), (4, 128, 4480), (5, 128, 4480),
        (7, 64, 3840), (8, 256, 4480),
    ):
        landed(wv.at[0:rows, 0:cols], ssem.at[phase])
    landed(unit, ssem.at[6])


def local(fresh, rows_index, counts, key_cache, value_cache, q_gain, k_gain, out_weight):
    any_spec = pl.BlockSpec(memory_space=pl.ANY)
    vmem = pl.BlockSpec(memory_space=pltpu.VMEM)
    dma = pltpu.SemaphoreType.DMA
    V = pltpu.VMEM

    def by_piece(*dims):
        return [V(dims + (HEAD_DIM,), BF)] * NP

    return pl.pallas_call(
        kernel,
        out_shape=V((ROWS, D), BF),
        in_specs=[any_spec, vmem, pl.BlockSpec(memory_space=pltpu.SMEM)] + [any_spec] * 5,
        out_specs=vmem,
        scratch_shapes=[
            V((3, ROWS, D), BF), V((D // 128, 128), BF), V((D // 128, 128), BF),
            V((L_BLK, GROUP), BF), V((L_BLK, GROUP), BF), V((GROUP, D), BF),
            V((2, NG, ROWS, GROUP), BF), V((2, CAP, GROUP), BF),
            by_piece(NG, ROWS), by_piece(CAP), by_piece(SPAN), by_piece(384),
            V((2, L_BLK, GROUP), BF), V((2, GROUP, L_BLK), BF), by_piece(8, CH),
            V((8, GROUP, CH), F32), V((8, NH, 2, CH), F32),
            V((2, 4, GROUP, CH), BF), V((2, 4, NH, 2, CH), F32),
            V((2, 4, GROUP, CH), BF), V((2, 4, NH, 2, CH), F32),
            by_piece(CH), by_piece(SPAN), V((CAP, SPAN), BF), V((CAP, GROUP), BF),
            V((4, 2, ROWS, D), BF),
            [V((6, 2, ROWS, w // 2), BF) for _, w in XG], [V((2, 2, ROWS, w // 2), BF) for _, w in XG],
            [V((ROWS, w), BF) for _, w in XG], [V((ROWS, w), BF) for _, w in XG],
            [V((4, ROWS, w), BF) for _, w in YG], [V((4, ROWS, w), BF) for _, w in YG],
            [V((6, ROWS, w // 2), BF) for _, w in YG], [V((2, ROWS, w // 2), BF) for _, w in YG],
            V((3, ROWS, YG[-1][1]), BF),
            V((35, 2, CH), F32), dma((8,)), dma((9,)), dma((NP,)), dma((2,)), dma((NP,)), dma((2,)),
            dma((4, NP)), dma((2, 4, NP)), dma((NP,)), dma((2, 3, 4)),
        ],
        compiler_params=pltpu.CompilerParams(
            collective_id=0, has_side_effects=True, vmem_limit_bytes=56 * 1024 * 1024
        ),
    )(
        jnp.transpose(fresh, (1, 0, 2)), rows_index.reshape(1, CAP), counts, key_cache, value_cache,
        q_gain.reshape(D // 128, 128), k_gain.reshape(D // 128, 128), out_weight,
    )


def solution(mesh):
    placed = (
        P(("cfg", "blk", "head"), None, None),
        P("blk"),
        P(),
        P(("cfg", "blk"), "head"),
        P(("cfg", "blk"), "head"),
        P(),
        P(),
        P("head", None),
    )
    return jax.shard_map(
        local,
        mesh=mesh,
        in_specs=placed,
        out_specs=P(("cfg", "blk", "head"), None),
        check_vma=False,
    )
```

```python
import functools
import math

import jax
import jax.numpy as jnp
from jax import lax
from jax.experimental import pallas as pl
from jax.experimental.pallas import tpu as pltpu
from jax.sharding import PartitionSpec as P

HEAD_DIM = 128
EPS = 1e-06
MESH = pl.DeviceIdType.MESH
BF = jnp.bfloat16
F32 = jnp.float32

D = 5120
GROUP = 640
NH = GROUP // HEAD_DIM
NG = 8
NB = 16
CAP = 256
L_BLK = 512
ROWS = 32
CH = 128
SPAN = 512
BASE = 192
NP = NH
LONG = ((0, 1), (2, 3, 4))
XG = ((0, 1024), (1024, 1536), (2560, 512))
YG = ((3072, 1536), (4608, 512))
SCALE2 = math.log2(math.e) / math.sqrt(HEAD_DIM)


def nt(a, b):
    return lax.dot_general(a, b, (((1,), (1,)), ((), ())), preferred_element_type=F32)


def mm(a, b):
    return jnp.dot(a, b, preferred_element_type=F32)


def kernel(
    fresh, ridx, counts, kcache, vcache, qgain, kgain, weight, out,
    fv, gq, gk, kc, vc, wv, sent, got, sentq, gotq, selq, rbuf, kfull, vt, qs,
    of, st, so, ss, ro, rs, abuf, cat, back, att, pb,
    rx1, ac1, ry1, sy1, ry2, sx2, rx2, ac2, rx3,
    unit, lsem, ssem, qrecv, arecv, rrecv, krecv, grecv, drecv, urecv, erecv,
):
    j = lax.axis_index("blk")
    h = lax.axis_index("head")
    core = lax.rem(j, 2)
    x, y = lax.div(h, 2), lax.rem(h, 2)

    def blk_at(offset):
        return {"blk": lax.rem(j + offset + NB, NB)}

    sibling = {"blk": j + 1 - 2 * core}

    def head_at(dx, dy):
        other_y = 1 - y if dy else y
        return lax.rem(x + dx, 4) * 2 + other_y

    def send(src, dst, phase, r, dev):
        pltpu.make_async_remote_copy(
            src_ref=src, dst_ref=dst, send_sem=ssem.at[phase], recv_sem=r, device_id=dev, device_id_type=MESH
        ).start()

    def landed(like, sem):
        pltpu.make_async_copy(like, like, sem).wait()

    loads = [
        pltpu.make_async_copy(src, dst, lsem.at[i])
        for i, (src, dst) in enumerate((
            (fresh.at[0], fv.at[0]), (qgain, gq), (fresh.at[1], fv.at[1]), (kgain, gk),
            (fresh.at[2], fv.at[2]), (kcache, kc), (vcache, vc), (weight, wv),
        ))
    ]
    for load in loads[:6]:
        load.start()

    barrier = pltpu.get_barrier_semaphore()
    pairs = [(2, 1), (1, 1), (3, 1), (2, 0), (0, 1), (1, 0), (3, 0)]
    for dx, dy in pairs:
        pl.semaphore_signal(barrier, inc=1, device_id={"head": head_at(dx, dy)}, device_id_type=MESH)
    for offset in (-2, -1, 1, 2):
        pl.semaphore_signal(barrier, inc=1, device_id=blk_at(offset), device_id_type=MESH)

    live = counts[j]
    before = jnp.int32(0)
    for i in range(NB):
        before = before + jnp.where(i < j, counts[i], 0)
    shift = before - CH * j + BASE

    my_rows = pl.ds(pl.multiple_of(h * ROWS, ROWS), ROWS)

    def prepare(t):
        loads[2 * t].wait()
        if t == 2:
            for g in range(NG):
                sent[1, g] = fv[t, :, g * GROUP:(g + 1) * GROUP]
            got[1, my_rows] = sent[1, h]
            return
        loads[2 * t + 1].wait()
        rows = fv[t].astype(F32)
        factor = lax.rsqrt(jnp.mean(rows * rows, axis=-1, keepdims=True) + EPS)
        gains = (gq if t == 0 else gk)[...].astype(F32)
        for c in range(D // HEAD_DIM):
            cols = slice(c * HEAD_DIM, (c + 1) * HEAD_DIM)
            g, i = c // NH, c % NH
            value = (rows[:, cols] * factor * gains[c:c + 1] * (SCALE2 if t == 0 else 1.0)).astype(BF)
            if t == 0:
                sentq[i][g] = value
            else:
                sent[0, g, :, i * HEAD_DIM:(i + 1) * HEAD_DIM] = value
        if t == 0:
            for p in range(NP):
                gotq[p][my_rows] = sentq[p][h]
        else:
            got[0, my_rows] = sent[0, h]

    def spread(t):
        for dx, dy in pairs:
            peer = head_at(dx, dy)
            send(sent.at[t, peer], got.at[t, my_rows], 1, arecv.at[t], {"head": peer})

    prepare(0)
    pl.semaphore_wait(barrier, len(pairs) + 4)
    for p in range(NP):
        for dx, dy in pairs:
            peer = head_at(dx, dy)
            send(sentq[p].at[peer], gotq[p].at[my_rows], 0, qrecv.at[p], {"head": peer})
    for load in loads[6:]:
        load.start()
    prepare(1)
    spread(0)
    prepare(2)
    spread(1)

    r_id = lax.broadcasted_iota(jnp.int32, (SPAN, CAP), 0)
    s_id = lax.broadcasted_iota(jnp.int32, (1, CAP), 1)
    place = jnp.where(r_id == jnp.where(s_id < live, s_id + shift, -1), 1.0, 0.0).astype(BF)
    for p in range(NP):
        landed(gotq[p].at[0:CAP - ROWS], qrecv.at[p])
        selq[p][...] = mm(place, gotq[p][...]).astype(BF)
        for first, size, to, offset in ((64, 128, 0, -1), (320, 128, 128, 1), (0, 64, 256, -2), (448, 64, 320, 2)):
            send(selq[p].at[pl.ds(first, size)], rbuf[p].at[pl.ds(to, size)], 2, rrecv.at[p], blk_at(offset))
    back[...] = place.T
    pos = lax.broadcasted_iota(jnp.int32, (L_BLK, CAP), 0)
    hits = jnp.where(pos == jnp.where(s_id < live, ridx[...], -1), 1.0, 0.0)
    hit = jnp.sum(hits, axis=1, keepdims=True) > 0.5
    hits = hits.astype(BF)

    def gather_send(way, step, p):
        src = (8 - (step - 1)) % 8 if way == 0 else step - 1
        dst = 8 - step if way == 0 else step
        send(qs[p].at[src], qs[p].at[dst], 4, grecv.at[step - 1, p], blk_at(2 if way == 0 else -2))

    def gathered(step, p):
        landed(qs[p].at[0:2] if step < 4 else qs[p].at[0], grecv.at[step - 1, p])

    def gather_step(step, p):
        gathered(step - 1, p)
        for way in range(2):
            if step < 4 or p in LONG[way]:
                gather_send(way, step, p)

    for p in range(NP):
        landed(rbuf[p], rrecv.at[p])
        mine = (selq[p][192:320].astype(F32) + rbuf[p][0:128].astype(F32)) + rbuf[p][128:256].astype(F32)
        qs[p][0, 0:64] = (mine[0:64] + rbuf[p][320:384].astype(F32)).astype(BF)
        qs[p][0, 64:128] = (mine[64:128] + rbuf[p][256:320].astype(F32)).astype(BF)
        gather_send(0, 1, p)
        gather_send(1, 1, p)

    landed(got.at[0, 0:CAP - ROWS], arecv.at[0])
    loads[5].wait()
    kfull[0] = jnp.where(hit, mm(hits, got[0]), kc[...].astype(F32)).astype(BF)
    send(kfull.at[0], kfull.at[1], 3, krecv.at[0], sibling)
    for p in (0, 1):
        gather_step(2, p)
    landed(got.at[1, 0:CAP - ROWS], arecv.at[1])
    loads[6].wait()
    vt[0] = jnp.where(hit, mm(hits, got[1]), vc[...].astype(F32)).T.astype(BF)
    send(vt.at[0], vt.at[1], 3, krecv.at[1], sibling)
    for p in (2, 3, 4):
        gather_step(2, p)

    def attend(slots, need=None, done=None):
        def scores(i, b):
            query = [qs[i][s] for s in slots]
            query = query[0] if len(slots) == 1 else jnp.concatenate(query, axis=0)
            cols = slice(i * HEAD_DIM, (i + 1) * HEAD_DIM)
            return nt(kfull[b // 2, b % 2 * 256:b % 2 * 256 + 256, cols], query)

        def weighted(i, b, weights):
            return mm(vt[b // 2, i * HEAD_DIM:(i + 1) * HEAD_DIM, b % 2 * 256:b % 2 * 256 + 256], weights)

        def keep(i, value):
            for n, s in enumerate(slots):
                of[s, i * HEAD_DIM:(i + 1) * HEAD_DIM, :] = value[:, n * CH:(n + 1) * CH]
            if done is not None:
                done(i)

        if need is not None:
            need(0)
        now = [scores(0, b) for b in range(4)]
        last = []
        for i in range(NH):
            top = functools.reduce(jnp.maximum, [jnp.max(block, axis=0, keepdims=True) for block in now])
            if i + 1 < NH and need is not None:
                need(i + 1)
            ahead, weights, total, value = [], [], 0.0, 0.0
            for b in range(4):
                if i + 1 < NH:
                    ahead.append(scores(i + 1, b))
                one = jnp.exp2(now[b] - top)
                total = total + jnp.sum(one, axis=0, keepdims=True)
                weights.append(one.astype(BF))
                if i:
                    value = value + weighted(i - 1, b, last[b])
            for n, s in enumerate(slots):
                st[s, i, 0:1, :] = top[:, n * CH:(n + 1) * CH]
                st[s, i, 1:2, :] = total[:, n * CH:(n + 1) * CH]
            if i:
                keep(i - 1, value)
            now, last = ahead, weights
        value = functools.reduce(jnp.add, [weighted(NH - 1, b, last[b]) for b in range(4)])
        keep(NH - 1, value)

    def first_needs(p):
        gather_step(3, p)
        if p == 2:
            landed(vt.at[1], krecv.at[1])

    landed(kfull.at[1], krecv.at[0])
    attend((0, 7, 1), need=first_needs)
    attend((6, 2), need=functools.partial(gather_step, 4))

    def joined(slot, i, arrivals):
        rows = slice(i * HEAD_DIM, (i + 1) * HEAD_DIM)
        tops = [st[slot, i, 0:1]] + [rs[way, step, i, 0:1] for way, step in arrivals]
        sums = [st[slot, i, 1:2]] + [rs[way, step, i, 1:2] for way, step in arrivals]
        top = functools.reduce(jnp.maximum, tops)
        factors = [jnp.exp2(t - top) for t in tops]
        total = sum(a * f for a, f in zip(sums, factors))
        value = of[slot, rows, :] * factors[0]
        for n, (way, step) in enumerate(arrivals):
            value = value + ro[way, step, rows, :].astype(F32) * factors[n + 1]
        return value, top, total

    def joins(way, step, p):
        return drecv.at[p if step == 1 else 25 + p if step == 4 else 5 + 10 * (step - 2) + 5 * way + p]

    def give(way, step, p):
        ahead = 5 - step
        slot = ahead if way == 0 else 8 - ahead
        rows = slice(p * HEAD_DIM, (p + 1) * HEAD_DIM)
        if step > (1 if p in LONG[way] else 2):
            landed(unit.at[0:33], joins(way, step - 1, p))
            value, top, total = joined(slot, p, [(way, step - 2)])
        else:
            value, top, total = of[slot, rows, :], st[slot, p, 0:1], st[slot, p, 1:2]
        so[way, step - 1, rows, :] = value.astype(BF)
        ss[way, step - 1, p, 0:1] = top
        ss[way, step - 1, p, 1:2] = total
        rows = pl.ds(p * HEAD_DIM, HEAD_DIM)
        dev = blk_at(2 if way == 0 else -2)
        send(ss.at[way, step - 1, p], rs.at[way, step - 1, p], 6, joins(way, step, p), dev)
        send(so.at[way, step - 1, rows], ro.at[way, step - 1, rows], 5, joins(way, step, p), dev)

    def long_way(p):
        return 0 if p in LONG[0] else 1

    attend((4,), need=lambda p: gathered(4, p), done=lambda p: give(long_way(p), 1, p))
    attend((5, 3), done=lambda p: give(1 - long_way(p), 2, p))
    for p in range(NP):
        give(long_way(p), 2, p)
    order = (LONG[1] + LONG[0], LONG[0] + LONG[1])
    for step in (3, 4):
        for both in zip(*order):
            for way in range(2):
                give(way, step, both[way])
    last_in = sorted(range(NP), key=lambda p: max(order[0].index(p), order[1].index(p)))

    for p in last_in:
        landed(unit, joins(0, 4, p))
        value, _, total = joined(0, p, [(0, 3), (1, 3)])
        abuf[p][...] = (value * (1.0 / total)).T.astype(BF)
        for first, size, to, offset in ((0, 128, 320, -1), (0, 128, 64, 1), (0, 64, 448, -2), (64, 64, 0, 2)):
            send(abuf[p].at[pl.ds(first, size)], cat[p].at[pl.ds(to, size)], 7, urecv.at[p], blk_at(offset))
        cat[p][192:320] = abuf[p][...]
    for p in last_in:
        landed(rbuf[p], urecv.at[p])
        att[:, p * HEAD_DIM:(p + 1) * HEAD_DIM] = mm(back[...], cat[p][...]).astype(BF)

    loads[7].wait()

    def project(first, last):
        for at in range(first, last, 512):
            cols = slice(at, at + 512)
            tile = mm(att[...], wv[:, cols]).astype(BF)
            for g in range(NG):
                pb[g // 2, g % 2, :, cols] = tile[g * ROWS:(g + 1) * ROWS]

    up, down, far = lax.rem(x + 1, 4), lax.rem(x + 3, 4), lax.rem(x + 2, 4)
    to_up, to_down = {"head": up * 2 + y}, {"head": down * 2 + y}
    to_pair = {"head": x * 2 + 1 - y}

    def give_sum(kind, g, n, src, dst, dev):
        send(src, dst, 8, erecv.at[kind, g, (0, 2, 1, 2, 2, 2, 3)[n]], dev)

    def ring_start(kind, g, part, dst, first, half):
        a, b = pl.ds(first, half), pl.ds(first + half, half)
        give_sum(kind, g, 0, part(far, a), dst.at[0], to_up)
        give_sum(kind, g, 2, part(far, b), dst.at[2], to_down)
        give_sum(kind, g, 1, part(down, a), dst.at[1], to_down)
        give_sum(kind, g, 3, part(up, b), dst.at[3], to_up)

    def ring_pass(kind, g, load, dst, total, first, half):
        for n, other, cols, dev in ((0, up, first, to_up), (2, down, first + half, to_down)):
            landed(dst.at[n], erecv.at[kind, g, n // 2])
            total[n // 2] = (dst[n].astype(F32) + load(other, slice(cols, cols + half)).astype(F32)).astype(BF)
            give_sum(kind, g, 4 + n // 2, total.at[n // 2], dst.at[4 + n // 2], dev)

    def add(*terms):
        return functools.reduce(jnp.add, [t.astype(F32) for t in terms])

    def x_start(g):
        first, width = XG[g]
        project(first, first + width)
        ring_start(0, g, lambda to, cols: pb.at[to, :, :, cols], rx1[g], first, width // 2)

    def x_pass(g):
        first, width = XG[g]
        ring_pass(0, g, lambda to, cols: pb[to, :, :, cols], rx1[g], ac1[g], first, width // 2)

    def x_sums(g, row):
        first, width = XG[g]
        half = width // 2
        return (
            add(pb[x, row, :, first:first + half], rx1[g][4, row], rx1[g][1, row]),
            add(pb[x, row, :, first + half:first + width], rx1[g][5, row], rx1[g][3, row]),
        )

    def x_turn(g):
        half = XG[g][1] // 2
        landed(rx1[g].at[0:4], erecv.at[0, g, 2])
        one, two = x_sums(g, 1 - y)
        sy1[g][:, 0:half] = one.astype(BF)
        sy1[g][:, half:2 * half] = two.astype(BF)
        give_sum(0, g, 6, sy1[g], ry1[g], to_pair)

    def x_end(g):
        first, width = XG[g]
        half = width // 2
        landed(ry1[g], erecv.at[0, g, 3])
        one, two = x_sums(g, y)
        out[:, first:first + half] = add(one, ry1[g][:, 0:half]).astype(BF)
        out[:, first + half:first + width] = add(two, ry1[g][:, half:width]).astype(BF)

    def y_start(g):
        first, width = YG[g]
        project(first, first + width)
        give_sum(1, g, 6, pb.at[:, 1 - y, :, pl.ds(first, width)], ry2[g], to_pair)

    def y_turn(g):
        first, width = YG[g]
        landed(ry2[g], erecv.at[1, g, 3])
        for i in range(4):
            sx2[g][i] = add(ry2[g][i], pb[i, y, :, first:first + width]).astype(BF)
        if g < len(YG) - 1:
            ring_start(1, g, lambda to, cols: sx2[g].at[to, :, cols], rx2[g], 0, width // 2)
            return
        for n, (to, dev) in enumerate(((far, {"head": far * 2 + y}), (up, to_up), (down, to_down))):
            send(sx2[g].at[to], rx3.at[n], 8, erecv.at[1, g, 2], dev)

    def y_pass(g):
        ring_pass(1, g, lambda to, cols: sx2[g][to, :, cols], rx2[g], ac2[g], 0, YG[g][1] // 2)

    def y_end(g):
        first, width = YG[g]
        half = width // 2
        if g == len(YG) - 1:
            landed(rx3, erecv.at[1, g, 2])
            out[:, first:first + width] = add(sx2[g][x], rx3[0], rx3[1], rx3[2]).astype(BF)
            return
        landed(rx2[g].at[0:4], erecv.at[1, g, 2])
        out[:, first:first + half] = add(sx2[g][x, :, 0:half], rx2[g][4], rx2[g][1]).astype(BF)
        out[:, first + half:first + width] = add(sx2[g][x, :, half:width], rx2[g][5], rx2[g][3]).astype(BF)

    x_start(0)
    y_start(0)
    x_start(1)
    y_start(1)
    x_start(2)
    x_pass(0)
    x_pass(1)
    y_turn(0)
    x_turn(0)
    x_pass(2)
    y_turn(1)
    x_turn(1)
    y_pass(0)
    x_turn(2)
    x_end(0)
    x_end(1)
    y_end(0)
    x_end(2)
    y_end(1)

    for phase, rows, cols in (
        (0, 32, 4480), (1, 64, 4480), (2, 64, 3840), (3, 128, 5120), (4, 128, 4480), (5, 128, 4480),
        (7, 64, 3840), (8, 256, 4480),
    ):
        landed(wv.at[0:rows, 0:cols], ssem.at[phase])
    landed(unit.at[0:35], ssem.at[6])


def local(fresh, rows_index, counts, key_cache, value_cache, q_gain, k_gain, out_weight):
    any_spec = pl.BlockSpec(memory_space=pl.ANY)
    vmem = pl.BlockSpec(memory_space=pltpu.VMEM)
    dma = pltpu.SemaphoreType.DMA
    V = pltpu.VMEM

    def by_piece(*dims):
        return [V(dims + (HEAD_DIM,), BF)] * NP

    return pl.pallas_call(
        kernel,
        out_shape=V((ROWS, D), BF),
        in_specs=[any_spec, vmem, pl.BlockSpec(memory_space=pltpu.SMEM)] + [any_spec] * 5,
        out_specs=vmem,
        scratch_shapes=[
            V((3, ROWS, D), BF), V((D // 128, 128), BF), V((D // 128, 128), BF),
            V((L_BLK, GROUP), BF), V((L_BLK, GROUP), BF), V((GROUP, D), BF),
            V((2, NG, ROWS, GROUP), BF), V((2, CAP, GROUP), BF),
            by_piece(NG, ROWS), by_piece(CAP), by_piece(SPAN), by_piece(384),
            V((2, L_BLK, GROUP), BF), V((2, GROUP, L_BLK), BF), by_piece(8, CH),
            V((8, GROUP, CH), F32), V((8, NH, 2, CH), F32),
            V((2, 4, GROUP, CH), BF), V((2, 4, NH, 2, CH), F32),
            V((2, 4, GROUP, CH), BF), V((2, 4, NH, 2, CH), F32),
            by_piece(CH), by_piece(SPAN), V((CAP, SPAN), BF), V((CAP, GROUP), BF),
            V((4, 2, ROWS, D), BF),
            [V((6, 2, ROWS, w // 2), BF) for _, w in XG], [V((2, 2, ROWS, w // 2), BF) for _, w in XG],
            [V((ROWS, w), BF) for _, w in XG], [V((ROWS, w), BF) for _, w in XG],
            [V((4, ROWS, w), BF) for _, w in YG], [V((4, ROWS, w), BF) for _, w in YG],
            [V((6, ROWS, w // 2), BF) for _, w in YG], [V((2, ROWS, w // 2), BF) for _, w in YG],
            V((3, ROWS, YG[-1][1]), BF),
            V((66, 2, CH), F32), dma((8,)), dma((9,)), dma((NP,)), dma((2,)), dma((NP,)), dma((2,)),
            dma((4, NP)), dma((30,)), dma((NP,)), dma((2, 3, 4)),
        ],
        compiler_params=pltpu.CompilerParams(
            collective_id=0, has_side_effects=True, vmem_limit_bytes=56 * 1024 * 1024
        ),
    )(
        jnp.transpose(fresh, (1, 0, 2)), rows_index.reshape(1, CAP), counts, key_cache, value_cache,
        q_gain.reshape(D // 128, 128), k_gain.reshape(D // 128, 128), out_weight,
    )


def solution(mesh):
    placed = (
        P(("cfg", "blk", "head"), None, None),
        P("blk"),
        P(),
        P(("cfg", "blk"), "head"),
        P(("cfg", "blk"), "head"),
        P(),
        P(),
        P("head", None),
    )
    return jax.shard_map(
        local,
        mesh=mesh,
        in_specs=placed,
        out_specs=P(("cfg", "blk", "head"), None),
        check_vma=False,
    )
```

```python
import functools
import math

import jax
import jax.numpy as jnp
from jax import lax
from jax.experimental import pallas as pl
from jax.experimental.pallas import tpu as pltpu
from jax.sharding import PartitionSpec as P

HEAD_DIM = 128
EPS = 1e-06
MESH = pl.DeviceIdType.MESH
BF = jnp.bfloat16
F32 = jnp.float32

D = 5120
GROUP = 640
NH = GROUP // HEAD_DIM
NG = 8
NB = 16
CAP = 256
L_BLK = 512
ROWS = 32
CH = 128
SPAN = 512
BASE = 192
NP = NH
LONG = ((0, 1), (2, 3, 4))
XG = ((0, 1024), (1024, 1536), (2560, 512))
YG = ((3072, 1536), (4608, 512))
SCALE2 = math.log2(math.e) / math.sqrt(HEAD_DIM)


def nt(a, b):
    return lax.dot_general(a, b, (((1,), (1,)), ((), ())), preferred_element_type=F32)


def mm(a, b):
    return jnp.dot(a, b, preferred_element_type=F32)


def kernel(
    fresh, ridx, counts, kcache, vcache, qgain, kgain, weight, out,
    fv, gq, gk, kc, vc, wv, sent, got, sentq, gotq, selq, rbuf, kfull, vt, qs,
    of, st, so, ss, ro, rs, abuf, cat, back, att, pb,
    rx1, ac1, ry1, sy1, ry2, sx2, rx2, ac2, rx3,
    unit, lsem, ssem, qrecv, arecv, rrecv, krecv, grecv, drecv, urecv, erecv,
):
    j = lax.axis_index("blk")
    h = lax.axis_index("head")
    core = lax.rem(j, 2)
    x, y = lax.div(h, 2), lax.rem(h, 2)

    def blk_at(offset):
        return {"blk": lax.rem(j + offset + NB, NB)}

    sibling = {"blk": j + 1 - 2 * core}

    def head_at(dx, dy):
        other_y = 1 - y if dy else y
        return lax.rem(x + dx, 4) * 2 + other_y

    def send(src, dst, phase, r, dev):
        pltpu.make_async_remote_copy(
            src_ref=src, dst_ref=dst, send_sem=ssem.at[phase], recv_sem=r, device_id=dev, device_id_type=MESH
        ).start()

    def landed(like, sem):
        pltpu.make_async_copy(like, like, sem).wait()

    loads = [
        pltpu.make_async_copy(src, dst, lsem.at[i])
        for i, (src, dst) in enumerate((
            (fresh.at[0], fv.at[0]), (qgain, gq), (fresh.at[1], fv.at[1]), (kgain, gk),
            (fresh.at[2], fv.at[2]), (kcache, kc), (vcache, vc), (weight, wv),
        ))
    ]
    for load in loads[:6]:
        load.start()

    barrier = pltpu.get_barrier_semaphore()
    pairs = [(2, 1), (1, 1), (3, 1), (2, 0), (0, 1), (1, 0), (3, 0)]
    for dx, dy in pairs:
        pl.semaphore_signal(barrier, inc=1, device_id={"head": head_at(dx, dy)}, device_id_type=MESH)
    for offset in (-2, -1, 1, 2):
        pl.semaphore_signal(barrier, inc=1, device_id=blk_at(offset), device_id_type=MESH)

    live = counts[j]
    before = jnp.int32(0)
    for i in range(NB):
        before = before + jnp.where(i < j, counts[i], 0)
    shift = before - CH * j + BASE

    my_rows = pl.ds(pl.multiple_of(h * ROWS, ROWS), ROWS)

    def prepare(t):
        loads[2 * t].wait()
        if t == 2:
            for g in range(NG):
                sent[1, g] = fv[t, :, g * GROUP:(g + 1) * GROUP]
            got[1, my_rows] = sent[1, h]
            return
        loads[2 * t + 1].wait()
        rows = fv[t].astype(F32)
        factor = lax.rsqrt(jnp.mean(rows * rows, axis=-1, keepdims=True) + EPS)
        gains = (gq if t == 0 else gk)[...].astype(F32)
        for c in range(D // HEAD_DIM):
            cols = slice(c * HEAD_DIM, (c + 1) * HEAD_DIM)
            g, i = c // NH, c % NH
            value = (rows[:, cols] * factor * gains[c:c + 1] * (SCALE2 if t == 0 else 1.0)).astype(BF)
            if t == 0:
                sentq[i][g] = value
            else:
                sent[0, g, :, i * HEAD_DIM:(i + 1) * HEAD_DIM] = value
        if t == 0:
            for p in range(NP):
                gotq[p][my_rows] = sentq[p][h]
        else:
            got[0, my_rows] = sent[0, h]

    def spread(t):
        for dx, dy in pairs:
            peer = head_at(dx, dy)
            send(sent.at[t, peer], got.at[t, my_rows], 1, arecv.at[t], {"head": peer})

    prepare(0)
    pl.semaphore_wait(barrier, len(pairs) + 4)
    for p in range(NP):
        for dx, dy in pairs:
            peer = head_at(dx, dy)
            send(sentq[p].at[peer], gotq[p].at[my_rows], 0, qrecv.at[p], {"head": peer})
    for load in loads[6:]:
        load.start()
    prepare(1)
    spread(0)
    prepare(2)
    spread(1)

    r_id = lax.broadcasted_iota(jnp.int32, (SPAN, CAP), 0)
    s_id = lax.broadcasted_iota(jnp.int32, (1, CAP), 1)
    place = jnp.where(r_id == jnp.where(s_id < live, s_id + shift, -1), 1.0, 0.0).astype(BF)
    for p in range(NP):
        landed(gotq[p].at[0:CAP - ROWS], qrecv.at[p])
        selq[p][...] = mm(place, gotq[p][...]).astype(BF)
        for first, size, to, offset in ((64, 128, 0, -1), (320, 128, 128, 1), (0, 64, 256, -2), (448, 64, 320, 2)):
            send(selq[p].at[pl.ds(first, size)], rbuf[p].at[pl.ds(to, size)], 2, rrecv.at[p], blk_at(offset))
    back[...] = place.T
    pos = lax.broadcasted_iota(jnp.int32, (L_BLK, CAP), 0)
    hits = jnp.where(pos == jnp.where(s_id < live, ridx[...], -1), 1.0, 0.0)
    hit = jnp.sum(hits, axis=1, keepdims=True) > 0.5
    hits = hits.astype(BF)

    def gather_send(way, step, p):
        src = (8 - (step - 1)) % 8 if way == 0 else step - 1
        dst = 8 - step if way == 0 else step
        send(qs[p].at[src], qs[p].at[dst], 4, grecv.at[step - 1, p], blk_at(2 if way == 0 else -2))

    def gathered(step, p):
        landed(qs[p].at[0:2] if step < 4 else qs[p].at[0], grecv.at[step - 1, p])

    def gather_step(step, p):
        gathered(step - 1, p)
        for way in range(2):
            if step < 4 or p in LONG[way]:
                gather_send(way, step, p)

    for p in range(NP):
        landed(rbuf[p], rrecv.at[p])
        mine = (selq[p][192:320].astype(F32) + rbuf[p][0:128].astype(F32)) + rbuf[p][128:256].astype(F32)
        qs[p][0, 0:64] = (mine[0:64] + rbuf[p][320:384].astype(F32)).astype(BF)
        qs[p][0, 64:128] = (mine[64:128] + rbuf[p][256:320].astype(F32)).astype(BF)
        gather_send(0, 1, p)
        gather_send(1, 1, p)

    landed(got.at[0, 0:CAP - ROWS], arecv.at[0])
    loads[5].wait()
    kfull[0] = jnp.where(hit, mm(hits, got[0]), kc[...].astype(F32)).astype(BF)
    send(kfull.at[0], kfull.at[1], 3, krecv.at[0], sibling)
    for p in (0, 1):
        gather_step(2, p)
    landed(got.at[1, 0:CAP - ROWS], arecv.at[1])
    loads[6].wait()
    vt[0] = jnp.where(hit, mm(hits, got[1]), vc[...].astype(F32)).T.astype(BF)
    send(vt.at[0], vt.at[1], 3, krecv.at[1], sibling)
    for p in (2, 3, 4):
        gather_step(2, p)

    def attend(slots, need=None, done=None):
        def scores(i, b):
            query = [qs[i][s] for s in slots]
            query = query[0] if len(slots) == 1 else jnp.concatenate(query, axis=0)
            cols = slice(i * HEAD_DIM, (i + 1) * HEAD_DIM)
            return nt(kfull[b // 2, b % 2 * 256:b % 2 * 256 + 256, cols], query)

        def weighted(i, b, weights):
            return mm(vt[b // 2, i * HEAD_DIM:(i + 1) * HEAD_DIM, b % 2 * 256:b % 2 * 256 + 256], weights)

        def keep(i, value):
            for n, s in enumerate(slots):
                of[s, i * HEAD_DIM:(i + 1) * HEAD_DIM, :] = value[:, n * CH:(n + 1) * CH]
            if done is not None:
                done(i)

        if need is not None:
            need(0)
        now = [scores(0, b) for b in range(4)]
        last = []
        for i in range(NH):
            top = functools.reduce(jnp.maximum, [jnp.max(block, axis=0, keepdims=True) for block in now])
            if i + 1 < NH and need is not None:
                need(i + 1)
            ahead, weights, total, value = [], [], 0.0, 0.0
            for b in range(4):
                if i + 1 < NH:
                    ahead.append(scores(i + 1, b))
                one = jnp.exp2(now[b] - top)
                total = total + jnp.sum(one, axis=0, keepdims=True)
                weights.append(one.astype(BF))
                if i:
                    value = value + weighted(i - 1, b, last[b])
            for n, s in enumerate(slots):
                st[s, i, 0:1, :] = top[:, n * CH:(n + 1) * CH]
                st[s, i, 1:2, :] = total[:, n * CH:(n + 1) * CH]
            if i:
                keep(i - 1, value)
            now, last = ahead, weights
        value = functools.reduce(jnp.add, [weighted(NH - 1, b, last[b]) for b in range(4)])
        keep(NH - 1, value)

    def first_needs(p):
        gather_step(3, p)
        if p == 2:
            landed(vt.at[1], krecv.at[1])

    landed(kfull.at[1], krecv.at[0])
    attend((0, 7, 1), need=first_needs)
    attend((6, 2), need=functools.partial(gather_step, 4))

    def joined(slot, i, arrivals):
        rows = slice(i * HEAD_DIM, (i + 1) * HEAD_DIM)
        tops = [st[slot, i, 0:1]] + [rs[way, step, i, 0:1] for way, step in arrivals]
        sums = [st[slot, i, 1:2]] + [rs[way, step, i, 1:2] for way, step in arrivals]
        top = functools.reduce(jnp.maximum, tops)
        factors = [jnp.exp2(t - top) for t in tops]
        total = sum(a * f for a, f in zip(sums, factors))
        value = of[slot, rows, :] * factors[0]
        for n, (way, step) in enumerate(arrivals):
            value = value + ro[way, step, rows, :].astype(F32) * factors[n + 1]
        return value, top, total

    def give(way, step, p):
        ahead = 5 - step
        slot = ahead if way == 0 else 8 - ahead
        rows = slice(p * HEAD_DIM, (p + 1) * HEAD_DIM)
        if step > (1 if p in LONG[way] else 2):
            landed(unit.at[0:33], drecv.at[way, step - 2, p])
            value, top, total = joined(slot, p, [(way, step - 2)])
        else:
            value, top, total = of[slot, rows, :], st[slot, p, 0:1], st[slot, p, 1:2]
        so[way, step - 1, rows, :] = value.astype(BF)
        rows = pl.ds(p * HEAD_DIM, HEAD_DIM)
        dev = blk_at(2 if way == 0 else -2)
        send(so.at[way, step - 1, rows], ro.at[way, step - 1, rows], 5, drecv.at[way, step - 1, p], dev)
        ss[way, step - 1, p, 0:1] = top
        ss[way, step - 1, p, 1:2] = total
        send(ss.at[way, step - 1, p], rs.at[way, step - 1, p], 6, drecv.at[way, step - 1, p], dev)

    def long_way(p):
        return 0 if p in LONG[0] else 1

    attend((4,), need=lambda p: gathered(4, p), done=lambda p: give(long_way(p), 1, p))
    attend((5, 3), done=lambda p: give(1 - long_way(p), 2, p))
    for p in range(NP):
        give(long_way(p), 2, p)
    order = (LONG[1] + LONG[0], LONG[0] + LONG[1])
    for step in (3, 4):
        for both in zip(*order):
            for way in range(2):
                give(way, step, both[way])
    last_in = sorted(range(NP), key=lambda p: max(order[0].index(p), order[1].index(p)))

    for p in last_in:
        for way in range(2):
            landed(unit.at[0:33], drecv.at[way, 3, p])
        value, _, total = joined(0, p, [(0, 3), (1, 3)])
        abuf[p][...] = (value / total).T.astype(BF)
        for first, size, to, offset in ((0, 128, 320, -1), (0, 128, 64, 1), (0, 64, 448, -2), (64, 64, 0, 2)):
            send(abuf[p].at[pl.ds(first, size)], cat[p].at[pl.ds(to, size)], 7, urecv.at[p], blk_at(offset))
        cat[p][192:320] = abuf[p][...]
    for p in last_in:
        landed(rbuf[p], urecv.at[p])
        att[:, p * HEAD_DIM:(p + 1) * HEAD_DIM] = mm(back[...], cat[p][...]).astype(BF)

    loads[7].wait()

    def project(first, last):
        for at in range(first, last, 512):
            cols = slice(at, at + 512)
            tile = mm(att[...], wv[:, cols]).astype(BF)
            for g in range(NG):
                pb[g // 2, g % 2, :, cols] = tile[g * ROWS:(g + 1) * ROWS]

    up, down, far = lax.rem(x + 1, 4), lax.rem(x + 3, 4), lax.rem(x + 2, 4)
    to_up, to_down = {"head": up * 2 + y}, {"head": down * 2 + y}
    to_pair = {"head": x * 2 + 1 - y}

    def give_sum(kind, g, n, src, dst, dev):
        send(src, dst, 8, erecv.at[kind, g, (0, 2, 1, 2, 2, 2, 3)[n]], dev)

    def ring_start(kind, g, part, dst, first, half):
        a, b = pl.ds(first, half), pl.ds(first + half, half)
        give_sum(kind, g, 0, part(far, a), dst.at[0], to_up)
        give_sum(kind, g, 2, part(far, b), dst.at[2], to_down)
        give_sum(kind, g, 1, part(down, a), dst.at[1], to_down)
        give_sum(kind, g, 3, part(up, b), dst.at[3], to_up)

    def ring_pass(kind, g, load, dst, total, first, half):
        for n, other, cols, dev in ((0, up, first, to_up), (2, down, first + half, to_down)):
            landed(dst.at[n], erecv.at[kind, g, n // 2])
            total[n // 2] = (dst[n].astype(F32) + load(other, slice(cols, cols + half)).astype(F32)).astype(BF)
            give_sum(kind, g, 4 + n // 2, total.at[n // 2], dst.at[4 + n // 2], dev)

    def add(*terms):
        return functools.reduce(jnp.add, [t.astype(F32) for t in terms])

    def x_start(g):
        first, width = XG[g]
        project(first, first + width)
        ring_start(0, g, lambda to, cols: pb.at[to, :, :, cols], rx1[g], first, width // 2)

    def x_pass(g):
        first, width = XG[g]
        ring_pass(0, g, lambda to, cols: pb[to, :, :, cols], rx1[g], ac1[g], first, width // 2)

    def x_sums(g, row):
        first, width = XG[g]
        half = width // 2
        return (
            add(pb[x, row, :, first:first + half], rx1[g][4, row], rx1[g][1, row]),
            add(pb[x, row, :, first + half:first + width], rx1[g][5, row], rx1[g][3, row]),
        )

    def x_turn(g):
        half = XG[g][1] // 2
        landed(rx1[g].at[0:4], erecv.at[0, g, 2])
        one, two = x_sums(g, 1 - y)
        sy1[g][:, 0:half] = one.astype(BF)
        sy1[g][:, half:2 * half] = two.astype(BF)
        give_sum(0, g, 6, sy1[g], ry1[g], to_pair)

    def x_end(g):
        first, width = XG[g]
        half = width // 2
        landed(ry1[g], erecv.at[0, g, 3])
        one, two = x_sums(g, y)
        out[:, first:first + half] = add(one, ry1[g][:, 0:half]).astype(BF)
        out[:, first + half:first + width] = add(two, ry1[g][:, half:width]).astype(BF)

    def y_start(g):
        first, width = YG[g]
        project(first, first + width)
        give_sum(1, g, 6, pb.at[:, 1 - y, :, pl.ds(first, width)], ry2[g], to_pair)

    def y_turn(g):
        first, width = YG[g]
        landed(ry2[g], erecv.at[1, g, 3])
        for i in range(4):
            sx2[g][i] = add(ry2[g][i], pb[i, y, :, first:first + width]).astype(BF)
        if g < len(YG) - 1:
            ring_start(1, g, lambda to, cols: sx2[g].at[to, :, cols], rx2[g], 0, width // 2)
            return
        for n, (to, dev) in enumerate(((far, {"head": far * 2 + y}), (up, to_up), (down, to_down))):
            send(sx2[g].at[to], rx3.at[n], 8, erecv.at[1, g, 2], dev)

    def y_pass(g):
        ring_pass(1, g, lambda to, cols: sx2[g][to, :, cols], rx2[g], ac2[g], 0, YG[g][1] // 2)

    def y_end(g):
        first, width = YG[g]
        half = width // 2
        if g == len(YG) - 1:
            landed(rx3, erecv.at[1, g, 2])
            out[:, first:first + width] = add(sx2[g][x], rx3[0], rx3[1], rx3[2]).astype(BF)
            return
        landed(rx2[g].at[0:4], erecv.at[1, g, 2])
        out[:, first:first + half] = add(sx2[g][x, :, 0:half], rx2[g][4], rx2[g][1]).astype(BF)
        out[:, first + half:first + width] = add(sx2[g][x, :, half:width], rx2[g][5], rx2[g][3]).astype(BF)

    x_start(0)
    y_start(0)
    x_start(1)
    y_start(1)
    x_start(2)
    x_pass(0)
    x_pass(1)
    y_turn(0)
    x_turn(0)
    x_pass(2)
    y_turn(1)
    x_turn(1)
    y_pass(0)
    x_turn(2)
    x_end(0)
    x_end(1)
    y_end(0)
    x_end(2)
    y_end(1)

    for phase, rows, cols in (
        (0, 32, 4480), (1, 64, 4480), (2, 64, 3840), (3, 128, 5120), (4, 128, 4480), (5, 128, 4480),
        (7, 64, 3840), (8, 256, 4480),
    ):
        landed(wv.at[0:rows, 0:cols], ssem.at[phase])
    landed(unit, ssem.at[6])


def local(fresh, rows_index, counts, key_cache, value_cache, q_gain, k_gain, out_weight):
    any_spec = pl.BlockSpec(memory_space=pl.ANY)
    vmem = pl.BlockSpec(memory_space=pltpu.VMEM)
    dma = pltpu.SemaphoreType.DMA
    V = pltpu.VMEM

    def by_piece(*dims):
        return [V(dims + (HEAD_DIM,), BF)] * NP

    return pl.pallas_call(
        kernel,
        out_shape=V((ROWS, D), BF),
        in_specs=[any_spec, vmem, pl.BlockSpec(memory_space=pltpu.SMEM)] + [any_spec] * 5,
        out_specs=vmem,
        scratch_shapes=[
            V((3, ROWS, D), BF), V((D // 128, 128), BF), V((D // 128, 128), BF),
            V((L_BLK, GROUP), BF), V((L_BLK, GROUP), BF), V((GROUP, D), BF),
            V((2, NG, ROWS, GROUP), BF), V((2, CAP, GROUP), BF),
            by_piece(NG, ROWS), by_piece(CAP), by_piece(SPAN), by_piece(384),
            V((2, L_BLK, GROUP), BF), V((2, GROUP, L_BLK), BF), by_piece(8, CH),
            V((8, GROUP, CH), F32), V((8, NH, 2, CH), F32),
            V((2, 4, GROUP, CH), BF), V((2, 4, NH, 2, CH), F32),
            V((2, 4, GROUP, CH), BF), V((2, 4, NH, 2, CH), F32),
            by_piece(CH), by_piece(SPAN), V((CAP, SPAN), BF), V((CAP, GROUP), BF),
            V((4, 2, ROWS, D), BF),
            [V((6, 2, ROWS, w // 2), BF) for _, w in XG], [V((2, 2, ROWS, w // 2), BF) for _, w in XG],
            [V((ROWS, w), BF) for _, w in XG], [V((ROWS, w), BF) for _, w in XG],
            [V((4, ROWS, w), BF) for _, w in YG], [V((4, ROWS, w), BF) for _, w in YG],
            [V((6, ROWS, w // 2), BF) for _, w in YG], [V((2, ROWS, w // 2), BF) for _, w in YG],
            V((3, ROWS, YG[-1][1]), BF),
            V((35, 2, CH), F32), dma((8,)), dma((9,)), dma((NP,)), dma((2,)), dma((NP,)), dma((2,)),
            dma((4, NP)), dma((2, 4, NP)), dma((NP,)), dma((2, 3, 4)),
        ],
        compiler_params=pltpu.CompilerParams(
            collective_id=0, has_side_effects=True, vmem_limit_bytes=56 * 1024 * 1024
        ),
    )(
        jnp.transpose(fresh, (1, 0, 2)), rows_index.reshape(1, CAP), counts, key_cache, value_cache,
        q_gain.reshape(D // 128, 128), k_gain.reshape(D // 128, 128), out_weight,
    )


def solution(mesh):
    placed = (
        P(("cfg", "blk", "head"), None, None),
        P("blk"),
        P(),
        P(("cfg", "blk"), "head"),
        P(("cfg", "blk"), "head"),
        P(),
        P(),
        P("head", None),
    )
    return jax.shard_map(
        local,
        mesh=mesh,
        in_specs=placed,
        out_specs=P(("cfg", "blk", "head"), None),
        check_vma=False,
    )
```
